32 devices in a mesh: feat: 4 (over y, x), dp: 8 (over z, core).
Axes of the slice: x: 2, y: 2, z: 4, core: 2. Of those that a mesh axis runs over, the one named last changes fastest.
Arguments:
- features: bfloat16 [1024, 4096], P('feat', 'dp'), may hold values from -6 to 6
- neighbors: int32 [4096, 10], P('dp'), may hold values from 0 to 511
- labels: int32 [4096], P('dp'), may hold values from 0 to 171
- loss_weight: float32 [4096], P('dp'), as said below
- w1_self: bfloat16 [1024, 256], P('feat'), may hold values from -0.1875 to 0.1875
- w1_neigh: bfloat16 [1024, 256], P('feat'), may hold values from -0.1875 to 0.1875
- w2_self: bfloat16 [256, 172], replicated, may hold values from -0.375 to 0.375
- w2_neigh: bfloat16 [256, 172], replicated, may hold values from -0.375 to 0.375
Outputs:
- loss: float32 [], replicated
- grad_w1: float32 [2, 1024, 256], P(None, ('feat', 'dp'))
- grad_w2: float32 [2, 256, 172], replicated
The draws below stay inside these ranges and needn't reach their ends.
Inputs may be any that keep to these rules, and one draw needn't show every extreme that they name: `loss_weight`: positive weights.
All inputs are finite; a program needn't handle non-finite values.
Results may differ from the reference program's by a relative error of at most 0.0055.
Values may be sent and summed in bfloat16 or wider, within the bound.
No kernel may reach another device: no remote copies, remote signals or barrier semaphores. Data moves between devices by JAX's collectives and lax.ppermute only.
A program may use at most 128 MiB of HBM per device.

```python
import jax
import jax.numpy as jnp
from jax import lax

FIN = 1024
HID = 256
CLS = 172
FAN = 10
SUB = 512
NODES = 4096


def draw_loss_weight(key, part):
    position = jnp.arange(NODES, dtype=jnp.float32)
    rising = 1.0 + 2.0 * position / (NODES - 1)
    factor = jnp.exp(jax.random.uniform(key, (NODES,), jnp.float32, -0.7, 0.7))
    return (factor * rising).astype(jnp.float32)


def plant(array, own_key, least, largest):
    longest = array.shape.index(max(array.shape))
    spots = []
    for shift in (0, 1):
        where = [jax.random.randint(jax.random.fold_in(own_key, axis), (), 0, length) for axis, length in enumerate(array.shape)]
        where[longest] = (where[longest] + shift) % array.shape[longest]
        spots.append(tuple(where))
    return array.at[spots[0]].set(least).at[spots[1]].set(largest)


def block_scale(own_key, extent, pieces, least, largest):
    gain = 1.0
    for axis_at, parts in pieces:
        steps = jax.random.uniform(jax.random.fold_in(jax.random.fold_in(own_key, 6), axis_at), (parts,), jnp.float32, least / len(pieces), largest / len(pieces))
        gain = gain * jnp.repeat(jnp.exp(steps), extent[axis_at] // parts).reshape((-1,) + (1,) * (len(extent) - 1 - axis_at))
    return gain


def gaussian(stream_key, extent, scale, most, split=(), kind=jnp.bfloat16):
    result = scale * jax.random.normal(stream_key, extent, jnp.float32)
    if split:
        result = result * block_scale(stream_key, extent, split, -0.22, 0.18)
    return jnp.clip(result, -most, most).astype(kind)


def setup_inputs(seed: int = 0) -> dict:
    key_list = jax.random.split(jax.random.key(seed), 9)
    return {
        "features": gaussian(key_list[0], (FIN, NODES), 1.0, 6.0, ((0, 4), (1, 8))),
        "neighbors": plant(jax.random.randint(key_list[1], (NODES, FAN), 0, SUB), jax.random.fold_in(key_list[1], 1), 0, SUB - 1).astype(jnp.int32),
        "labels": plant(jax.random.randint(key_list[2], (NODES,), 0, CLS), jax.random.fold_in(key_list[2], 1), 0, CLS - 1).astype(jnp.int32),
        "loss_weight": draw_loss_weight(jax.random.fold_in(key_list[8], 71), 0),
        "w1_self": gaussian(key_list[4], (FIN, HID), FIN ** -0.5, 0.1875, ((0, 4),)),
        "w1_neigh": gaussian(key_list[5], (FIN, HID), FIN ** -0.5, 0.1875, ((0, 4),)),
        "w2_self": gaussian(key_list[6], (HID, CLS), HID ** -0.5, 0.375),
        "w2_neigh": gaussian(key_list[7], (HID, CLS), HID ** -0.5, 0.375),
    }


def focal_rows(logits, targets):
    logprob = jax.nn.log_softmax(logits, axis=-1)
    picked = jnp.take_along_axis(logprob, targets[:, None], axis=1)[:, 0]
    chance = jnp.exp(picked)
    return -(1.0 - chance) * (1.0 - chance) * picked

def neighbor_mean(lookup_table, indices):
    total = jnp.zeros((indices.shape[0], lookup_table.shape[1]), jnp.float32)
    for which in range(indices.shape[1]):
        total = total + jnp.take(lookup_table, indices[:, which], axis=0).astype(jnp.float32)
    return total / indices.shape[1]

def adjoint_sum(values, indices, total_rows):
    total = jnp.zeros((total_rows, values.shape[1]), jnp.float32)
    for which in range(indices.shape[1]):
        total = total + jax.ops.segment_sum(values, indices[:, which], num_segments=total_rows)
    return total

def contract_first(left_side, right_side):
    return lax.dot_general(left_side, right_side, (((0,), (0,)), ((), ())), preferred_element_type=jnp.float32)

def contract_last(left_side, right_side):
    return lax.dot_general(left_side, right_side, (((1,), (1,)), ((), ())), preferred_element_type=jnp.float32)

def reference(features, neighbors, labels, loss_weight, w1_self, w1_neigh, w2_self, w2_neigh):
    offsets = (jnp.arange(NODES, dtype=jnp.int32) // SUB * SUB).astype(jnp.int32)
    global_ids = (neighbors + offsets[:, None]).astype(jnp.int32)
    fanout = neighbors.shape[1]
    proj_self = contract_first(features, w1_self)
    proj_neigh = contract_first(features, w1_neigh).astype(jnp.bfloat16)
    first_pre = proj_self + neighbor_mean(proj_neigh, global_ids)
    hidden = jax.nn.relu(first_pre).astype(jnp.bfloat16)
    second_agg = neighbor_mean(hidden, global_ids).astype(jnp.bfloat16)
    logits = jnp.dot(hidden, w2_self, preferred_element_type=jnp.float32) + jnp.dot(second_agg, w2_neigh, preferred_element_type=jnp.float32)
    focal_terms, focal_vjp = jax.vjp(lambda values: focal_rows(values, labels), logits)
    grad_logits = focal_vjp(loss_weight)[0].astype(jnp.bfloat16)
    norm_total = jnp.sum(loss_weight)
    loss = jnp.sum(loss_weight * focal_terms) / norm_total
    grad_w2 = jnp.stack([contract_first(hidden, grad_logits), contract_first(second_agg, grad_logits)]) / norm_total
    hidden_own = contract_last(grad_logits, w2_self)
    agg_grad = contract_last(grad_logits, w2_neigh)
    hidden_grad = hidden_own + adjoint_sum(agg_grad, global_ids, NODES) / fanout
    pre_grad = jnp.where(first_pre > 0, hidden_grad, 0.0).astype(jnp.bfloat16)
    proj_grad = (adjoint_sum(pre_grad.astype(jnp.float32), global_ids, NODES) / fanout).astype(jnp.bfloat16)
    grad_w1 = jnp.stack([jnp.dot(features, pre_grad, preferred_element_type=jnp.float32), jnp.dot(features, proj_grad, preferred_element_type=jnp.float32)]) / norm_total
    return (loss, grad_w1, grad_w2)
```

```python
import functools

import jax
import jax.numpy as jnp
from jax import lax
from jax.experimental import pallas as pl
from jax.experimental.pallas import tpu as pltpu
from jax.sharding import PartitionSpec as P

BF16 = jnp.bfloat16
F32 = jnp.float32
VMEM_LIMIT = 56 * 1024 * 1024


def dot_nn(left, right):
    return lax.dot_general(left, right, (((1,), (0,)), ((), ())), preferred_element_type=F32)


def dot_nt(left, right):
    return lax.dot_general(left, right, (((1,), (1,)), ((), ())), preferred_element_type=F32)


def dot_tn(left, right):
    return lax.dot_general(left, right, (((0,), (0,)), ((), ())), preferred_element_type=F32)


def tree_sum(terms):
    terms = list(terms)
    while len(terms) > 1:
        terms = [terms[i] + terms[i + 1] for i in range(0, len(terms), 2)]
    return terms[0]


def call(kernel, outs, args, scratch=(), flops=0, smem=()):
    size = sum(a.size * a.dtype.itemsize for a in args)
    size += sum(o.size * o.dtype.itemsize for o in outs)
    specs = [
        pl.BlockSpec(memory_space=pltpu.SMEM if i in smem else pltpu.VMEM) for i in range(len(args))
    ]
    return pl.pallas_call(
        kernel,
        out_shape=outs,
        in_specs=specs,
        out_specs=[pl.BlockSpec(memory_space=pltpu.VMEM)] * len(outs),
        scratch_shapes=list(scratch),
        cost_estimate=pl.CostEstimate(flops=flops, bytes_accessed=size, transcendentals=0),
        compiler_params=pltpu.CompilerParams(vmem_limit_bytes=VMEM_LIMIT),
    )(*args)


def shape(dims, dtype):
    return jax.ShapeDtypeStruct(dims, dtype)


def count_kernel(fanout, nbr_ref, at_ref):
    nodes = at_ref.shape[1]
    step = 32

    def body(i, carry):
        row = lax.broadcasted_iota(jnp.int32, (step, nodes), 0) + i * step
        total = jnp.zeros((step, nodes), F32)
        for k in range(fanout):
            total = total + jnp.where(nbr_ref[k : k + 1, :] == row, 1.0, 0.0)
        at_ref[pl.ds(pl.multiple_of(i * step, step), step), :] = total.astype(BF16)
        return carry

    lax.fori_loop(0, nodes // step, body, 0)


def forward_kernel(feat_count, fanout, *refs):
    core_ref, labels_ref, weight_ref, at_ref, w2s_ref, w2n_ref, ws_ref, wn_ref = refs[:8]
    f_refs = refs[8 : 8 + feat_count]
    mine_refs = refs[8 + feat_count : 7 + 2 * feat_count]
    partner_refs = refs[7 + 2 * feat_count : 6 + 3 * feat_count]
    send_ref, keep_ref, g_ref, hidden_ref, proj, pair = refs[6 + 3 * feat_count :]
    core = core_ref[0]
    classes = w2s_ref.shape[1]
    nodes = at_ref.shape[1]
    scale = 1.0 / fanout
    first = core == 0
    own_mine = jnp.where(first, ws_ref[...], wn_ref[...])
    own_partner = jnp.where(first, wn_ref[...], ws_ref[...])
    proj[core] = tree_sum(
        [dot_tn(own_mine, f_refs[0][...])]
        + [dot_tn(mine_refs[s - 1][...], f_refs[s][...]) for s in range(1, feat_count)]
    )
    proj[1 - core] = tree_sum(
        [dot_tn(own_partner, f_refs[0][...])]
        + [dot_tn(partner_refs[s - 1][...], f_refs[s][...]) for s in range(1, feat_count)]
    )
    at = at_ref[...]
    pre = proj[0] + dot_nn(proj[1].astype(BF16), at) * scale
    hidden = jnp.maximum(pre, 0.0).astype(BF16)
    hidden_ref[...] = hidden
    second = (dot_nn(hidden, at) * scale).astype(BF16)
    logits = dot_tn(w2s_ref[...], hidden) + dot_tn(w2n_ref[...], second)
    shifted = logits - jnp.max(logits, axis=0, keepdims=True)
    logprob = shifted - jnp.log(jnp.sum(jnp.exp(shifted), axis=0, keepdims=True))
    hot = lax.broadcasted_iota(jnp.int32, (classes, nodes), 0) == labels_ref[...]
    picked = jnp.sum(jnp.where(hot, logprob, 0.0), axis=0, keepdims=True)
    chance = jnp.exp(picked)
    rest = 1.0 - chance
    weight = weight_ref[...]
    terms = -rest * rest * picked
    slope = weight * (2.0 * rest * chance * picked - rest * rest)
    grad = (slope * (jnp.where(hot, 1.0, 0.0) - jnp.exp(logprob))).astype(BF16)
    g_ref[...] = grad
    pair[0] = hidden
    pair[1] = second
    loss_part = jnp.sum(weight * terms)
    norm_part = jnp.sum(weight)
    for out_ref, which in ((send_ref, 1 - core), (keep_ref, core)):
        rows, cols = out_ref.shape
        row = lax.broadcasted_iota(jnp.int32, (rows, cols), 0)
        col = lax.broadcasted_iota(jnp.int32, (rows, cols), 1)
        extra = jnp.where(col == 0, loss_part, jnp.where(col == 1, norm_part, 0.0))
        out_ref[...] = jnp.where(row >= classes, extra, 0.0)
        out_ref[:classes, :] = dot_nt(grad, pair[which])


def backward_kernel(
    fanout, groups, core_ref, g_ref, hidden_ref, at_ref, w2s_ref, w2n_ref, f_ref, send_ref, keep_ref
):
    core = core_ref[0]
    scale = 1.0 / fanout
    grad = g_ref[...]
    at = at_ref[...]
    summed = dot_nt(grad, at)
    high = summed.astype(BF16)
    low = (summed - high.astype(F32)).astype(BF16)
    w2n = w2n_ref[...]
    hidden_grad = dot_nn(w2s_ref[...], grad) + (dot_nn(w2n, high) + dot_nn(w2n, low)) * scale
    pre_grad = jnp.where(hidden_ref[...] > 0, hidden_grad, 0.0).astype(BF16)
    proj_grad = (dot_nt(pre_grad, at) * scale).astype(BF16)
    features = f_ref[...]
    full = (dot_nt(features, pre_grad), dot_nt(features, proj_grad))
    rows = send_ref.shape[2]
    first = core == 0
    for z in range(groups):
        for part in range(2):
            low_rows = full[part][2 * z * rows : (2 * z + 1) * rows]
            high_rows = full[part][(2 * z + 1) * rows : (2 * z + 2) * rows]
            send_ref[z, part] = jnp.where(first, high_rows, low_rows)
            keep_ref[z, part] = jnp.where(first, low_rows, high_rows)


def pair_kernel(classes, keep_ref, recv_ref, out_ref):
    total = keep_ref[...] + recv_ref[...]
    high = total.astype(BF16).astype(F32)
    rest = total - high
    middle = rest.astype(BF16).astype(F32)
    low = rest - middle
    row = lax.broadcasted_iota(jnp.int32, total.shape, 0)
    out = jnp.where(row == classes + 1, middle, jnp.where(row == classes + 2, low, high))
    out_ref[...] = out.astype(BF16)


def chunk_kernel(groups, z_ref, keep_ref, recv_ref, own_ref, *out_refs):
    z = z_ref[0]
    own_ref[...] = keep_ref[z] + recv_ref[z]
    for s in range(1, groups):
        other = jnp.bitwise_xor(z, s)
        out_refs[s - 1][...] = (keep_ref[other] + recv_ref[other]).astype(BF16)


def second_sum_kernel(*refs):
    refs[-1][...] = tree_sum([r[...].astype(F32) for r in refs[:-1]])


def scalars(total, classes):
    row = lax.broadcasted_iota(jnp.int32, total.shape, 0)
    col = lax.broadcasted_iota(jnp.int32, total.shape, 1)
    inside = jnp.logical_and(row >= classes, row < classes + 3)
    loss = jnp.sum(jnp.where(jnp.logical_and(inside, col == 0), total, 0.0), keepdims=True)
    norm = jnp.sum(jnp.where(jnp.logical_and(inside, col == 1), total, 0.0), keepdims=True)
    return loss, norm


def second_out_kernel(classes, core_ref, own_ref, other_ref, out_ref, loss_ref):
    core = core_ref[0]
    loss, norm = scalars(own_ref[...], classes)
    inverse = 1.0 / norm
    out_ref[core] = (own_ref[...] * inverse).T[:, :classes]
    out_ref[1 - core] = (other_ref[...] * inverse).T[:, :classes]
    loss_ref[...] = loss * inverse


def first_out_kernel(classes, total_ref, *refs):
    _, norm = scalars(total_ref[...], classes)
    out_ref = refs[-1]
    summed = tree_sum([r[...].astype(F32) for r in refs[:-1]])
    out_ref[...] = summed * (1.0 / norm)[None]


def exchange(value, axis, step):
    size = lax.axis_size(axis)
    return lax.ppermute(value, axis, [(i, i ^ step) for i in range(size)])


def on_device(features, neighbors, labels, loss_weight, w1_self, w1_neigh, w2_self, w2_neigh):
    feat_count = lax.axis_size("feat")
    dp_count = lax.axis_size("dp")
    groups = dp_count // 2
    nodes, fanout = neighbors.shape
    rows, hid = w1_self.shape
    classes = w2_self.shape[1]
    place = lax.axis_index("dp").astype(jnp.int32)
    core = (place % 2).reshape(1)
    z = (place // 2).reshape(1)

    wide = [features] + [exchange(features, "feat", s) for s in range(1, feat_count)]
    mine_own = jnp.where(core[0] == 0, w1_self, w1_neigh)
    mine = [exchange(mine_own, "feat", s) for s in range(1, feat_count)]
    partner = [exchange(m, "dp", 1) for m in mine]

    (at,) = call(
        functools.partial(count_kernel, fanout),
        [shape((nodes, nodes), BF16)],
        [neighbors.T],
        flops=nodes * nodes * fanout,
    )
    padded = (classes + 3 + 15) // 16 * 16
    send2, keep2, grad, hidden = call(
        functools.partial(forward_kernel, feat_count, fanout),
        [
            shape((padded, hid), F32),
            shape((padded, hid), F32),
            shape((classes, nodes), BF16),
            shape((hid, nodes), BF16),
        ],
        [core, labels.reshape(1, nodes), loss_weight.reshape(1, nodes), at, w2_self, w2_neigh, w1_self, w1_neigh]
        + wide
        + mine
        + partner,
        scratch=[pltpu.VMEM((2, hid, nodes), F32), pltpu.VMEM((2, hid, nodes), BF16)],
        flops=2 * nodes * hid * 2 * (rows * feat_count + nodes),
        smem=(0,),
    )
    recv2 = exchange(send2, "dp", 1)
    send1, keep1 = call(
        functools.partial(backward_kernel, fanout, groups),
        [shape((groups, 2, rows // dp_count, hid), F32)] * 2,
        [core, grad, hidden, at, w2_self, w2_neigh, features],
        flops=2 * nodes * hid * 2 * (rows + nodes),
        smem=(0,),
    )
    (chip2,) = call(functools.partial(pair_kernel, classes), [shape((padded, hid), BF16)], [keep2, recv2])
    far2 = [exchange(chip2, "dp", 2 * s) for s in range(1, groups)]
    recv1 = exchange(send1, "dp", 1)
    own1, *chunks = call(
        functools.partial(chunk_kernel, groups),
        [shape((2, rows // dp_count, hid), F32)] + [shape((2, rows // dp_count, hid), BF16)] * (groups - 1),
        [z, keep1, recv1],
        smem=(0,),
    )
    far1 = [exchange(chunks[s - 1], "dp", 2 * s) for s in range(1, groups)]
    (total2,) = call(second_sum_kernel, [shape((padded, hid), F32)], [chip2] + far2)
    other2 = exchange(total2, "dp", 1)
    (grad_w1,) = call(
        functools.partial(first_out_kernel, classes),
        [shape((2, rows // dp_count, hid), F32)],
        [total2, own1] + far1,
    )
    grad_w2, loss = call(
        functools.partial(second_out_kernel, classes),
        [shape((2, hid, classes), F32), shape((1, 1), F32)],
        [core, total2, other2],
        smem=(0,),
    )
    return loss[0, 0], grad_w1, grad_w2


def solution(mesh):
    in_specs = (
        P("feat", "dp"),
        P("dp", None),
        P("dp"),
        P("dp"),
        P("feat", None),
        P("feat", None),
        P(),
        P(),
    )
    out_specs = (P(), P(None, ("feat", "dp"), None), P())
    return jax.shard_map(
        on_device, mesh=mesh, in_specs=in_specs, out_specs=out_specs, check_vma=False
    )
```

```python
import functools

import jax
import jax.numpy as jnp
from jax import lax
from jax.experimental import pallas as pl
from jax.experimental.pallas import tpu as pltpu
from jax.sharding import PartitionSpec as P

BF16 = jnp.bfloat16
F32 = jnp.float32


def dot_nn(left, right):
    return lax.dot_general(left, right, (((1,), (0,)), ((), ())), preferred_element_type=F32)


def dot_nt(left, right):
    return lax.dot_general(left, right, (((1,), (1,)), ((), ())), preferred_element_type=F32)


def dot_tn(left, right):
    return lax.dot_general(left, right, (((0,), (0,)), ((), ())), preferred_element_type=F32)


def tree_sum(terms):
    terms = list(terms)
    while len(terms) > 1:
        terms = [terms[i] + terms[i + 1] for i in range(0, len(terms), 2)]
    return terms[0]


def call(kernel, outs, args, flops=0, scratch=(), smem=(), limit=16, final=False):
    size = sum(a.size * a.dtype.itemsize for a in args)
    size += sum(o.dtype.itemsize * o.size for o in outs)
    spaces = [pltpu.SMEM if i in smem else pltpu.VMEM for i in range(len(args))]
    placed = [a if i in smem else pltpu.with_memory_space_constraint(a, pltpu.VMEM) for i, a in enumerate(args)]
    return pl.pallas_call(
        kernel,
        out_shape=outs if final else [pltpu.VMEM(o.shape, o.dtype) for o in outs],
        in_specs=[pl.BlockSpec(memory_space=space) for space in spaces],
        out_specs=[pl.BlockSpec(memory_space=pltpu.VMEM)] * len(outs),
        scratch_shapes=list(scratch),
        cost_estimate=pl.CostEstimate(flops=flops, bytes_accessed=size, transcendentals=0),
        compiler_params=pltpu.CompilerParams(vmem_limit_bytes=limit * 1024 * 1024),
    )(*placed)


def shape(dims, dtype):
    return jax.ShapeDtypeStruct(dims, dtype)


def count_kernel(fanout, nbr_ref, *refs):
    at_ref, stack_ref = refs[-2:]
    for i, ref in enumerate(refs[:-2]):
        stack_ref[i] = ref[...]
    nodes = at_ref.shape[1]
    step = 32

    def body(i, carry):
        row = lax.broadcasted_iota(jnp.int32, (step, nodes), 0) + i * step
        total = jnp.zeros((step, nodes), F32)
        for k in range(fanout):
            total = total + jnp.where(nbr_ref[k : k + 1, :] == row, 1.0, 0.0)
        at_ref[pl.ds(pl.multiple_of(i * step, step), step), :] = total.astype(BF16)
        return carry

    lax.fori_loop(0, nodes // step, body, 0)


def forward_kernel(parts, fanout, *refs):
    core_ref, labels_ref, weight_ref, at_ref, w2s_ref, w2n_ref, ws_ref, wn_ref, mine_ref, partner_ref = refs[:10]
    feat_count = len(parts)
    f_refs = refs[10 : 10 + sum(parts)]
    send_ref, keep_ref, g_ref, hidden_ref, proj, pair, joined = refs[10 + sum(parts) :]
    blocks, at_ref_index, join_index = [], 0, 0
    for count in parts:
        if count == 1:
            blocks.append(f_refs[at_ref_index][...])
        else:
            start = 0
            for ref in f_refs[at_ref_index : at_ref_index + count]:
                joined[join_index, start : start + ref.shape[0]] = ref[...]
                start += ref.shape[0]
            blocks.append(joined[join_index])
            join_index += 1
        at_ref_index += count
    core = core_ref[0]
    classes = w2s_ref.shape[0]
    nodes = at_ref.shape[1]
    scale = 1.0 / fanout
    first = core == 0
    own_mine = jnp.where(first, ws_ref[...], wn_ref[...])
    own_partner = jnp.where(first, wn_ref[...], ws_ref[...])
    proj[core] = tree_sum(
        [dot_tn(own_mine, blocks[0])]
        + [dot_tn(mine_ref[s - 1], blocks[s]) for s in range(1, feat_count)]
    )
    proj[1 - core] = tree_sum(
        [dot_tn(own_partner, blocks[0])]
        + [dot_tn(partner_ref[s - 1], blocks[s]) for s in range(1, feat_count)]
    )
    at = at_ref[...]
    pre = proj[0] + dot_nn(proj[1].astype(BF16), at) * scale
    hidden = jnp.maximum(pre, 0.0).astype(BF16)
    hidden_ref[...] = hidden
    second = (dot_nn(hidden, at) * scale).astype(BF16)
    logits = dot_nn(w2s_ref[...], hidden) + dot_nn(w2n_ref[...], second)
    shifted = logits - jnp.max(logits, axis=0, keepdims=True)
    logprob = shifted - jnp.log(jnp.sum(jnp.exp(shifted), axis=0, keepdims=True))
    hot = lax.broadcasted_iota(jnp.int32, (classes, nodes), 0) == labels_ref[...]
    picked = jnp.sum(jnp.where(hot, logprob, 0.0), axis=0, keepdims=True)
    chance = jnp.exp(picked)
    rest = 1.0 - chance
    weight = weight_ref[...]
    terms = -rest * rest * picked
    slope = weight * (2.0 * rest * chance * picked - rest * rest)
    grad = (slope * (jnp.where(hot, 1.0, 0.0) - jnp.exp(logprob))).astype(BF16)
    g_ref[...] = grad
    pair[0] = hidden
    pair[1] = second
    loss_part = jnp.sum(weight * terms)
    norm_part = jnp.sum(weight)
    for out_ref, which in ((send_ref, 1 - core), (keep_ref, core)):
        rows, cols = out_ref.shape
        row = lax.broadcasted_iota(jnp.int32, (rows, cols), 0)
        col = lax.broadcasted_iota(jnp.int32, (rows, cols), 1)
        extra = jnp.where(col == 0, loss_part, jnp.where(col == 1, norm_part, 0.0))
        out_ref[...] = jnp.where(row >= classes, extra, 0.0)
        out_ref[:classes, :] = dot_nt(grad, pair[which])


def backward_kernel(
    fanout, groups, core_ref, g_ref, hidden_ref, at_ref, w2s_ref, w2n_ref, f_ref, send_ref, keep_ref
):
    core = core_ref[0]
    scale = 1.0 / fanout
    grad = g_ref[...]
    at = at_ref[...]
    summed = dot_nt(grad, at)
    high = summed.astype(BF16)
    low = (summed - high.astype(F32)).astype(BF16)
    w2n = w2n_ref[...]
    hidden_grad = dot_tn(w2s_ref[...], grad) + (dot_tn(w2n, high) + dot_tn(w2n, low)) * scale
    pre_grad = jnp.where(hidden_ref[...] > 0, hidden_grad, 0.0).astype(BF16)
    proj_grad = (dot_nt(pre_grad, at) * scale).astype(BF16)
    features = f_ref[...]
    full = (dot_nt(features, pre_grad), dot_nt(features, proj_grad))
    rows = send_ref.shape[1] // 2
    first = core == 0
    for z in range(groups):
        for part in range(2):
            low_rows = full[part][2 * z * rows : (2 * z + 1) * rows]
            high_rows = full[part][(2 * z + 1) * rows : (2 * z + 2) * rows]
            send_ref[z, part * rows : (part + 1) * rows] = jnp.where(first, high_rows, low_rows)
            keep_ref[z, part * rows : (part + 1) * rows] = jnp.where(first, low_rows, high_rows)


def pack_kernel(classes, groups, z_ref, keep2_ref, recv2_ref, keep1_ref, recv1_ref, own2_ref, own1_ref, *pack_refs):
    z = z_ref[0]
    total = keep2_ref[...] + recv2_ref[...]
    high = total.astype(BF16).astype(F32)
    rest = total - high
    middle = rest.astype(BF16).astype(F32)
    low = rest - middle
    row = lax.broadcasted_iota(jnp.int32, total.shape, 0)
    out = jnp.where(row == classes + 1, middle, jnp.where(row == classes + 2, low, high)).astype(BF16)
    own2_ref[...] = out
    own1_ref[...] = keep1_ref[z] + recv1_ref[z]
    padded = total.shape[0]
    for s in range(1, groups):
        other = jnp.bitwise_xor(z, s)
        pack_refs[s - 1][:padded] = out
        pack_refs[s - 1][padded:] = (keep1_ref[other] + recv1_ref[other]).astype(BF16)


def second_sum_kernel(*refs):
    out_ref = refs[-1]
    padded = out_ref.shape[0]
    out_ref[...] = tree_sum([r[:padded].astype(F32) for r in refs[:-1]])


def scalars(total, classes):
    row = lax.broadcasted_iota(jnp.int32, total.shape, 0)
    col = lax.broadcasted_iota(jnp.int32, total.shape, 1)
    inside = jnp.logical_and(row >= classes, row < classes + 3)
    loss = jnp.sum(jnp.where(jnp.logical_and(inside, col == 0), total, 0.0), keepdims=True)
    norm = jnp.sum(jnp.where(jnp.logical_and(inside, col == 1), total, 0.0), keepdims=True)
    return loss, norm


def second_out_kernel(classes, core_ref, own_ref, other_ref, out_ref, loss_ref):
    first = core_ref[0] == 0
    loss, norm = scalars(own_ref[...], classes)
    inverse = 1.0 / norm
    own = own_ref[:classes, :] * inverse
    other = other_ref[:classes, :] * inverse
    out_ref[:, 0, :] = jnp.where(first, own, other)
    out_ref[:, 1, :] = jnp.where(first, other, own)
    loss_ref[...] = loss * inverse


def first_out_kernel(classes, total_ref, own_ref, *refs):
    _, norm = scalars(total_ref[...], classes)
    out_ref = refs[-1]
    padded = total_ref.shape[0]
    summed = tree_sum([own_ref[...]] + [r[padded:].astype(F32) for r in refs[:-1]]) * (1.0 / norm)
    rows = out_ref.shape[1]
    out_ref[0] = summed[:rows]
    out_ref[1] = summed[rows:]


def exchange(value, axis, step):
    size = lax.axis_size(axis)
    return lax.ppermute(value, axis, [(i, i ^ step) for i in range(size)])


def gather_parts(block, count):
    half = block.shape[0] // 2
    parts = [[block]]
    for s in range(1, count):
        low_bit = s & -s
        rest = s ^ low_bit
        if rest == 0:
            parts.append([exchange(block, "feat", s)])
        else:
            low = parts[rest][0][:half] if len(parts[rest]) == 1 else parts[rest][0]
            high = parts[low_bit][0][half:]
            parts.append([exchange(low, "feat", low_bit), exchange(high, "feat", rest)])
    return parts


def on_device(features, neighbors, labels, loss_weight, w1_self, w1_neigh, w2_self, w2_neigh):
    feat_count = lax.axis_size("feat")
    dp_count = lax.axis_size("dp")
    groups = dp_count // 2
    nodes, fanout = neighbors.shape
    rows, hid = w1_self.shape
    classes = w2_self.shape[1]
    place = lax.axis_index("dp").astype(jnp.int32)
    core = (place % 2).reshape(1)
    z = (place // 2).reshape(1)

    wide = gather_parts(features, feat_count)
    parts = tuple(len(w) for w in wide)
    mine_own = jnp.where(core[0] == 0, w1_self, w1_neigh)
    mine = [exchange(mine_own, "feat", s) for s in range(1, feat_count)]
    at, stacked = call(
        functools.partial(count_kernel, fanout),
        [shape((nodes, nodes), BF16), shape((feat_count - 1, rows, hid), BF16)],
        [neighbors.T] + mine,
        flops=nodes * nodes * fanout,
    )
    partner = exchange(stacked, "dp", 1)
    w2s, w2n = w2_self.T, w2_neigh.T
    limit = 12 + 6 * nodes * nodes // (1024 * 1024)
    padded = (classes + 3 + 15) // 16 * 16
    send2, keep2, grad, hidden = call(
        functools.partial(forward_kernel, parts, fanout),
        [
            shape((padded, hid), F32),
            shape((padded, hid), F32),
            shape((classes, nodes), BF16),
            shape((hid, nodes), BF16),
        ],
        [core, labels.reshape(1, nodes), loss_weight.reshape(1, nodes), at, w2s, w2n, w1_self, w1_neigh, stacked, partner]
        + [part for block in wide for part in block],
        scratch=[
            pltpu.VMEM((2, hid, nodes), F32),
            pltpu.VMEM((2, hid, nodes), BF16),
            pltpu.VMEM((max(1, sum(p > 1 for p in parts)), rows, nodes), BF16),
        ],
        flops=2 * nodes * hid * 2 * (rows * feat_count + nodes),
        smem=(0,),
        limit=limit,
    )
    recv2 = exchange(send2, "dp", 1)
    chunk = 2 * (rows // dp_count)
    send1, keep1 = call(
        functools.partial(backward_kernel, fanout, groups),
        [shape((groups, chunk, hid), F32)] * 2,
        [core, grad, hidden, at, w2s, w2n, features],
        flops=2 * nodes * hid * 2 * (rows + nodes),
        smem=(0,),
        limit=limit,
    )
    recv1 = exchange(send1, "dp", 1)
    own2, own1, *packs = call(
        functools.partial(pack_kernel, classes, groups),
        [shape((padded, hid), BF16), shape((chunk, hid), F32)] + [shape((padded + chunk, hid), BF16)] * (groups - 1),
        [z, keep2, recv2, keep1, recv1],
        smem=(0,),
    )
    far = [exchange(packs[s - 1], "dp", 2 * s) for s in range(1, groups)]
    (total2,) = call(second_sum_kernel, [shape((padded, hid), F32)], [own2] + far)
    other2 = exchange(total2, "dp", 1)
    (grad_w1,) = call(
        functools.partial(first_out_kernel, classes),
        [shape((2, rows // dp_count, hid), F32)],
        [total2, own1] + far,
        final=True,
    )
    grad_w2, loss = call(
        functools.partial(second_out_kernel, classes),
        [shape((classes, 2, hid), F32), shape((1, 1), F32)],
        [core, total2, other2],
        smem=(0,),
        final=True,
    )
    return loss[0, 0], grad_w1, grad_w2.transpose(1, 2, 0)


def solution(mesh):
    in_specs = (
        P("feat", "dp"),
        P("dp", None),
        P("dp"),
        P("dp"),
        P("feat", None),
        P("feat", None),
        P(),
        P(),
    )
    out_specs = (P(), P(None, ("feat", "dp"), None), P())
    return jax.shard_map(
        on_device, mesh=mesh, in_specs=in_specs, out_specs=out_specs, check_vma=False
    )
```

```python
import functools

import jax
import jax.numpy as jnp
from jax import lax
from jax.experimental import pallas as pl
from jax.experimental.pallas import tpu as pltpu
from jax.sharding import PartitionSpec as P

BF16 = jnp.bfloat16
F32 = jnp.float32


def dot_nn(left, right):
    return lax.dot_general(left, right, (((1,), (0,)), ((), ())), preferred_element_type=F32)


def dot_nt(left, right):
    return lax.dot_general(left, right, (((1,), (1,)), ((), ())), preferred_element_type=F32)


def dot_tn(left, right):
    return lax.dot_general(left, right, (((0,), (0,)), ((), ())), preferred_element_type=F32)


def tree_sum(terms):
    terms = list(terms)
    while len(terms) > 1:
        terms = [terms[i] + terms[i + 1] for i in range(0, len(terms), 2)]
    return terms[0]


def call(kernel, outs, args, flops=0, scratch=(), smem=(), limit=16, final=False):
    size = sum(a.size * a.dtype.itemsize for a in args)
    size += sum(o.dtype.itemsize * o.size for o in outs)
    spaces = [pltpu.SMEM if i in smem else pltpu.VMEM for i in range(len(args))]
    placed = [a if i in smem else pltpu.with_memory_space_constraint(a, pltpu.VMEM) for i, a in enumerate(args)]
    return pl.pallas_call(
        kernel,
        out_shape=outs if final else [pltpu.VMEM(o.shape, o.dtype) for o in outs],
        in_specs=[pl.BlockSpec(memory_space=space) for space in spaces],
        out_specs=[pl.BlockSpec(memory_space=pltpu.VMEM)] * len(outs),
        scratch_shapes=list(scratch),
        cost_estimate=pl.CostEstimate(flops=flops, bytes_accessed=size, transcendentals=0),
        compiler_params=pltpu.CompilerParams(vmem_limit_bytes=limit * 1024 * 1024),
    )(*placed)


def shape(dims, dtype):
    return jax.ShapeDtypeStruct(dims, dtype)


def count_kernel(fanout, nbr_ref, labels_ref, weight_ref, *refs):
    at_ref, stack_ref, labels_out_ref, weight_out_ref = refs[-4:]
    labels_out_ref[...] = labels_ref[...]
    weight_out_ref[...] = weight_ref[...]
    for i, ref in enumerate(refs[:-4]):
        stack_ref[i] = ref[...]
    nodes = at_ref.shape[1]
    step = 32

    def body(i, carry):
        row = lax.broadcasted_iota(jnp.int32, (step, nodes), 0) + i * step
        total = jnp.zeros((step, nodes), F32)
        for k in range(fanout):
            total = total + jnp.where(nbr_ref[k : k + 1, :] == row, 1.0, 0.0)
        at_ref[pl.ds(pl.multiple_of(i * step, step), step), :] = total.astype(BF16)
        return carry

    lax.fori_loop(0, nodes // step, body, 0)


def project(own, others_ref, f_refs):
    products = [dot_tn(own, f_refs[0][...])]
    for s in range(1, len(f_refs)):
        products.append(dot_tn(others_ref[s - 1], f_refs[s][...]))
    return tree_sum(products)


def mine_kernel(parts, core_ref, ws_ref, wn_ref, mine_ref, *refs):
    out_ref, joined_refs = refs[sum(parts)], refs[sum(parts) + 1 :]
    own = jnp.where(core_ref[0] == 0, ws_ref[...], wn_ref[...])
    blocks, at, done = [], 0, 0
    for count in parts:
        block = refs[at]
        if count > 1:
            block, start = joined_refs[done], 0
            for ref in refs[at : at + count]:
                block[start : start + ref.shape[0]] = ref[...]
                start += ref.shape[0]
            done += 1
        blocks.append(block)
        at += count
    out_ref[...] = project(own, mine_ref, blocks)


def forward_kernel(feat_count, fanout, *refs):
    f_refs, refs = refs[:feat_count], refs[feat_count:]
    core_ref, labels_ref, weight_ref, at_ref, w2s_ref, w2n_ref, ws_ref, wn_ref, partner_ref, mine_ref = refs[:10]
    send_ref, keep_ref, g_ref, hidden_ref, proj, pair = refs[10:]
    core = core_ref[0]
    classes = w2s_ref.shape[0]
    nodes = at_ref.shape[1]
    scale = 1.0 / fanout
    own = jnp.where(core == 0, wn_ref[...], ws_ref[...])
    proj[core] = mine_ref[...]
    proj[1 - core] = project(own, partner_ref, f_refs)
    at = at_ref[...]
    pre = proj[0] + dot_nn(proj[1].astype(BF16), at) * scale
    hidden = jnp.maximum(pre, 0.0).astype(BF16)
    hidden_ref[...] = hidden
    second = (dot_nn(hidden, at) * scale).astype(BF16)
    logits = dot_nn(w2s_ref[...], hidden) + dot_nn(w2n_ref[...], second)
    shifted = logits - jnp.max(logits, axis=0, keepdims=True)
    logprob = shifted - jnp.log(jnp.sum(jnp.exp(shifted), axis=0, keepdims=True))
    hot = lax.broadcasted_iota(jnp.int32, (classes, nodes), 0) == labels_ref[...]
    picked = jnp.sum(jnp.where(hot, logprob, 0.0), axis=0, keepdims=True)
    chance = jnp.exp(picked)
    rest = 1.0 - chance
    weight = weight_ref[...]
    terms = -rest * rest * picked
    slope = weight * (2.0 * rest * chance * picked - rest * rest)
    grad = (slope * (jnp.where(hot, 1.0, 0.0) - jnp.exp(logprob))).astype(BF16)
    g_ref[...] = grad
    pair[0] = hidden
    pair[1] = second
    loss_part = jnp.sum(weight * terms)
    norm_part = jnp.sum(weight)
    for out_ref, which in ((send_ref, 1 - core), (keep_ref, core)):
        rows, cols = out_ref.shape
        row = lax.broadcasted_iota(jnp.int32, (rows, cols), 0)
        col = lax.broadcasted_iota(jnp.int32, (rows, cols), 1)
        extra = jnp.where(col == 0, loss_part, jnp.where(col == 1, norm_part, 0.0))
        out_ref[...] = jnp.where(row >= classes, extra, 0.0)
        out_ref[:classes, :] = dot_nt(grad, pair[which])


def backward_kernel(
    fanout, groups, core_ref, g_ref, hidden_ref, at_ref, w2s_ref, w2n_ref, f_ref, send_ref, keep_ref
):
    core = core_ref[0]
    scale = 1.0 / fanout
    grad = g_ref[...]
    at = at_ref[...]
    summed = dot_nt(grad, at)
    high = summed.astype(BF16)
    low = (summed - high.astype(F32)).astype(BF16)
    w2n = w2n_ref[...]
    hidden_grad = dot_tn(w2s_ref[...], grad) + (dot_tn(w2n, high) + dot_tn(w2n, low)) * scale
    pre_grad = jnp.where(hidden_ref[...] > 0, hidden_grad, 0.0).astype(BF16)
    proj_grad = (dot_nt(pre_grad, at) * scale).astype(BF16)
    features = f_ref[...]
    full = (dot_nt(features, pre_grad), dot_nt(features, proj_grad))
    rows = send_ref.shape[1] // 2
    first = core == 0
    for z in range(groups):
        for part in range(2):
            low_rows = full[part][2 * z * rows : (2 * z + 1) * rows]
            high_rows = full[part][(2 * z + 1) * rows : (2 * z + 2) * rows]
            send_ref[z, part * rows : (part + 1) * rows] = jnp.where(first, high_rows, low_rows)
            keep_ref[z, part * rows : (part + 1) * rows] = jnp.where(first, low_rows, high_rows)


def pack_kernel(classes, groups, z_ref, keep2_ref, recv2_ref, keep1_ref, recv1_ref, own2_ref, own1_ref, *pack_refs):
    z = z_ref[0]
    total = keep2_ref[...] + recv2_ref[...]
    high = total.astype(BF16).astype(F32)
    rest = total - high
    middle = rest.astype(BF16).astype(F32)
    low = rest - middle
    row = lax.broadcasted_iota(jnp.int32, total.shape, 0)
    out = jnp.where(row == classes + 1, middle, jnp.where(row == classes + 2, low, high)).astype(BF16)
    own2_ref[...] = out
    own1_ref[...] = keep1_ref[z] + recv1_ref[z]
    padded = total.shape[0]
    for s in range(1, groups):
        other = jnp.bitwise_xor(z, s)
        pack_refs[s - 1][:padded] = out
        pack_refs[s - 1][padded:] = (keep1_ref[other] + recv1_ref[other]).astype(BF16)


def second_sum_kernel(*refs):
    out_ref = refs[-1]
    padded = out_ref.shape[0]
    out_ref[...] = tree_sum([r[:padded].astype(F32) for r in refs[:-1]])


def scalars(total, classes):
    row = lax.broadcasted_iota(jnp.int32, total.shape, 0)
    col = lax.broadcasted_iota(jnp.int32, total.shape, 1)
    inside = jnp.logical_and(row >= classes, row < classes + 3)
    loss = jnp.sum(jnp.where(jnp.logical_and(inside, col == 0), total, 0.0), keepdims=True)
    norm = jnp.sum(jnp.where(jnp.logical_and(inside, col == 1), total, 0.0), keepdims=True)
    return loss, norm


def second_out_kernel(classes, core_ref, own_ref, other_ref, out_ref, loss_ref):
    first = core_ref[0] == 0
    loss, norm = scalars(own_ref[...], classes)
    inverse = 1.0 / norm
    own = own_ref[:classes, :] * inverse
    other = other_ref[:classes, :] * inverse
    out_ref[:, 0, :] = jnp.where(first, own, other)
    out_ref[:, 1, :] = jnp.where(first, other, own)
    loss_ref[...] = loss * inverse


def first_out_kernel(classes, total_ref, own_ref, *refs):
    _, norm = scalars(total_ref[...], classes)
    out_ref = refs[-1]
    padded = total_ref.shape[0]
    summed = tree_sum([own_ref[...]] + [r[padded:].astype(F32) for r in refs[:-1]]) * (1.0 / norm)
    rows = out_ref.shape[1]
    out_ref[0] = summed[:rows]
    out_ref[1] = summed[rows:]


def exchange(value, axis, step):
    size = lax.axis_size(axis)
    return lax.ppermute(value, axis, [(i, i ^ step) for i in range(size)])


def gather_parts(block, count):
    half = block.shape[0] // 2
    parts = [[block]]
    for s in range(1, count):
        low_bit = s & -s
        rest = s ^ low_bit
        if rest == 0:
            parts.append([exchange(block, "feat", s)])
        else:
            low = parts[rest][0][:half] if len(parts[rest]) == 1 else parts[rest][0]
            high = parts[low_bit][0][half:]
            parts.append([exchange(low, "feat", low_bit), exchange(high, "feat", rest)])
    return parts


def on_device(features, neighbors, labels, loss_weight, w1_self, w1_neigh, w2_self, w2_neigh):
    feat_count = lax.axis_size("feat")
    dp_count = lax.axis_size("dp")
    groups = dp_count // 2
    nodes, fanout = neighbors.shape
    rows, hid = w1_self.shape
    classes = w2_self.shape[1]
    place = lax.axis_index("dp").astype(jnp.int32)
    core = (place % 2).reshape(1)
    z = (place // 2).reshape(1)

    wide = gather_parts(features, feat_count)
    parts = tuple(len(block) for block in wide)
    mine_own = jnp.where(core[0] == 0, w1_self, w1_neigh)
    mine = [exchange(mine_own, "feat", s) for s in range(1, feat_count)]
    limit = 12 + 6 * nodes * nodes // (1024 * 1024)
    at, stacked, labels, loss_weight = call(
        functools.partial(count_kernel, fanout),
        [
            shape((nodes, nodes), BF16),
            shape((feat_count - 1, rows, hid), BF16),
            shape((1, nodes), jnp.int32),
            shape((1, nodes), F32),
        ],
        [neighbors.T, labels.reshape(1, nodes), loss_weight.reshape(1, nodes)] + mine,
        flops=nodes * nodes * fanout,
    )
    mine_proj, *joined = call(
        functools.partial(mine_kernel, parts),
        [shape((hid, nodes), F32)] + [shape((rows, nodes), BF16)] * sum(count > 1 for count in parts),
        [core, w1_self, w1_neigh, stacked] + [part for block in wide for part in block],
        flops=30 * nodes * hid * rows * feat_count,
        smem=(0,),
        limit=limit,
    )
    rest = iter(joined)
    whole = [block[0] if len(block) == 1 else next(rest) for block in wide]
    partner = exchange(stacked, "dp", 1)
    w2s, w2n = w2_self.T, w2_neigh.T
    padded = (classes + 3 + 15) // 16 * 16
    send2, keep2, grad, hidden = call(
        functools.partial(forward_kernel, feat_count, fanout),
        [
            shape((padded, hid), F32),
            shape((padded, hid), F32),
            shape((classes, nodes), BF16),
            shape((hid, nodes), BF16),
        ],
        whole + [core, labels, loss_weight, at, w2s, w2n, w1_self, w1_neigh, partner, mine_proj],
        scratch=[
            pltpu.VMEM((2, hid, nodes), F32),
            pltpu.VMEM((2, hid, nodes), BF16),
        ],
        flops=2 * nodes * hid * 2 * (rows * feat_count + nodes),
        smem=(feat_count,),
        limit=limit,
    )
    recv2 = exchange(send2, "dp", 1)
    chunk = 2 * (rows // dp_count)
    send1, keep1 = call(
        functools.partial(backward_kernel, fanout, groups),
        [shape((groups, chunk, hid), F32)] * 2,
        [core, grad, hidden, at, w2s, w2n, features],
        flops=2 * nodes * hid * 2 * (rows + nodes),
        smem=(0,),
        limit=limit,
    )
    recv1 = exchange(send1, "dp", 1)
    own2, own1, *packs = call(
        functools.partial(pack_kernel, classes, groups),
        [shape((padded, hid), BF16), shape((chunk, hid), F32)] + [shape((padded + chunk, hid), BF16)] * (groups - 1),
        [z, keep2, recv2, keep1, recv1],
        smem=(0,),
    )
    far = [exchange(packs[s - 1], "dp", 2 * s) for s in range(1, groups)]
    (total2,) = call(second_sum_kernel, [shape((padded, hid), F32)], [own2] + far)
    other2 = exchange(total2, "dp", 1)
    (grad_w1,) = call(
        functools.partial(first_out_kernel, classes),
        [shape((2, rows // dp_count, hid), F32)],
        [total2, own1] + far,
        final=True,
    )
    grad_w2, loss = call(
        functools.partial(second_out_kernel, classes),
        [shape((classes, 2, hid), F32), shape((1, 1), F32)],
        [core, total2, other2],
        smem=(0,),
        final=True,
    )
    return loss[0, 0], grad_w1, grad_w2.transpose(1, 2, 0)


def solution(mesh):
    in_specs = (
        P("feat", "dp"),
        P("dp", None),
        P("dp"),
        P("dp"),
        P("feat", None),
        P("feat", None),
        P(),
        P(),
    )
    out_specs = (P(), P(None, ("feat", "dp"), None), P())
    return jax.shard_map(
        on_device, mesh=mesh, in_specs=in_specs, out_specs=out_specs, check_vma=False
    )
```

```python
import functools

import jax
import jax.numpy as jnp
from jax import lax
from jax.experimental import pallas as pl
from jax.experimental.pallas import tpu as pltpu
from jax.sharding import PartitionSpec as P

BF16 = jnp.bfloat16
F32 = jnp.float32


def dot_nn(left, right):
    return lax.dot_general(left, right, (((1,), (0,)), ((), ())), preferred_element_type=F32)


def dot_nt(left, right):
    return lax.dot_general(left, right, (((1,), (1,)), ((), ())), preferred_element_type=F32)


def dot_tn(left, right):
    return lax.dot_general(left, right, (((0,), (0,)), ((), ())), preferred_element_type=F32)


def tree_sum(terms):
    terms = list(terms)
    while len(terms) > 1:
        terms = [terms[i] + terms[i + 1] for i in range(0, len(terms), 2)]
    return terms[0]


def call(kernel, outs, args, flops=0, scratch=(), smem=(), limit=16, final=False):
    size = sum(a.size * a.dtype.itemsize for a in args)
    size += sum(o.dtype.itemsize * o.size for o in outs)
    spaces = [pltpu.SMEM if i in smem else pltpu.VMEM for i in range(len(args))]
    placed = [a if i in smem else pltpu.with_memory_space_constraint(a, pltpu.VMEM) for i, a in enumerate(args)]
    return pl.pallas_call(
        kernel,
        out_shape=outs if final else [pltpu.VMEM(o.shape, o.dtype) for o in outs],
        in_specs=[pl.BlockSpec(memory_space=space) for space in spaces],
        out_specs=[pl.BlockSpec(memory_space=pltpu.VMEM)] * len(outs),
        scratch_shapes=list(scratch),
        cost_estimate=pl.CostEstimate(flops=flops, bytes_accessed=size, transcendentals=0),
        compiler_params=pltpu.CompilerParams(vmem_limit_bytes=limit * 1024 * 1024),
    )(*placed)


def shape(dims, dtype):
    return jax.ShapeDtypeStruct(dims, dtype)


def count_kernel(fanout, nbr_ref, labels_ref, weight_ref, at_ref, labels_out_ref, weight_out_ref):
    labels_out_ref[...] = labels_ref[...]
    weight_out_ref[...] = weight_ref[...]
    nodes = at_ref.shape[1]
    step = 32

    def body(i, carry):
        row = lax.broadcasted_iota(jnp.int32, (step, nodes), 0) + i * step
        total = jnp.zeros((step, nodes), F32)
        for k in range(fanout):
            total = total + jnp.where(nbr_ref[k : k + 1, :] == row, 1.0, 0.0)
        at_ref[pl.ds(pl.multiple_of(i * step, step), step), :] = total.astype(BF16)
        return carry

    lax.fori_loop(0, nodes // step, body, 0)


def project(own, others_refs, f_refs):
    products = [dot_tn(own, f_refs[0][...])]
    for s in range(1, len(f_refs)):
        products.append(dot_tn(others_refs[s - 1][...], f_refs[s][...]))
    return tree_sum(products)


def mine_kernel(parts, core_ref, ws_ref, wn_ref, *refs):
    mine_refs, refs = refs[: len(parts) - 1], refs[len(parts) - 1 :]
    out_ref, joined_refs = refs[sum(parts)], refs[sum(parts) + 1 :]
    own = jnp.where(core_ref[0] == 0, ws_ref[...], wn_ref[...])
    blocks, at, done = [], 0, 0
    for count in parts:
        block = refs[at]
        if count > 1:
            block, start = joined_refs[done], 0
            for ref in refs[at : at + count]:
                block[start : start + ref.shape[0]] = ref[...]
                start += ref.shape[0]
            done += 1
        blocks.append(block)
        at += count
    out_ref[...] = project(own, mine_refs, blocks)


def forward_kernel(feat_count, fanout, *refs):
    f_refs, refs = refs[:feat_count], refs[feat_count:]
    core_ref, labels_ref, weight_ref, at_ref, w2s_ref, w2n_ref, ws_ref, wn_ref, mine_ref = refs[:9]
    partner_refs = refs[9 : 8 + feat_count]
    send_ref, keep_ref, g_ref, hidden_ref, proj, pair = refs[8 + feat_count :]
    core = core_ref[0]
    classes = w2s_ref.shape[0]
    nodes = at_ref.shape[1]
    scale = 1.0 / fanout
    own = jnp.where(core == 0, wn_ref[...], ws_ref[...])
    proj[core] = mine_ref[...]
    proj[1 - core] = project(own, partner_refs, f_refs)
    at = at_ref[...]
    pre = proj[0] + dot_nn(proj[1].astype(BF16), at) * scale
    hidden = jnp.maximum(pre, 0.0).astype(BF16)
    hidden_ref[...] = hidden
    second = (dot_nn(hidden, at) * scale).astype(BF16)
    logits = dot_nn(w2s_ref[...], hidden) + dot_nn(w2n_ref[...], second)
    shifted = logits - jnp.max(logits, axis=0, keepdims=True)
    logprob = shifted - jnp.log(jnp.sum(jnp.exp(shifted), axis=0, keepdims=True))
    hot = lax.broadcasted_iota(jnp.int32, (classes, nodes), 0) == labels_ref[...]
    picked = jnp.sum(jnp.where(hot, logprob, 0.0), axis=0, keepdims=True)
    chance = jnp.exp(picked)
    rest = 1.0 - chance
    weight = weight_ref[...]
    terms = -rest * rest * picked
    slope = weight * (2.0 * rest * chance * picked - rest * rest)
    grad = (slope * (jnp.where(hot, 1.0, 0.0) - jnp.exp(logprob))).astype(BF16)
    g_ref[...] = grad
    pair[0] = hidden
    pair[1] = second
    loss_part = jnp.sum(weight * terms)
    norm_part = jnp.sum(weight)
    for out_ref, which in ((send_ref, 1 - core), (keep_ref, core)):
        rows, cols = out_ref.shape
        row = lax.broadcasted_iota(jnp.int32, (rows, cols), 0)
        col = lax.broadcasted_iota(jnp.int32, (rows, cols), 1)
        extra = jnp.where(col == 0, loss_part, jnp.where(col == 1, norm_part, 0.0))
        out_ref[...] = jnp.where(row >= classes, extra, 0.0)
        out_ref[:classes, :] = dot_nt(grad, pair[which])


def backward_kernel(
    fanout, groups, core_ref, g_ref, hidden_ref, at_ref, w2s_ref, w2n_ref, f_ref, send_ref, keep_ref
):
    core = core_ref[0]
    scale = 1.0 / fanout
    grad = g_ref[...]
    at = at_ref[...]
    summed = dot_nt(grad, at)
    high = summed.astype(BF16)
    low = (summed - high.astype(F32)).astype(BF16)
    w2n = w2n_ref[...]
    hidden_grad = dot_tn(w2s_ref[...], grad) + (dot_tn(w2n, high) + dot_tn(w2n, low)) * scale
    pre_grad = jnp.where(hidden_ref[...] > 0, hidden_grad, 0.0).astype(BF16)
    proj_grad = (dot_nt(pre_grad, at) * scale).astype(BF16)
    features = f_ref[...]
    full = (dot_nt(features, pre_grad), dot_nt(features, proj_grad))
    rows = send_ref.shape[1] // 2
    first = core == 0
    for z in range(groups):
        for part in range(2):
            low_rows = full[part][2 * z * rows : (2 * z + 1) * rows]
            high_rows = full[part][(2 * z + 1) * rows : (2 * z + 2) * rows]
            send_ref[z, part * rows : (part + 1) * rows] = jnp.where(first, high_rows, low_rows)
            keep_ref[z, part * rows : (part + 1) * rows] = jnp.where(first, low_rows, high_rows)


def pair_kernel(classes, keep_ref, recv_ref, out_ref):
    total = keep_ref[...] + recv_ref[...]
    high = total.astype(BF16).astype(F32)
    rest = total - high
    middle = rest.astype(BF16).astype(F32)
    low = rest - middle
    row = lax.broadcasted_iota(jnp.int32, total.shape, 0)
    out_ref[...] = jnp.where(row == classes + 1, middle, jnp.where(row == classes + 2, low, high)).astype(BF16)


def chunk_kernel(groups, z_ref, keep_ref, recv_ref, own_ref, *out_refs):
    z = z_ref[0]
    own_ref[...] = keep_ref[z] + recv_ref[z]
    for s in range(1, groups):
        other = jnp.bitwise_xor(z, s)
        out_refs[s - 1][...] = (keep_ref[other] + recv_ref[other]).astype(BF16)


def second_sum_kernel(*refs):
    out_ref = refs[-1]
    out_ref[...] = tree_sum([r[...].astype(F32) for r in refs[:-1]])


def scalars(total, classes):
    row = lax.broadcasted_iota(jnp.int32, total.shape, 0)
    col = lax.broadcasted_iota(jnp.int32, total.shape, 1)
    inside = jnp.logical_and(row >= classes, row < classes + 3)
    loss = jnp.sum(jnp.where(jnp.logical_and(inside, col == 0), total, 0.0), keepdims=True)
    norm = jnp.sum(jnp.where(jnp.logical_and(inside, col == 1), total, 0.0), keepdims=True)
    return loss, norm


def second_out_kernel(classes, core_ref, own_ref, other_ref, out_ref, loss_ref):
    first = core_ref[0] == 0
    loss, norm = scalars(own_ref[...], classes)
    inverse = 1.0 / norm
    own = own_ref[:classes, :] * inverse
    other = other_ref[:classes, :] * inverse
    out_ref[:, 0, :] = jnp.where(first, own, other)
    out_ref[:, 1, :] = jnp.where(first, other, own)
    loss_ref[...] = loss * inverse


def first_out_kernel(classes, total_ref, own_ref, *refs):
    _, norm = scalars(total_ref[...], classes)
    out_ref = refs[-1]
    summed = tree_sum([own_ref[...]] + [r[...].astype(F32) for r in refs[:-1]]) * (1.0 / norm)
    rows = out_ref.shape[1]
    out_ref[0] = summed[:rows]
    out_ref[1] = summed[rows:]


def exchange(value, axis, step):
    size = lax.axis_size(axis)
    return lax.ppermute(value, axis, [(i, i ^ step) for i in range(size)])


def gather_parts(block, count):
    half = block.shape[0] // 2
    parts = [[block]]
    for s in range(1, count):
        low_bit = s & -s
        rest = s ^ low_bit
        if rest == 0:
            parts.append([exchange(block, "feat", s)])
        else:
            low = parts[rest][0][:half] if len(parts[rest]) == 1 else parts[rest][0]
            high = parts[low_bit][0][half:]
            parts.append([exchange(low, "feat", low_bit), exchange(high, "feat", rest)])
    return parts


def on_device(features, neighbors, labels, loss_weight, w1_self, w1_neigh, w2_self, w2_neigh):
    feat_count = lax.axis_size("feat")
    dp_count = lax.axis_size("dp")
    groups = dp_count // 2
    nodes, fanout = neighbors.shape
    rows, hid = w1_self.shape
    classes = w2_self.shape[1]
    place = lax.axis_index("dp").astype(jnp.int32)
    core = (place % 2).reshape(1)
    z = (place // 2).reshape(1)

    wide = gather_parts(features, feat_count)
    parts = tuple(len(block) for block in wide)
    mine_own = jnp.where(core[0] == 0, w1_self, w1_neigh)
    mine = [exchange(mine_own, "feat", s) for s in range(1, feat_count)]
    limit = 12 + 6 * nodes * nodes // (1024 * 1024)
    at, labels, loss_weight = call(
        functools.partial(count_kernel, fanout),
        [
            shape((nodes, nodes), BF16),
            shape((1, nodes), jnp.int32),
            shape((1, nodes), F32),
        ],
        [neighbors.T, labels.reshape(1, nodes), loss_weight.reshape(1, nodes)],
        flops=nodes * nodes * fanout,
    )
    mine_proj, *joined = call(
        functools.partial(mine_kernel, parts),
        [shape((hid, nodes), F32)] + [shape((rows, nodes), BF16)] * sum(count > 1 for count in parts),
        [core, w1_self, w1_neigh] + mine + [part for block in wide for part in block],
        flops=30 * nodes * hid * rows * feat_count,
        smem=(0,),
        limit=limit,
    )
    rest = iter(joined)
    whole = [block[0] if len(block) == 1 else next(rest) for block in wide]
    partner = [exchange(block, "dp", 1) for block in mine]
    w2s, w2n = w2_self.T, w2_neigh.T
    padded = (classes + 3 + 15) // 16 * 16
    send2, keep2, grad, hidden = call(
        functools.partial(forward_kernel, feat_count, fanout),
        [
            shape((padded, hid), F32),
            shape((padded, hid), F32),
            shape((classes, nodes), BF16),
            shape((hid, nodes), BF16),
        ],
        whole + [core, labels, loss_weight, at, w2s, w2n, w1_self, w1_neigh, mine_proj] + partner,
        scratch=[
            pltpu.VMEM((2, hid, nodes), F32),
            pltpu.VMEM((2, hid, nodes), BF16),
        ],
        flops=2 * nodes * hid * 2 * (rows * feat_count + nodes),
        smem=(feat_count,),
        limit=limit,
    )
    recv2 = exchange(send2, "dp", 1)
    chunk = 2 * (rows // dp_count)
    send1, keep1 = call(
        functools.partial(backward_kernel, fanout, groups),
        [shape((groups, chunk, hid), F32)] * 2,
        [core, grad, hidden, at, w2s, w2n, features],
        flops=2 * nodes * hid * 2 * (rows + nodes),
        smem=(0,),
        limit=limit,
    )
    recv1 = exchange(send1, "dp", 1)
    (own2,) = call(functools.partial(pair_kernel, classes), [shape((padded, hid), BF16)], [keep2, recv2])
    far2 = [exchange(own2, "dp", 2 * s) for s in range(1, groups)]
    own1, *chunks = call(
        functools.partial(chunk_kernel, groups),
        [shape((chunk, hid), F32)] + [shape((chunk, hid), BF16)] * (groups - 1),
        [z, keep1, recv1],
        smem=(0,),
    )
    far1 = [exchange(chunks[s - 1], "dp", 2 * s) for s in range(1, groups)]
    (total2,) = call(second_sum_kernel, [shape((padded, hid), F32)], [own2] + far2)
    other2 = exchange(total2, "dp", 1)
    (grad_w1,) = call(
        functools.partial(first_out_kernel, classes),
        [shape((2, rows // dp_count, hid), F32)],
        [total2, own1] + far1,
        flops=300 * rows * nodes * hid,
        final=True,
    )
    grad_w2, loss = call(
        functools.partial(second_out_kernel, classes),
        [shape((classes, 2, hid), F32), shape((1, 1), F32)],
        [core, total2, other2],
        smem=(0,),
        final=True,
    )
    return loss[0, 0], grad_w1, grad_w2.transpose(1, 2, 0)


def solution(mesh):
    in_specs = (
        P("feat", "dp"),
        P("dp", None),
        P("dp"),
        P("dp"),
        P("feat", None),
        P("feat", None),
        P(),
        P(),
    )
    out_specs = (P(), P(None, ("feat", "dp"), None), P())
    return jax.shard_map(
        on_device, mesh=mesh, in_specs=in_specs, out_specs=out_specs, check_vma=False
    )
```

```python
import functools

import jax
import jax.numpy as jnp
from jax import lax
from jax.experimental import pallas as pl
from jax.experimental.pallas import tpu as pltpu
from jax.sharding import PartitionSpec as P

BF16 = jnp.bfloat16
F32 = jnp.float32


def dot_nn(left, right):
    return lax.dot_general(left, right, (((1,), (0,)), ((), ())), preferred_element_type=F32)


def dot_nt(left, right):
    return lax.dot_general(left, right, (((1,), (1,)), ((), ())), preferred_element_type=F32)


def dot_tn(left, right):
    return lax.dot_general(left, right, (((0,), (0,)), ((), ())), preferred_element_type=F32)


def tree_sum(terms):
    terms = list(terms)
    while len(terms) > 1:
        terms = [terms[i] + terms[i + 1] for i in range(0, len(terms), 2)]
    return terms[0]


def call(kernel, outs, args, flops=0, scratch=(), smem=(), limit=16, final=False):
    size = sum(a.size * a.dtype.itemsize for a in args)
    size += sum(o.dtype.itemsize * o.size for o in outs)
    spaces = [pltpu.SMEM if i in smem else pltpu.VMEM for i in range(len(args))]
    placed = [a if i in smem else pltpu.with_memory_space_constraint(a, pltpu.VMEM) for i, a in enumerate(args)]
    return pl.pallas_call(
        kernel,
        out_shape=outs if final else [pltpu.VMEM(o.shape, o.dtype) for o in outs],
        in_specs=[pl.BlockSpec(memory_space=space) for space in spaces],
        out_specs=[pl.BlockSpec(memory_space=pltpu.VMEM)] * len(outs),
        scratch_shapes=list(scratch),
        cost_estimate=pl.CostEstimate(flops=flops, bytes_accessed=size, transcendentals=0),
        compiler_params=pltpu.CompilerParams(vmem_limit_bytes=limit * 1024 * 1024),
    )(*placed)


def shape(dims, dtype):
    return jax.ShapeDtypeStruct(dims, dtype)


def count_kernel(fanout, nbr_ref, *refs):
    passing = len(refs) // 2
    at_ref = refs[passing]
    for i in range(passing):
        refs[passing + 1 + i][...] = refs[i][...]
    nodes = at_ref.shape[1]
    step = 32

    def body(i, carry):
        row = lax.broadcasted_iota(jnp.int32, (step, nodes), 0) + i * step
        total = jnp.zeros((step, nodes), F32)
        for k in range(fanout):
            total = total + jnp.where(nbr_ref[k : k + 1, :] == row, 1.0, 0.0)
        at_ref[pl.ds(pl.multiple_of(i * step, step), step), :] = total.astype(BF16)
        return carry

    lax.fori_loop(0, nodes // step, body, 0)


def project(own, others_refs, f_refs):
    products = [dot_tn(own, f_refs[0][...])]
    for s in range(1, len(f_refs)):
        products.append(dot_tn(others_refs[s - 1][...], f_refs[s][...]))
    return tree_sum(products)


def mine_kernel(parts, core_ref, ws_ref, wn_ref, *refs):
    mine_refs, refs = refs[: len(parts) - 1], refs[len(parts) - 1 :]
    out_ref, joined_refs = refs[sum(parts)], refs[sum(parts) + 1 :]
    own = jnp.where(core_ref[0] == 0, ws_ref[...], wn_ref[...])
    blocks, at, done = [], 0, 0
    for count in parts:
        block = refs[at]
        if count > 1:
            block, start = joined_refs[done], 0
            for ref in refs[at : at + count]:
                block[start : start + ref.shape[0]] = ref[...]
                start += ref.shape[0]
            done += 1
        blocks.append(block)
        at += count
    out_ref[...] = project(own, mine_refs, blocks)


def forward_kernel(feat_count, fanout, *refs):
    f_refs, refs = refs[:feat_count], refs[feat_count:]
    core_ref, labels_ref, weight_ref, at_ref, w2s_ref, w2n_ref, ws_ref, wn_ref, mine_ref = refs[:9]
    partner_refs = refs[9 : 8 + feat_count]
    send_ref, keep_ref, g_ref, hidden_ref, proj, pair = refs[8 + feat_count :]
    core = core_ref[0]
    classes = w2s_ref.shape[0]
    nodes = at_ref.shape[1]
    scale = 1.0 / fanout
    own = jnp.where(core == 0, wn_ref[...], ws_ref[...])
    proj[core] = mine_ref[...]
    proj[1 - core] = project(own, partner_refs, f_refs)
    at = at_ref[...]
    pre = proj[0] + dot_nn(proj[1].astype(BF16), at) * scale
    hidden = jnp.maximum(pre, 0.0).astype(BF16)
    hidden_ref[...] = hidden
    second = (dot_nn(hidden, at) * scale).astype(BF16)
    logits = dot_nn(w2s_ref[...], hidden) + dot_nn(w2n_ref[...], second)
    shifted = logits - jnp.max(logits, axis=0, keepdims=True)
    logprob = shifted - jnp.log(jnp.sum(jnp.exp(shifted), axis=0, keepdims=True))
    hot = lax.broadcasted_iota(jnp.int32, (classes, nodes), 0) == labels_ref[...]
    picked = jnp.sum(jnp.where(hot, logprob, 0.0), axis=0, keepdims=True)
    chance = jnp.exp(picked)
    rest = 1.0 - chance
    weight = weight_ref[...]
    terms = -rest * rest * picked
    slope = weight * (2.0 * rest * chance * picked - rest * rest)
    grad = (slope * (jnp.where(hot, 1.0, 0.0) - jnp.exp(logprob))).astype(BF16)
    g_ref[...] = grad
    pair[0] = hidden
    pair[1] = second
    loss_part = jnp.sum(weight * terms)
    norm_part = jnp.sum(weight)
    for out_ref, which in ((send_ref, 1 - core), (keep_ref, core)):
        rows, cols = out_ref.shape
        row = lax.broadcasted_iota(jnp.int32, (rows, cols), 0)
        col = lax.broadcasted_iota(jnp.int32, (rows, cols), 1)
        extra = jnp.where(col == 0, loss_part, jnp.where(col == 1, norm_part, 0.0))
        out_ref[...] = jnp.where(row >= classes, extra, 0.0)
        out_ref[:classes, :] = dot_nt(grad, pair[which])


def backward_kernel(
    fanout, groups, core_ref, g_ref, hidden_ref, at_ref, w2s_ref, w2n_ref, f_ref, send_ref, keep_ref
):
    core = core_ref[0]
    scale = 1.0 / fanout
    grad = g_ref[...]
    at = at_ref[...]
    summed = dot_nt(grad, at)
    high = summed.astype(BF16)
    low = (summed - high.astype(F32)).astype(BF16)
    w2n = w2n_ref[...]
    hidden_grad = dot_tn(w2s_ref[...], grad) + (dot_tn(w2n, high) + dot_tn(w2n, low)) * scale
    pre_grad = jnp.where(hidden_ref[...] > 0, hidden_grad, 0.0).astype(BF16)
    proj_grad = (dot_nt(pre_grad, at) * scale).astype(BF16)
    features = f_ref[...]
    full = (dot_nt(features, pre_grad), dot_nt(features, proj_grad))
    rows = send_ref.shape[1] // 2
    first = core == 0
    for z in range(groups):
        for part in range(2):
            low_rows = full[part][2 * z * rows : (2 * z + 1) * rows]
            high_rows = full[part][(2 * z + 1) * rows : (2 * z + 2) * rows]
            send_ref[z, part * rows : (part + 1) * rows] = jnp.where(first, high_rows, low_rows)
            keep_ref[z, part * rows : (part + 1) * rows] = jnp.where(first, low_rows, high_rows)


def pair_kernel(classes, keep_ref, recv_ref, out_ref):
    total = keep_ref[...] + recv_ref[...]
    high = total.astype(BF16).astype(F32)
    rest = total - high
    middle = rest.astype(BF16).astype(F32)
    low = rest - middle
    row = lax.broadcasted_iota(jnp.int32, total.shape, 0)
    out_ref[...] = jnp.where(row == classes + 1, middle, jnp.where(row == classes + 2, low, high)).astype(BF16)


def chunk_kernel(groups, z_ref, keep_ref, recv_ref, own_ref, *out_refs):
    z = z_ref[0]
    own_ref[...] = keep_ref[z] + recv_ref[z]
    for s in range(1, groups):
        other = jnp.bitwise_xor(z, s)
        out_refs[s - 1][...] = (keep_ref[other] + recv_ref[other]).astype(BF16)


def second_sum_kernel(*refs):
    out_ref = refs[-1]
    out_ref[...] = tree_sum([r[...].astype(F32) for r in refs[:-1]])


def scalars(total, classes):
    row = lax.broadcasted_iota(jnp.int32, total.shape, 0)
    col = lax.broadcasted_iota(jnp.int32, total.shape, 1)
    inside = jnp.logical_and(row >= classes, row < classes + 3)
    loss = jnp.sum(jnp.where(jnp.logical_and(inside, col == 0), total, 0.0), keepdims=True)
    norm = jnp.sum(jnp.where(jnp.logical_and(inside, col == 1), total, 0.0), keepdims=True)
    return loss, norm


def first_sum_kernel(own_ref, *refs):
    refs[-1][...] = tree_sum([own_ref[...]] + [r[...].astype(F32) for r in refs[:-1]])


def out_kernel(classes, core_ref, own_ref, other_ref, first_ref, grad1_ref, grad2_ref, loss_ref):
    first = core_ref[0] == 0
    loss, norm = scalars(own_ref[...], classes)
    inverse = 1.0 / norm
    own = own_ref[:classes, :] * inverse
    other = other_ref[:classes, :] * inverse
    grad2_ref[:, 0, :] = jnp.where(first, own, other)
    grad2_ref[:, 1, :] = jnp.where(first, other, own)
    loss_ref[...] = loss * inverse
    rows = grad1_ref.shape[1]
    grad1_ref[0] = first_ref[:rows] * inverse
    grad1_ref[1] = first_ref[rows:] * inverse


def exchange(value, axis, step):
    size = lax.axis_size(axis)
    return lax.ppermute(value, axis, [(i, i ^ step) for i in range(size)])


def gather_parts(block, count):
    half = block.shape[0] // 2
    parts = [[block]]
    for s in range(1, count):
        low_bit = s & -s
        rest = s ^ low_bit
        if rest == 0:
            parts.append([exchange(block, "feat", s)])
        else:
            low = parts[rest][0][:half] if len(parts[rest]) == 1 else parts[rest][0]
            high = parts[low_bit][0][half:]
            parts.append([exchange(low, "feat", low_bit), exchange(high, "feat", rest)])
    return parts


def on_device(features, neighbors, labels, loss_weight, w1_self, w1_neigh, w2_self, w2_neigh):
    feat_count = lax.axis_size("feat")
    dp_count = lax.axis_size("dp")
    groups = dp_count // 2
    nodes, fanout = neighbors.shape
    rows, hid = w1_self.shape
    classes = w2_self.shape[1]
    place = lax.axis_index("dp").astype(jnp.int32)
    core = (place % 2).reshape(1)
    z = (place // 2).reshape(1)

    wide = gather_parts(features, feat_count)
    parts = tuple(len(block) for block in wide)
    mine_own = jnp.where(core[0] == 0, w1_self, w1_neigh)
    mine = [exchange(mine_own, "feat", s) for s in range(1, feat_count)]
    limit = 12 + 6 * nodes * nodes // (1024 * 1024)
    passing = [labels.reshape(1, nodes), loss_weight.reshape(1, nodes), w2_self.T, w2_neigh.T]
    at, labels, loss_weight, w2s, w2n = call(
        functools.partial(count_kernel, fanout),
        [shape((nodes, nodes), BF16)] + [shape(p.shape, p.dtype) for p in passing],
        [neighbors.T] + passing,
        flops=nodes * nodes * fanout,
    )
    mine_proj, *joined = call(
        functools.partial(mine_kernel, parts),
        [shape((hid, nodes), F32)] + [shape((rows, nodes), BF16)] * sum(count > 1 for count in parts),
        [core, w1_self, w1_neigh] + mine + [part for block in wide for part in block],
        flops=30 * nodes * hid * rows * feat_count,
        smem=(0,),
        limit=limit,
    )
    rest = iter(joined)
    whole = [block[0] if len(block) == 1 else next(rest) for block in wide]
    partner = [exchange(block, "dp", 1) for block in mine]
    padded = (classes + 3 + 15) // 16 * 16
    send2, keep2, grad, hidden = call(
        functools.partial(forward_kernel, feat_count, fanout),
        [
            shape((padded, hid), F32),
            shape((padded, hid), F32),
            shape((classes, nodes), BF16),
            shape((hid, nodes), BF16),
        ],
        whole + [core, labels, loss_weight, at, w2s, w2n, w1_self, w1_neigh, mine_proj] + partner,
        scratch=[
            pltpu.VMEM((2, hid, nodes), F32),
            pltpu.VMEM((2, hid, nodes), BF16),
        ],
        flops=2 * nodes * hid * 2 * (rows * feat_count + nodes),
        smem=(feat_count,),
        limit=limit,
    )
    recv2 = exchange(send2, "dp", 1)
    chunk = 2 * (rows // dp_count)
    send1, keep1 = call(
        functools.partial(backward_kernel, fanout, groups),
        [shape((groups, chunk, hid), F32)] * 2,
        [core, grad, hidden, at, w2s, w2n, features],
        flops=2 * nodes * hid * 2 * (rows + nodes),
        smem=(0,),
        limit=limit,
    )
    recv1 = exchange(send1, "dp", 1)
    (own2,) = call(functools.partial(pair_kernel, classes), [shape((padded, hid), BF16)], [keep2, recv2])
    far2 = [exchange(own2, "dp", 2 * s) for s in range(1, groups)]
    own1, *chunks = call(
        functools.partial(chunk_kernel, groups),
        [shape((chunk, hid), F32)] + [shape((chunk, hid), BF16)] * (groups - 1),
        [z, keep1, recv1],
        smem=(0,),
    )
    far1 = [exchange(chunks[s - 1], "dp", 2 * s) for s in range(1, groups)]
    (total2,) = call(second_sum_kernel, [shape((padded, hid), F32)], [own2] + far2)
    other2 = exchange(total2, "dp", 1)
    (sum1,) = call(first_sum_kernel, [shape((chunk, hid), F32)], [own1] + far1, flops=300 * rows * nodes * hid)
    grad_w1, grad_w2, loss = call(
        functools.partial(out_kernel, classes),
        [shape((2, rows // dp_count, hid), F32), shape((classes, 2, hid), F32), shape((1, 1), F32)],
        [core, total2, other2, sum1],
        smem=(0,),
        final=True,
    )
    return loss[0, 0], grad_w1, grad_w2.transpose(1, 2, 0)


def solution(mesh):
    in_specs = (
        P("feat", "dp"),
        P("dp", None),
        P("dp"),
        P("dp"),
        P("feat", None),
        P("feat", None),
        P(),
        P(),
    )
    out_specs = (P(), P(None, ("feat", "dp"), None), P())
    return jax.shard_map(
        on_device, mesh=mesh, in_specs=in_specs, out_specs=out_specs, check_vma=False
    )
```

```python
import functools

import jax
import jax.numpy as jnp
from jax import lax
from jax.experimental import pallas as pl
from jax.experimental.pallas import tpu as pltpu
from jax.sharding import PartitionSpec as P

BF16 = jnp.bfloat16
F32 = jnp.float32


def dot_nn(left, right):
    return lax.dot_general(left, right, (((1,), (0,)), ((), ())), preferred_element_type=F32)


def dot_nt(left, right):
    return lax.dot_general(left, right, (((1,), (1,)), ((), ())), preferred_element_type=F32)


def dot_tn(left, right):
    return lax.dot_general(left, right, (((0,), (0,)), ((), ())), preferred_element_type=F32)


def tree_sum(terms):
    terms = list(terms)
    while len(terms) > 1:
        terms = [terms[i] + terms[i + 1] for i in range(0, len(terms), 2)]
    return terms[0]


def call(kernel, outs, args, flops=0, scratch=(), smem=(), limit=16, final=False):
    size = sum(a.size * a.dtype.itemsize for a in args)
    size += sum(o.dtype.itemsize * o.size for o in outs)
    spaces = [pltpu.SMEM if i in smem else pltpu.VMEM for i in range(len(args))]
    placed = [a if i in smem else pltpu.with_memory_space_constraint(a, pltpu.VMEM) for i, a in enumerate(args)]
    return pl.pallas_call(
        kernel,
        out_shape=outs if final else [pltpu.VMEM(o.shape, o.dtype) for o in outs],
        in_specs=[pl.BlockSpec(memory_space=space) for space in spaces],
        out_specs=[pl.BlockSpec(memory_space=pltpu.VMEM)] * len(outs),
        scratch_shapes=list(scratch),
        cost_estimate=pl.CostEstimate(flops=flops, bytes_accessed=size, transcendentals=0),
        compiler_params=pltpu.CompilerParams(vmem_limit_bytes=limit * 1024 * 1024),
    )(*placed)


def shape(dims, dtype):
    return jax.ShapeDtypeStruct(dims, dtype)


def count_kernel(fanout, nbr_ref, *refs):
    passing = len(refs) // 2
    at_ref = refs[passing]
    for i in range(passing):
        refs[passing + 1 + i][...] = refs[i][...]
    nodes = at_ref.shape[1]
    step = 32

    def body(i, carry):
        row = lax.broadcasted_iota(jnp.int32, (step, nodes), 0) + i * step
        total = jnp.zeros((step, nodes), F32)
        for k in range(fanout):
            total = total + jnp.where(nbr_ref[k : k + 1, :] == row, 1.0, 0.0)
        at_ref[pl.ds(pl.multiple_of(i * step, step), step), :] = total.astype(BF16)
        return carry

    lax.fori_loop(0, nodes // step, body, 0)


def early_nodes(early, first, last):
    if all(s in early for s in range(first, last)):
        return [(first, last)]
    if last - first == 1:
        return []
    middle = (first + last) // 2
    return early_nodes(early, first, middle) + early_nodes(early, middle, last)


def tree_product(first, last, known, leaf):
    if (first, last) in known:
        return known[(first, last)][...]
    if last - first == 1:
        return leaf(first)
    middle = (first + last) // 2
    return tree_product(first, middle, known, leaf) + tree_product(middle, last, known, leaf)


def early_kernel(nodes_mine, early, core_ref, ws_ref, wn_ref, *refs):
    f_refs = dict(zip(early, refs))
    w_refs = dict(zip(early[1:], refs[len(early) :]))
    outs = refs[2 * len(early) - 1 :]
    first = core_ref[0] == 0
    own = jnp.where(first, ws_ref[...], wn_ref[...])
    other = jnp.where(first, wn_ref[...], ws_ref[...])
    for (begin, end), out_ref in zip(nodes_mine, outs):
        leaf = lambda s: dot_tn(own if s == 0 else w_refs[s][...], f_refs[s][...])
        out_ref[...] = tree_product(begin, end, {}, leaf)
    outs[-1][...] = dot_tn(other, f_refs[0][...])


def mine_kernel(nodes_mine, late, feat_count, *refs):
    known = dict(zip(nodes_mine, refs))
    refs = refs[len(nodes_mine) :]
    w_refs = dict(zip(late, refs))
    halves = refs[len(late) : 3 * len(late)]
    out_ref, joined = refs[3 * len(late)], refs[3 * len(late) + 1 :]
    for i, block in enumerate(joined):
        low, high = halves[2 * i : 2 * i + 2]
        block[: low.shape[0]] = low[...]
        block[low.shape[0] :] = high[...]
    f_refs = dict(zip(late, joined))
    out_ref[...] = tree_product(0, feat_count, known, lambda s: dot_tn(w_refs[s][...], f_refs[s][...]))


def forward_kernel(feat_count, fanout, *refs):
    f_refs, refs = refs[: feat_count - 1], refs[feat_count - 1 :]
    core_ref, labels_ref, weight_ref, at_ref, w2s_ref, w2n_ref, mine_ref, other_ref = refs[:8]
    partner_refs = refs[8 : 7 + feat_count]
    send_ref, keep_ref, g_ref, hidden_ref, proj, pair = refs[7 + feat_count :]
    core = core_ref[0]
    classes = w2s_ref.shape[0]
    nodes = at_ref.shape[1]
    scale = 1.0 / fanout
    proj[core] = mine_ref[...]
    proj[1 - core] = tree_product(
        0, feat_count, {(0, 1): other_ref}, lambda s: dot_tn(partner_refs[s - 1][...], f_refs[s - 1][...])
    )
    at = at_ref[...]
    pre = proj[0] + dot_nn(proj[1].astype(BF16), at) * scale
    hidden = jnp.maximum(pre, 0.0).astype(BF16)
    hidden_ref[...] = hidden
    second = (dot_nn(hidden, at) * scale).astype(BF16)
    logits = dot_nn(w2s_ref[...], hidden) + dot_nn(w2n_ref[...], second)
    shifted = logits - jnp.max(logits, axis=0, keepdims=True)
    powers = jnp.exp(shifted)
    total = jnp.sum(powers, axis=0, keepdims=True)
    hot = lax.broadcasted_iota(jnp.int32, (classes, nodes), 0) == labels_ref[...]
    picked = jnp.sum(jnp.where(hot, shifted, 0.0), axis=0, keepdims=True) - jnp.log(total)
    chance = jnp.exp(picked)
    rest = 1.0 - chance
    weight = weight_ref[...]
    terms = -rest * rest * picked
    slope = weight * (2.0 * rest * chance * picked - rest * rest)
    grad = (jnp.where(hot, slope, 0.0) - (slope / total) * powers).astype(BF16)
    g_ref[...] = grad
    pair[0] = hidden
    pair[1] = second
    loss_part = jnp.sum(weight * terms)
    norm_part = jnp.sum(weight)
    for out_ref, which in ((send_ref, 1 - core), (keep_ref, core)):
        rows, cols = out_ref.shape
        row = lax.broadcasted_iota(jnp.int32, (rows, cols), 0)
        col = lax.broadcasted_iota(jnp.int32, (rows, cols), 1)
        extra = jnp.where(col == 0, loss_part, jnp.where(col == 1, norm_part, 0.0))
        out_ref[...] = jnp.where(row >= classes, extra, 0.0)
        out_ref[:classes, :] = dot_nt(grad, pair[which])


def backward_kernel(
    fanout, groups, core_ref, g_ref, hidden_ref, at_ref, w2s_ref, w2n_ref, f_ref, send_ref, keep_ref
):
    core = core_ref[0]
    scale = 1.0 / fanout
    grad = g_ref[...]
    at = at_ref[...]
    summed = dot_nt(grad, at)
    high = summed.astype(BF16)
    low = (summed - high.astype(F32)).astype(BF16)
    w2n = w2n_ref[...]
    hidden_grad = dot_tn(w2s_ref[...], grad) + (dot_tn(w2n, high) + dot_tn(w2n, low)) * scale
    pre_grad = jnp.where(hidden_ref[...] > 0, hidden_grad, 0.0).astype(BF16)
    proj_grad = (dot_nt(pre_grad, at) * scale).astype(BF16)
    features = f_ref[...]
    full = (dot_nt(features, pre_grad), dot_nt(features, proj_grad))
    rows = send_ref.shape[1] // 2
    first = core == 0
    for z in range(groups):
        for part in range(2):
            low_rows = full[part][2 * z * rows : (2 * z + 1) * rows]
            high_rows = full[part][(2 * z + 1) * rows : (2 * z + 2) * rows]
            send_ref[z, part * rows : (part + 1) * rows] = jnp.where(first, high_rows, low_rows)
            keep_ref[z, part * rows : (part + 1) * rows] = jnp.where(first, low_rows, high_rows)


def pair_kernel(classes, keep_ref, recv_ref, out_ref):
    total = keep_ref[...] + recv_ref[...]
    high = total.astype(BF16).astype(F32)
    rest = total - high
    middle = rest.astype(BF16).astype(F32)
    low = rest - middle
    row = lax.broadcasted_iota(jnp.int32, total.shape, 0)
    out_ref[...] = jnp.where(row == classes + 1, middle, jnp.where(row == classes + 2, low, high)).astype(BF16)


def chunk_kernel(groups, z_ref, keep_ref, recv_ref, own_ref, *out_refs):
    z = z_ref[0]
    own_ref[...] = keep_ref[z] + recv_ref[z]
    for s in range(1, groups):
        other = jnp.bitwise_xor(z, s)
        out_refs[s - 1][...] = (keep_ref[other] + recv_ref[other]).astype(BF16)


def second_sum_kernel(*refs):
    out_ref = refs[-1]
    out_ref[...] = tree_sum([r[...].astype(F32) for r in refs[:-1]])


def scalars(total, classes):
    row = lax.broadcasted_iota(jnp.int32, total.shape, 0)
    col = lax.broadcasted_iota(jnp.int32, total.shape, 1)
    inside = jnp.logical_and(row >= classes, row < classes + 3)
    loss = jnp.sum(jnp.where(jnp.logical_and(inside, col == 0), total, 0.0), keepdims=True)
    norm = jnp.sum(jnp.where(jnp.logical_and(inside, col == 1), total, 0.0), keepdims=True)
    return loss, norm


def first_sum_kernel(own_ref, *refs):
    refs[-1][...] = tree_sum([own_ref[...]] + [r[...].astype(F32) for r in refs[:-1]])


def out_kernel(classes, core_ref, own_ref, other_ref, first_ref, grad1_ref, grad2_ref, loss_ref):
    first = core_ref[0] == 0
    loss, norm = scalars(own_ref[...], classes)
    inverse = 1.0 / norm
    own = own_ref[:classes, :] * inverse
    other = other_ref[:classes, :] * inverse
    for slot, half in enumerate((jnp.where(first, own, other), jnp.where(first, other, own))):
        lanes = half.shape[1] // 128
        for j in range(lanes):
            grad2_ref[pl.ds(2 * j + slot, classes, stride=2 * lanes), :] = half[:, 128 * j : 128 * (j + 1)]
    loss_ref[...] = loss * inverse
    rows = grad1_ref.shape[1]
    grad1_ref[0] = first_ref[:rows] * inverse
    grad1_ref[1] = first_ref[rows:] * inverse


def exchange(value, axis, step):
    size = lax.axis_size(axis)
    return lax.ppermute(value, axis, [(i, i ^ step) for i in range(size)])


def gather_parts(block, count):
    half = block.shape[0] // 2
    parts = [[block]]
    for s in range(1, count):
        low_bit = s & -s
        rest = s ^ low_bit
        if rest == 0:
            parts.append([exchange(block, "feat", s)])
        else:
            low = parts[rest][0][:half] if len(parts[rest]) == 1 else parts[rest][0]
            high = parts[low_bit][0][half:]
            parts.append([exchange(low, "feat", low_bit), exchange(high, "feat", rest)])
    return parts


def on_device(features, neighbors, labels, loss_weight, w1_self, w1_neigh, w2_self, w2_neigh):
    feat_count = lax.axis_size("feat")
    dp_count = lax.axis_size("dp")
    groups = dp_count // 2
    nodes, fanout = neighbors.shape
    rows, hid = w1_self.shape
    classes = w2_self.shape[1]
    place = lax.axis_index("dp").astype(jnp.int32)
    core = (place % 2).reshape(1)
    z = (place // 2).reshape(1)

    wide = gather_parts(features, feat_count)
    early = [s for s in range(feat_count) if len(wide[s]) == 1]
    late = [s for s in range(feat_count) if len(wide[s]) > 1]
    nodes_mine = early_nodes(early, 0, feat_count)
    mine_own = jnp.where(core[0] == 0, w1_self, w1_neigh)
    mine = [exchange(mine_own, "feat", s) for s in range(1, feat_count)]
    limit = 12 + 6 * nodes * nodes // (1024 * 1024)
    passing = [labels.reshape(1, nodes), loss_weight.reshape(1, nodes), w2_self.T, w2_neigh.T]
    at, labels, loss_weight, w2s, w2n = call(
        functools.partial(count_kernel, fanout),
        [shape((nodes, nodes), BF16)] + [shape(p.shape, p.dtype) for p in passing],
        [neighbors.T] + passing,
        flops=nodes * nodes * fanout,
    )
    *known, other_proj = call(
        functools.partial(early_kernel, nodes_mine, early),
        [shape((hid, nodes), F32)] * (len(nodes_mine) + 1),
        [core, w1_self, w1_neigh] + [wide[s][0] for s in early] + [mine[s - 1] for s in early[1:]],
        flops=2 * nodes * hid * rows * (len(early) + 1),
        smem=(0,),
        limit=limit,
    )
    mine_proj, *joined = call(
        functools.partial(mine_kernel, nodes_mine, late, feat_count),
        [shape((hid, nodes), F32)] + [shape((rows, nodes), BF16)] * len(late),
        known + [mine[s - 1] for s in late] + [part for s in late for part in wide[s]],
        flops=30 * nodes * hid * rows * feat_count,
        limit=limit,
    )
    rest = iter(joined)
    whole = [block[0] if len(block) == 1 else next(rest) for block in wide]
    partner = [exchange(block, "dp", 1) for block in mine]
    padded = (classes + 3 + 15) // 16 * 16
    send2, keep2, grad, hidden = call(
        functools.partial(forward_kernel, feat_count, fanout),
        [
            shape((padded, hid), F32),
            shape((padded, hid), F32),
            shape((classes, nodes), BF16),
            shape((hid, nodes), BF16),
        ],
        whole[1:] + [core, labels, loss_weight, at, w2s, w2n, mine_proj, other_proj] + partner,
        scratch=[
            pltpu.VMEM((2, hid, nodes), F32),
            pltpu.VMEM((2, hid, nodes), BF16),
        ],
        flops=2 * nodes * hid * 2 * (rows * feat_count + nodes),
        smem=(feat_count - 1,),
        limit=limit,
    )
    recv2 = exchange(send2, "dp", 1)
    chunk = 2 * (rows // dp_count)
    send1, keep1 = call(
        functools.partial(backward_kernel, fanout, groups),
        [shape((groups, chunk, hid), F32)] * 2,
        [core, grad, hidden, at, w2s, w2n, features],
        flops=2 * nodes * hid * 2 * (rows + nodes),
        smem=(0,),
        limit=limit,
    )
    recv1 = exchange(send1, "dp", 1)
    (own2,) = call(functools.partial(pair_kernel, classes), [shape((padded, hid), BF16)], [keep2, recv2])
    far2 = [exchange(own2, "dp", 2 * s) for s in range(1, groups)]
    own1, *chunks = call(
        functools.partial(chunk_kernel, groups),
        [shape((chunk, hid), F32)] + [shape((chunk, hid), BF16)] * (groups - 1),
        [z, keep1, recv1],
        smem=(0,),
    )
    far1 = [exchange(chunks[s - 1], "dp", 2 * s) for s in range(1, groups)]
    (total2,) = call(second_sum_kernel, [shape((padded, hid), F32)], far2[::-1] + [own2])
    other2 = exchange(total2, "dp", 1)
    (sum1,) = call(first_sum_kernel, [shape((chunk, hid), F32)], [own1] + far1, flops=300 * rows * nodes * hid)
    grad_w1, grad_w2, loss = call(
        functools.partial(out_kernel, classes),
        [shape((2, rows // dp_count, hid), F32), shape((classes * 2 * (hid // 128), 128), F32), shape((1, 1), F32)],
        [core, total2, other2, sum1],
        smem=(0,),
        final=True,
    )
    grad_w2 = grad_w2.reshape(classes, hid // 128, 2, 128).transpose(2, 1, 3, 0).reshape(2, hid, classes)
    return loss[0, 0], grad_w1, grad_w2


def solution(mesh):
    in_specs = (
        P("feat", "dp"),
        P("dp", None),
        P("dp"),
        P("dp"),
        P("feat", None),
        P("feat", None),
        P(),
        P(),
    )
    out_specs = (P(), P(None, ("feat", "dp"), None), P())
    return jax.shard_map(
        on_device, mesh=mesh, in_specs=in_specs, out_specs=out_specs, check_vma=False
    )
```

```python
import functools

import jax
import jax.numpy as jnp
from jax import lax
from jax.experimental import pallas as pl
from jax.experimental.pallas import tpu as pltpu
from jax.sharding import PartitionSpec as P

BF16 = jnp.bfloat16
F32 = jnp.float32


def dot_nn(left, right):
    return lax.dot_general(left, right, (((1,), (0,)), ((), ())), preferred_element_type=F32)


def dot_nt(left, right):
    return lax.dot_general(left, right, (((1,), (1,)), ((), ())), preferred_element_type=F32)


def dot_tn(left, right):
    return lax.dot_general(left, right, (((0,), (0,)), ((), ())), preferred_element_type=F32)


def tree_sum(terms):
    terms = list(terms)
    while len(terms) > 1:
        terms = [terms[i] + terms[i + 1] for i in range(0, len(terms), 2)]
    return terms[0]


def call(kernel, outs, args, flops=0, scratch=(), smem=(), limit=16, final=False):
    size = sum(a.size * a.dtype.itemsize for a in args)
    size += sum(o.dtype.itemsize * o.size for o in outs)
    spaces = [pltpu.SMEM if i in smem else pltpu.VMEM for i in range(len(args))]
    placed = [a if i in smem else pltpu.with_memory_space_constraint(a, pltpu.VMEM) for i, a in enumerate(args)]
    return pl.pallas_call(
        kernel,
        out_shape=outs if final else [pltpu.VMEM(o.shape, o.dtype) for o in outs],
        in_specs=[pl.BlockSpec(memory_space=space) for space in spaces],
        out_specs=[pl.BlockSpec(memory_space=pltpu.VMEM)] * len(outs),
        scratch_shapes=list(scratch),
        cost_estimate=pl.CostEstimate(flops=flops, bytes_accessed=size, transcendentals=0),
        compiler_params=pltpu.CompilerParams(vmem_limit_bytes=limit * 1024 * 1024),
    )(*placed)


def shape(dims, dtype):
    return jax.ShapeDtypeStruct(dims, dtype)


def count_kernel(fanout, nbr_ref, *refs):
    passing = len(refs) // 2
    at_ref = refs[passing]
    for i in range(passing):
        refs[passing + 1 + i][...] = refs[i][...]
    nodes = at_ref.shape[1]
    step = 32

    def body(i, carry):
        row = lax.broadcasted_iota(jnp.int32, (step, nodes), 0) + i * step
        total = jnp.zeros((step, nodes), F32)
        for k in range(fanout):
            total = total + jnp.where(nbr_ref[k : k + 1, :] == row, 1.0, 0.0)
        at_ref[pl.ds(pl.multiple_of(i * step, step), step), :] = total.astype(BF16)
        return carry

    lax.fori_loop(0, nodes // step, body, 0)


def early_nodes(early, first, last):
    if all(s in early for s in range(first, last)):
        return [(first, last)]
    if last - first == 1:
        return []
    middle = (first + last) // 2
    return early_nodes(early, first, middle) + early_nodes(early, middle, last)


def tree_product(first, last, known, leaf):
    if (first, last) in known:
        return known[(first, last)][...]
    if last - first == 1:
        return leaf(first)
    middle = (first + last) // 2
    return tree_product(first, middle, known, leaf) + tree_product(middle, last, known, leaf)


def early_kernel(nodes_mine, early, core_ref, ws_ref, wn_ref, *refs):
    f_refs = dict(zip(early, refs))
    w_refs = dict(zip(early[1:], refs[len(early) :]))
    outs = refs[2 * len(early) - 1 :]
    first = core_ref[0] == 0
    own = jnp.where(first, ws_ref[...], wn_ref[...])
    other = jnp.where(first, wn_ref[...], ws_ref[...])
    for (begin, end), out_ref in zip(nodes_mine, outs):
        leaf = lambda s: dot_tn(own if s == 0 else w_refs[s][...], f_refs[s][...])
        out_ref[...] = tree_product(begin, end, {}, leaf)
    outs[-1][...] = dot_tn(other, f_refs[0][...])


def mine_kernel(nodes_mine, late, feat_count, *refs):
    known = dict(zip(nodes_mine, refs))
    refs = refs[len(nodes_mine) :]
    w_refs = dict(zip(late, refs))
    halves = refs[len(late) : 3 * len(late)]
    out_ref, joined = refs[3 * len(late)], refs[3 * len(late) + 1 :]
    for i, block in enumerate(joined):
        low, high = halves[2 * i : 2 * i + 2]
        block[: low.shape[0]] = low[...]
        block[low.shape[0] :] = high[...]
    f_refs = dict(zip(late, joined))
    out_ref[...] = tree_product(0, feat_count, known, lambda s: dot_tn(w_refs[s][...], f_refs[s][...]))


def forward_kernel(feat_count, fanout, *refs):
    f_refs, refs = refs[: feat_count - 1], refs[feat_count - 1 :]
    core_ref, labels_ref, weight_ref, at_ref, w2s_ref, w2n_ref, mine_ref, other_ref = refs[:8]
    partner_refs = refs[8 : 7 + feat_count]
    send_ref, keep_ref, g_ref, hidden_ref, proj, pair = refs[7 + feat_count :]
    core = core_ref[0]
    classes = w2s_ref.shape[0]
    nodes = at_ref.shape[1]
    scale = 1.0 / fanout
    proj[core] = mine_ref[...]
    proj[1 - core] = tree_product(
        0, feat_count, {(0, 1): other_ref}, lambda s: dot_tn(partner_refs[swapped(s, feat_count) - 1][...], f_refs[s - 1][...])
    )
    at = at_ref[...]
    pre = proj[0] + dot_nn(proj[1].astype(BF16), at) * scale
    hidden = jnp.maximum(pre, 0.0).astype(BF16)
    hidden_ref[...] = hidden
    second = (dot_nn(hidden, at) * scale).astype(BF16)
    logits = dot_nn(w2s_ref[...], hidden) + dot_nn(w2n_ref[...], second)
    shifted = logits - jnp.max(logits, axis=0, keepdims=True)
    powers = jnp.exp(shifted)
    total = jnp.sum(powers, axis=0, keepdims=True)
    hot = lax.broadcasted_iota(jnp.int32, (classes, nodes), 0) == labels_ref[...]
    picked = jnp.sum(jnp.where(hot, shifted, 0.0), axis=0, keepdims=True) - jnp.log(total)
    chance = jnp.exp(picked)
    rest = 1.0 - chance
    weight = weight_ref[...]
    terms = -rest * rest * picked
    slope = weight * (2.0 * rest * chance * picked - rest * rest)
    grad = (jnp.where(hot, slope, 0.0) - (slope / total) * powers).astype(BF16)
    g_ref[...] = grad
    pair[0] = hidden
    pair[1] = second
    loss_part = jnp.sum(weight * terms)
    norm_part = jnp.sum(weight)
    for out_ref, which in ((send_ref, 1 - core), (keep_ref, core)):
        rows, cols = out_ref.shape
        row = lax.broadcasted_iota(jnp.int32, (rows, cols), 0)
        col = lax.broadcasted_iota(jnp.int32, (rows, cols), 1)
        extra = jnp.where(col == 0, loss_part, jnp.where(col == 1, norm_part, 0.0))
        out_ref[...] = jnp.where(row >= classes, extra, 0.0)
        out_ref[:classes, :] = dot_nt(grad, pair[which])


def backward_kernel(
    fanout, groups, core_ref, g_ref, hidden_ref, at_ref, w2s_ref, w2n_ref, f_ref, send_ref, keep_ref
):
    core = core_ref[0]
    scale = 1.0 / fanout
    grad = g_ref[...]
    at = at_ref[...]
    summed = dot_nt(grad, at)
    high = summed.astype(BF16)
    low = (summed - high.astype(F32)).astype(BF16)
    w2n = w2n_ref[...]
    hidden_grad = dot_tn(w2s_ref[...], grad) + (dot_tn(w2n, high) + dot_tn(w2n, low)) * scale
    pre_grad = jnp.where(hidden_ref[...] > 0, hidden_grad, 0.0).astype(BF16)
    proj_grad = (dot_nt(pre_grad, at) * scale).astype(BF16)
    features = f_ref[...]
    full = (dot_nt(features, pre_grad), dot_nt(features, proj_grad))
    rows = send_ref.shape[1] // 2
    first = core == 0
    for z in range(groups):
        for part in range(2):
            low_rows = full[part][2 * z * rows : (2 * z + 1) * rows]
            high_rows = full[part][(2 * z + 1) * rows : (2 * z + 2) * rows]
            send_ref[z, part * rows : (part + 1) * rows] = jnp.where(first, high_rows, low_rows)
            keep_ref[z, part * rows : (part + 1) * rows] = jnp.where(first, low_rows, high_rows)


def pair_kernel(classes, keep_ref, recv_ref, out_ref):
    total = keep_ref[...] + recv_ref[...]
    high = total.astype(BF16).astype(F32)
    rest = total - high
    middle = rest.astype(BF16).astype(F32)
    low = rest - middle
    row = lax.broadcasted_iota(jnp.int32, total.shape, 0)
    out_ref[...] = jnp.where(row == classes + 1, middle, jnp.where(row == classes + 2, low, high)).astype(BF16)


def chunk_kernel(groups, z_ref, keep_ref, recv_ref, own_ref, *out_refs):
    z = z_ref[0]
    own_ref[...] = keep_ref[z] + recv_ref[z]
    for s in range(1, groups):
        other = jnp.bitwise_xor(z, s)
        out_refs[s - 1][...] = (keep_ref[other] + recv_ref[other]).astype(BF16)


def second_sum_kernel(*refs):
    out_ref = refs[-1]
    out_ref[...] = tree_sum([r[...].astype(F32) for r in refs[:-1]])


def scalars(total, classes):
    row = lax.broadcasted_iota(jnp.int32, total.shape, 0)
    col = lax.broadcasted_iota(jnp.int32, total.shape, 1)
    inside = jnp.logical_and(row >= classes, row < classes + 3)
    loss = jnp.sum(jnp.where(jnp.logical_and(inside, col == 0), total, 0.0), keepdims=True)
    norm = jnp.sum(jnp.where(jnp.logical_and(inside, col == 1), total, 0.0), keepdims=True)
    return loss, norm


def first_sum_kernel(own_ref, *refs):
    refs[-1][...] = tree_sum([own_ref[...]] + [r[...].astype(F32) for r in refs[:-1]])


def out_kernel(classes, core_ref, own_ref, other_ref, first_ref, grad1_ref, grad2_ref, loss_ref):
    first = core_ref[0] == 0
    loss, norm = scalars(own_ref[...], classes)
    inverse = 1.0 / norm
    own = own_ref[:classes, :] * inverse
    other = other_ref[:classes, :] * inverse
    for slot, half in enumerate((jnp.where(first, own, other), jnp.where(first, other, own))):
        lanes = half.shape[1] // 128
        for j in range(lanes):
            grad2_ref[pl.ds(2 * j + slot, classes, stride=2 * lanes), :] = half[:, 128 * j : 128 * (j + 1)]
    loss_ref[...] = loss * inverse
    rows = grad1_ref.shape[1]
    grad1_ref[0] = first_ref[:rows] * inverse
    grad1_ref[1] = first_ref[rows:] * inverse


def exchange(value, axis, step):
    size = lax.axis_size(axis)
    return lax.ppermute(value, axis, [(i, i ^ step) for i in range(size)])


def swapped(step, count):
    bits = count.bit_length() - 1
    if bits % 2:
        return step
    half = bits // 2
    return (step & ((1 << half) - 1)) << half | step >> half


def hop(value, step):
    count, wide = lax.axis_size("feat"), lax.axis_size("dp")
    pairs = []
    for f in range(count):
        for d in range(wide):
            other = f ^ (step if d % 2 == 0 else swapped(step, count))
            pairs.append((f * wide + d, other * wide + d))
    return lax.ppermute(value, ("feat", "dp"), pairs)


def gather_parts(block, count):
    half = block.shape[0] // 2
    parts = [[block]]
    for s in range(1, count):
        low_bit = s & -s
        rest = s ^ low_bit
        if rest == 0:
            parts.append([hop(block, s)])
        else:
            low = parts[rest][0][:half] if len(parts[rest]) == 1 else parts[rest][0]
            high = parts[low_bit][0][half:]
            parts.append([hop(low, low_bit), hop(high, rest)])
    return parts


def on_device(features, neighbors, labels, loss_weight, w1_self, w1_neigh, w2_self, w2_neigh):
    feat_count = lax.axis_size("feat")
    dp_count = lax.axis_size("dp")
    groups = dp_count // 2
    nodes, fanout = neighbors.shape
    rows, hid = w1_self.shape
    classes = w2_self.shape[1]
    place = lax.axis_index("dp").astype(jnp.int32)
    core = (place % 2).reshape(1)
    z = (place // 2).reshape(1)

    wide = gather_parts(features, feat_count)
    early = [s for s in range(feat_count) if len(wide[s]) == 1]
    late = [s for s in range(feat_count) if len(wide[s]) > 1]
    nodes_mine = early_nodes(early, 0, feat_count)
    mine_own = jnp.where(core[0] == 0, w1_self, w1_neigh)
    mine = [hop(mine_own, s) for s in range(1, feat_count)]
    limit = 12 + 6 * nodes * nodes // (1024 * 1024)
    passing = [labels.reshape(1, nodes), loss_weight.reshape(1, nodes), w2_self.T, w2_neigh.T]
    at, labels, loss_weight, w2s, w2n = call(
        functools.partial(count_kernel, fanout),
        [shape((nodes, nodes), BF16)] + [shape(p.shape, p.dtype) for p in passing],
        [neighbors.T] + passing,
        flops=nodes * nodes * fanout,
    )
    *known, other_proj = call(
        functools.partial(early_kernel, nodes_mine, early),
        [shape((hid, nodes), F32)] * (len(nodes_mine) + 1),
        [core, w1_self, w1_neigh] + [wide[s][0] for s in early] + [mine[s - 1] for s in early[1:]],
        flops=2 * nodes * hid * rows * (len(early) + 1),
        smem=(0,),
        limit=limit,
    )
    mine_proj, *joined = call(
        functools.partial(mine_kernel, nodes_mine, late, feat_count),
        [shape((hid, nodes), F32)] + [shape((rows, nodes), BF16)] * len(late),
        known + [mine[s - 1] for s in late] + [part for s in late for part in wide[s]],
        flops=30 * nodes * hid * rows * feat_count,
        limit=limit,
    )
    rest = iter(joined)
    whole = [block[0] if len(block) == 1 else next(rest) for block in wide]
    partner = [exchange(block, "dp", 1) for block in mine]
    padded = (classes + 3 + 15) // 16 * 16
    send2, keep2, grad, hidden = call(
        functools.partial(forward_kernel, feat_count, fanout),
        [
            shape((padded, hid), F32),
            shape((padded, hid), F32),
            shape((classes, nodes), BF16),
            shape((hid, nodes), BF16),
        ],
        whole[1:] + [core, labels, loss_weight, at, w2s, w2n, mine_proj, other_proj] + partner,
        scratch=[
            pltpu.VMEM((2, hid, nodes), F32),
            pltpu.VMEM((2, hid, nodes), BF16),
        ],
        flops=2 * nodes * hid * 2 * (rows * feat_count + nodes),
        smem=(feat_count - 1,),
        limit=limit,
    )
    recv2 = exchange(send2, "dp", 1)
    chunk = 2 * (rows // dp_count)
    send1, keep1 = call(
        functools.partial(backward_kernel, fanout, groups),
        [shape((groups, chunk, hid), F32)] * 2,
        [core, grad, hidden, at, w2s, w2n, features],
        flops=2 * nodes * hid * 2 * (rows + nodes),
        smem=(0,),
        limit=limit,
    )
    recv1 = exchange(send1, "dp", 1)
    (own2,) = call(functools.partial(pair_kernel, classes), [shape((padded, hid), BF16)], [keep2, recv2])
    far2 = [exchange(own2, "dp", 2 * s) for s in range(1, groups)]
    own1, *chunks = call(
        functools.partial(chunk_kernel, groups),
        [shape((chunk, hid), F32)] + [shape((chunk, hid), BF16)] * (groups - 1),
        [z, keep1, recv1],
        smem=(0,),
    )
    far1 = [exchange(chunks[s - 1], "dp", 2 * s) for s in range(1, groups)]
    (total2,) = call(second_sum_kernel, [shape((padded, hid), F32)], far2[::-1] + [own2])
    other2 = exchange(total2, "dp", 1)
    (sum1,) = call(first_sum_kernel, [shape((chunk, hid), F32)], [own1] + far1, flops=300 * rows * nodes * hid)
    grad_w1, grad_w2, loss = call(
        functools.partial(out_kernel, classes),
        [shape((2, rows // dp_count, hid), F32), shape((classes * 2 * (hid // 128), 128), F32), shape((1, 1), F32)],
        [core, total2, other2, sum1],
        smem=(0,),
        final=True,
    )
    grad_w2 = grad_w2.reshape(classes, hid // 128, 2, 128).transpose(2, 1, 3, 0).reshape(2, hid, classes)
    return loss[0, 0], grad_w1, grad_w2


def solution(mesh):
    in_specs = (
        P("feat", "dp"),
        P("dp", None),
        P("dp"),
        P("dp"),
        P("feat", None),
        P("feat", None),
        P(),
        P(),
    )
    out_specs = (P(), P(None, ("feat", "dp"), None), P())
    return jax.shard_map(
        on_device, mesh=mesh, in_specs=in_specs, out_specs=out_specs, check_vma=False
    )
```

```python
import functools

import jax
import jax.numpy as jnp
from jax import lax
from jax.experimental import pallas as pl
from jax.experimental.pallas import tpu as pltpu
from jax.sharding import PartitionSpec as P

BF16 = jnp.bfloat16
F32 = jnp.float32


def dot_nn(left, right):
    return lax.dot_general(left, right, (((1,), (0,)), ((), ())), preferred_element_type=F32)


def dot_nt(left, right):
    return lax.dot_general(left, right, (((1,), (1,)), ((), ())), preferred_element_type=F32)


def dot_tn(left, right):
    return lax.dot_general(left, right, (((0,), (0,)), ((), ())), preferred_element_type=F32)


def tree_sum(terms):
    terms = list(terms)
    while len(terms) > 1:
        terms = [terms[i] + terms[i + 1] for i in range(0, len(terms), 2)]
    return terms[0]


def call(kernel, outs, args, flops=0, scratch=(), smem=(), limit=16, final=False):
    size = sum(a.size * a.dtype.itemsize for a in args)
    size += sum(o.dtype.itemsize * o.size for o in outs)
    spaces = [pltpu.SMEM if i in smem else pltpu.VMEM for i in range(len(args))]
    placed = [a if i in smem else pltpu.with_memory_space_constraint(a, pltpu.VMEM) for i, a in enumerate(args)]
    return pl.pallas_call(
        kernel,
        out_shape=outs if final else [pltpu.VMEM(o.shape, o.dtype) for o in outs],
        in_specs=[pl.BlockSpec(memory_space=space) for space in spaces],
        out_specs=[pl.BlockSpec(memory_space=pltpu.VMEM)] * len(outs),
        scratch_shapes=list(scratch),
        cost_estimate=pl.CostEstimate(flops=flops, bytes_accessed=size, transcendentals=0),
        compiler_params=pltpu.CompilerParams(vmem_limit_bytes=limit * 1024 * 1024),
    )(*placed)


def shape(dims, dtype):
    return jax.ShapeDtypeStruct(dims, dtype)


def count_kernel(fanout, nbr_ref, *refs):
    passing = len(refs) // 2
    at_ref = refs[passing]
    for i in range(passing):
        refs[passing + 1 + i][...] = refs[i][...]
    nodes = at_ref.shape[1]
    step = 32

    def body(i, carry):
        row = lax.broadcasted_iota(jnp.int32, (step, nodes), 0) + i * step
        total = jnp.zeros((step, nodes), F32)
        for k in range(fanout):
            total = total + jnp.where(nbr_ref[k : k + 1, :] == row, 1.0, 0.0)
        at_ref[pl.ds(pl.multiple_of(i * step, step), step), :] = total.astype(BF16)
        return carry

    lax.fori_loop(0, nodes // step, body, 0)


def early_nodes(early, first, last):
    if all(s in early for s in range(first, last)):
        return [(first, last)]
    if last - first == 1:
        return []
    middle = (first + last) // 2
    return early_nodes(early, first, middle) + early_nodes(early, middle, last)


def tree_product(first, last, known, leaf):
    if (first, last) in known:
        return known[(first, last)][...]
    if last - first == 1:
        return leaf(first)
    middle = (first + last) // 2
    return tree_product(first, middle, known, leaf) + tree_product(middle, last, known, leaf)


def early_kernel(nodes_mine, early, core_ref, ws_ref, wn_ref, *refs):
    f_refs = dict(zip(early, refs))
    w_refs = dict(zip(early[1:], refs[len(early) :]))
    outs = refs[2 * len(early) - 1 :]
    first = core_ref[0] == 0
    own = jnp.where(first, ws_ref[...], wn_ref[...])
    other = jnp.where(first, wn_ref[...], ws_ref[...])
    for (begin, end), out_ref in zip(nodes_mine, outs):
        leaf = lambda s: dot_tn(own if s == 0 else w_refs[s][...], f_refs[s][...])
        out_ref[...] = tree_product(begin, end, {}, leaf)
    outs[-1][...] = dot_tn(other, f_refs[0][...])


def mine_kernel(nodes_mine, late, feat_count, *refs):
    known = dict(zip(nodes_mine, refs))
    refs = refs[len(nodes_mine) :]
    w_refs = dict(zip(late, refs))
    halves = refs[len(late) : 3 * len(late)]
    out_ref, joined = refs[3 * len(late)], refs[3 * len(late) + 1 :]
    for i, block in enumerate(joined):
        low, high = halves[2 * i : 2 * i + 2]
        block[: low.shape[0]] = low[...]
        block[low.shape[0] :] = high[...]
    f_refs = dict(zip(late, joined))
    out_ref[...] = tree_product(0, feat_count, known, lambda s: dot_tn(w_refs[s][...], f_refs[s][...]))


def forward_kernel(feat_count, fanout, *refs):
    f_refs, refs = refs[: feat_count - 1], refs[feat_count - 1 :]
    core_ref, labels_ref, weight_ref, at_ref, w2s_ref, w2n_ref, mine_ref, other_ref = refs[:8]
    partner_refs = refs[8 : 7 + feat_count]
    send_ref, keep_ref, g_ref, hidden_ref, proj, pair = refs[7 + feat_count :]
    core = core_ref[0]
    classes = w2s_ref.shape[0]
    nodes = at_ref.shape[1]
    scale = 1.0 / fanout
    proj[core] = mine_ref[...]
    proj[1 - core] = tree_product(
        0, feat_count, {(0, 1): other_ref}, lambda s: dot_tn(partner_refs[swapped(s, feat_count) - 1][...], f_refs[s - 1][...])
    )
    at = at_ref[...]
    pre = proj[0] + dot_nn(proj[1].astype(BF16), at) * scale
    hidden = jnp.maximum(pre, 0.0).astype(BF16)
    hidden_ref[...] = hidden
    second = (dot_nn(hidden, at) * scale).astype(BF16)
    logits = dot_nn(w2s_ref[...], hidden) + dot_nn(w2n_ref[...], second)
    shifted = logits - jnp.max(logits, axis=0, keepdims=True)
    powers = jnp.exp(shifted)
    total = jnp.sum(powers, axis=0, keepdims=True)
    hot = lax.broadcasted_iota(jnp.int32, (classes, nodes), 0) == labels_ref[...]
    picked = jnp.sum(jnp.where(hot, shifted, 0.0), axis=0, keepdims=True) - jnp.log(total)
    chance = jnp.exp(picked)
    rest = 1.0 - chance
    weight = weight_ref[...]
    terms = -rest * rest * picked
    slope = weight * (2.0 * rest * chance * picked - rest * rest)
    grad = (jnp.where(hot, slope, 0.0) - (slope / total) * powers).astype(BF16)
    g_ref[...] = grad
    pair[0] = hidden
    pair[1] = second
    loss_part = jnp.sum(weight * terms)
    norm_part = jnp.sum(weight)
    for out_ref, which in ((send_ref, 1 - core), (keep_ref, core)):
        rows, cols = out_ref.shape
        row = lax.broadcasted_iota(jnp.int32, (rows, cols), 0)
        col = lax.broadcasted_iota(jnp.int32, (rows, cols), 1)
        extra = jnp.where(col == 0, loss_part, jnp.where(col == 1, norm_part, 0.0))
        out_ref[...] = jnp.where(row >= classes, extra, 0.0)
        out_ref[:classes, :] = dot_nt(grad, pair[which])


def backward_kernel(
    fanout, groups, core_ref, g_ref, hidden_ref, at_ref, w2s_ref, w2n_ref, f_ref, send_ref, keep_ref
):
    core = core_ref[0]
    scale = 1.0 / fanout
    grad = g_ref[...]
    at = at_ref[...]
    summed = dot_nt(grad, at)
    high = summed.astype(BF16)
    low = (summed - high.astype(F32)).astype(BF16)
    w2n = w2n_ref[...]
    hidden_grad = dot_tn(w2s_ref[...], grad) + (dot_tn(w2n, high) + dot_tn(w2n, low)) * scale
    pre_grad = jnp.where(hidden_ref[...] > 0, hidden_grad, 0.0).astype(BF16)
    proj_grad = (dot_nt(pre_grad, at) * scale).astype(BF16)
    features = f_ref[...]
    full = (dot_nt(features, pre_grad), dot_nt(features, proj_grad))
    rows = send_ref.shape[1] // 2
    first = core == 0
    for z in range(groups):
        for part in range(2):
            low_rows = full[part][2 * z * rows : (2 * z + 1) * rows]
            high_rows = full[part][(2 * z + 1) * rows : (2 * z + 2) * rows]
            send_ref[z, part * rows : (part + 1) * rows] = jnp.where(first, high_rows, low_rows)
            keep_ref[z, part * rows : (part + 1) * rows] = jnp.where(first, low_rows, high_rows)


def split_rows(total, classes):
    high = total.astype(BF16).astype(F32)
    rest = total - high
    middle = rest.astype(BF16).astype(F32)
    low = rest - middle
    row = lax.broadcasted_iota(jnp.int32, total.shape, 0)
    return jnp.where(row == classes + 1, middle, jnp.where(row == classes + 2, low, high)).astype(BF16)


def pair_kernel(classes, keep_ref, recv_ref, out_ref):
    out_ref[...] = split_rows(keep_ref[...] + recv_ref[...], classes)


def fold_second_kernel(classes, order_ref, own_ref, recv_ref, out_ref):
    total = own_ref[...].astype(F32) + recv_ref[...].astype(F32)
    row = lax.broadcasted_iota(jnp.int32, total.shape, 0)
    inside = jnp.logical_and(row >= classes, row < classes + 3)
    whole = jnp.sum(jnp.where(inside, total, 0.0), axis=0, keepdims=True)
    out_ref[...] = split_rows(jnp.where(row >= classes, whole, total), classes)


def chunk_kernel(groups, z_ref, keep_ref, recv_ref, kept_ref, send_ref):
    z, chunk = z_ref[0], keep_ref.shape[1]
    for i in range(groups // 2):
        here, there = jnp.bitwise_xor(z, 2 * i), jnp.bitwise_xor(z, 2 * i + 1)
        kept_ref[i] = keep_ref[here] + recv_ref[here]
        send_ref[i * chunk : (i + 1) * chunk] = (keep_ref[there] + recv_ref[there]).astype(BF16)


def fold_first_kernel(own_ref, recv_ref, kept_ref, send_ref):
    chunk = own_ref.shape[1]
    for i in range(own_ref.shape[0] // 2):
        kept_ref[i] = own_ref[2 * i] + recv_ref[2 * i * chunk : (2 * i + 1) * chunk].astype(F32)
        other = own_ref[2 * i + 1] + recv_ref[(2 * i + 1) * chunk : (2 * i + 2) * chunk].astype(F32)
        send_ref[i * chunk : (i + 1) * chunk] = other.astype(BF16)


def second_sum_kernel(*refs):
    out_ref = refs[-1]
    out_ref[...] = tree_sum([r[...].astype(F32) for r in refs[:-1]])


def scalars(total, classes):
    row = lax.broadcasted_iota(jnp.int32, total.shape, 0)
    col = lax.broadcasted_iota(jnp.int32, total.shape, 1)
    inside = jnp.logical_and(row >= classes, row < classes + 3)
    loss = jnp.sum(jnp.where(jnp.logical_and(inside, col == 0), total, 0.0), keepdims=True)
    norm = jnp.sum(jnp.where(jnp.logical_and(inside, col == 1), total, 0.0), keepdims=True)
    return loss, norm


def first_sum_kernel(own_ref, *refs):
    refs[-1][...] = own_ref[0] + refs[0][...].astype(F32)


def out_kernel(classes, core_ref, own_ref, other_ref, first_ref, grad1_ref, grad2_ref, loss_ref):
    first = core_ref[0] == 0
    loss, norm = scalars(own_ref[...], classes)
    own = own_ref[:classes, :] / norm
    other = other_ref[:classes, :] / norm
    for slot, half in enumerate((jnp.where(first, own, other), jnp.where(first, other, own))):
        lanes = half.shape[1] // 128
        for j in range(lanes):
            grad2_ref[pl.ds(2 * j + slot, classes, stride=2 * lanes), :] = half[:, 128 * j : 128 * (j + 1)]
    loss_ref[...] = loss / norm
    rows = grad1_ref.shape[1]
    grad1_ref[0] = first_ref[:rows] / norm
    grad1_ref[1] = first_ref[rows:] / norm


def exchange(value, axis, step):
    size = lax.axis_size(axis)
    return lax.ppermute(value, axis, [(i, i ^ step) for i in range(size)])


def swapped(step, count):
    bits = count.bit_length() - 1
    if bits % 2:
        return step
    half = bits // 2
    return (step & ((1 << half) - 1)) << half | step >> half


def hop(value, step):
    count, wide = lax.axis_size("feat"), lax.axis_size("dp")
    pairs = []
    for f in range(count):
        for d in range(wide):
            other = f ^ (step if d % 2 == 0 else swapped(step, count))
            pairs.append((f * wide + d, other * wide + d))
    return lax.ppermute(value, ("feat", "dp"), pairs)


def gather_parts(block, count):
    half = block.shape[0] // 2
    parts = [[block]]
    for s in range(1, count):
        low_bit = s & -s
        rest = s ^ low_bit
        if rest == 0:
            parts.append([hop(block, s)])
        else:
            low = parts[rest][0][:half] if len(parts[rest]) == 1 else parts[rest][0]
            high = parts[low_bit][0][half:]
            parts.append([hop(low, low_bit), hop(high, rest)])
    return parts


def on_device(features, neighbors, labels, loss_weight, w1_self, w1_neigh, w2_self, w2_neigh):
    feat_count = lax.axis_size("feat")
    dp_count = lax.axis_size("dp")
    groups = dp_count // 2
    nodes, fanout = neighbors.shape
    rows, hid = w1_self.shape
    classes = w2_self.shape[1]
    place = lax.axis_index("dp").astype(jnp.int32)
    core = (place % 2).reshape(1)
    z = (place // 2).reshape(1)

    wide = gather_parts(features, feat_count)
    early = [s for s in range(feat_count) if len(wide[s]) == 1]
    late = [s for s in range(feat_count) if len(wide[s]) > 1]
    nodes_mine = early_nodes(early, 0, feat_count)
    mine_own = jnp.where(core[0] == 0, w1_self, w1_neigh)
    mine = [hop(mine_own, s) for s in range(1, feat_count)]
    limit = 12 + 6 * nodes * nodes // (1024 * 1024)
    passing = [labels.reshape(1, nodes), loss_weight.reshape(1, nodes), w2_self.T, w2_neigh.T]
    at, labels, loss_weight, w2s, w2n = call(
        functools.partial(count_kernel, fanout),
        [shape((nodes, nodes), BF16)] + [shape(p.shape, p.dtype) for p in passing],
        [neighbors.T] + passing,
        flops=nodes * nodes * fanout,
    )
    *known, other_proj = call(
        functools.partial(early_kernel, nodes_mine, early),
        [shape((hid, nodes), F32)] * (len(nodes_mine) + 1),
        [core, w1_self, w1_neigh] + [wide[s][0] for s in early] + [mine[s - 1] for s in early[1:]],
        flops=2 * nodes * hid * rows * (len(early) + 1),
        smem=(0,),
        limit=limit,
    )
    mine_proj, *joined = call(
        functools.partial(mine_kernel, nodes_mine, late, feat_count),
        [shape((hid, nodes), F32)] + [shape((rows, nodes), BF16)] * len(late),
        known + [mine[s - 1] for s in late] + [part for s in late for part in wide[s]],
        flops=30 * nodes * hid * rows * feat_count,
        limit=limit,
    )
    rest = iter(joined)
    whole = [block[0] if len(block) == 1 else next(rest) for block in wide]
    partner = [exchange(block, "dp", 1) for block in mine]
    padded = (classes + 3 + 15) // 16 * 16
    send2, keep2, grad, hidden = call(
        functools.partial(forward_kernel, feat_count, fanout),
        [
            shape((padded, hid), F32),
            shape((padded, hid), F32),
            shape((classes, nodes), BF16),
            shape((hid, nodes), BF16),
        ],
        whole[1:] + [core, labels, loss_weight, at, w2s, w2n, mine_proj, other_proj] + partner,
        scratch=[
            pltpu.VMEM((2, hid, nodes), F32),
            pltpu.VMEM((2, hid, nodes), BF16),
        ],
        flops=2 * nodes * hid * 2 * (rows * feat_count + nodes),
        smem=(feat_count - 1,),
        limit=limit,
    )
    recv2 = exchange(send2, "dp", 1)
    chunk = 2 * (rows // dp_count)
    send1, keep1 = call(
        functools.partial(backward_kernel, fanout, groups),
        [shape((groups, chunk, hid), F32)] * 2,
        [core, grad, hidden, at, w2s, w2n, features],
        flops=2 * nodes * hid * 2 * (rows + nodes),
        smem=(0,),
        limit=limit,
    )
    recv1 = exchange(send1, "dp", 1)
    (own2,) = call(functools.partial(pair_kernel, classes), [shape((padded, hid), BF16)], [keep2, recv2])
    left = groups // 2
    kept1, send1 = call(
        functools.partial(chunk_kernel, groups),
        [shape((left, chunk, hid), F32), shape((left * chunk, hid), BF16)],
        [z, keep1, recv1],
        smem=(0,),
    )
    step = 2
    while left > 1:
        far2, far1 = exchange(own2, "dp", step), exchange(send1, "dp", step)
        left, step = left // 2, 2 * step
        (own2,) = call(
            functools.partial(fold_second_kernel, classes), [shape((padded, hid), BF16)], [kept1, own2, far2]
        )
        kept1, send1 = call(
            fold_first_kernel,
            [shape((left, chunk, hid), F32), shape((left * chunk, hid), BF16)],
            [kept1, far1],
        )
    far2, far1 = exchange(own2, "dp", step), exchange(send1, "dp", step)
    (total2,) = call(second_sum_kernel, [shape((padded, hid), F32)], [own2, far2])
    other2 = exchange(total2, "dp", 1)
    (sum1,) = call(first_sum_kernel, [shape((chunk, hid), F32)], [kept1, far1], flops=300 * rows * nodes * hid)
    grad_w1, grad_w2, loss = call(
        functools.partial(out_kernel, classes),
        [shape((2, rows // dp_count, hid), F32), shape((classes * 2 * (hid // 128), 128), F32), shape((1, 1), F32)],
        [core, total2, other2, sum1],
        smem=(0,),
        final=True,
    )
    grad_w2 = grad_w2.reshape(classes, hid // 128, 2, 128).transpose(2, 1, 3, 0).reshape(2, hid, classes)
    return loss[0, 0], grad_w1, grad_w2


def solution(mesh):
    in_specs = (
        P("feat", "dp"),
        P("dp", None),
        P("dp"),
        P("dp"),
        P("feat", None),
        P("feat", None),
        P(),
        P(),
    )
    out_specs = (P(), P(None, ("feat", "dp"), None), P())
    return jax.shard_map(
        on_device, mesh=mesh, in_specs=in_specs, out_specs=out_specs, check_vma=False
    )
```

```python
import functools

import jax
import jax.numpy as jnp
from jax import lax
from jax.experimental import pallas as pl
from jax.experimental.pallas import tpu as pltpu
from jax.sharding import PartitionSpec as P

BF16 = jnp.bfloat16
F32 = jnp.float32


def dot_nn(left, right):
    return lax.dot_general(left, right, (((1,), (0,)), ((), ())), preferred_element_type=F32)


def dot_nt(left, right):
    return lax.dot_general(left, right, (((1,), (1,)), ((), ())), preferred_element_type=F32)


def dot_tn(left, right):
    return lax.dot_general(left, right, (((0,), (0,)), ((), ())), preferred_element_type=F32)


def tree_sum(terms):
    terms = list(terms)
    while len(terms) > 1:
        terms = [terms[i] + terms[i + 1] for i in range(0, len(terms), 2)]
    return terms[0]


def call(kernel, outs, args, flops=0, scratch=(), smem=(), limit=16, final=False):
    size = sum(a.size * a.dtype.itemsize for a in args)
    size += sum(o.dtype.itemsize * o.size for o in outs)
    spaces = [pltpu.SMEM if i in smem else pltpu.VMEM for i in range(len(args))]
    placed = [a if i in smem else pltpu.with_memory_space_constraint(a, pltpu.VMEM) for i, a in enumerate(args)]
    return pl.pallas_call(
        kernel,
        out_shape=outs if final else [pltpu.VMEM(o.shape, o.dtype) for o in outs],
        in_specs=[pl.BlockSpec(memory_space=space) for space in spaces],
        out_specs=[pl.BlockSpec(memory_space=pltpu.VMEM)] * len(outs),
        scratch_shapes=list(scratch),
        cost_estimate=pl.CostEstimate(flops=flops, bytes_accessed=size, transcendentals=0),
        compiler_params=pltpu.CompilerParams(vmem_limit_bytes=limit * 1024 * 1024),
    )(*placed)


def shape(dims, dtype):
    return jax.ShapeDtypeStruct(dims, dtype)


def count_kernel(fanout, nbr_ref, *refs):
    passing = len(refs) // 2
    at_ref = refs[passing]
    for i in range(passing):
        refs[passing + 1 + i][...] = refs[i][...]
    nodes = at_ref.shape[1]
    step = 32

    def body(i, carry):
        row = lax.broadcasted_iota(jnp.int32, (step, nodes), 0) + i * step
        total = jnp.zeros((step, nodes), F32)
        for k in range(fanout):
            total = total + jnp.where(nbr_ref[k : k + 1, :] == row, 1.0, 0.0)
        at_ref[pl.ds(pl.multiple_of(i * step, step), step), :] = total.astype(BF16)
        return carry

    lax.fori_loop(0, nodes // step, body, 0)


def early_nodes(early, first, last):
    if all(s in early for s in range(first, last)):
        return [(first, last)]
    if last - first == 1:
        return []
    middle = (first + last) // 2
    return early_nodes(early, first, middle) + early_nodes(early, middle, last)


def tree_product(first, last, known, leaf):
    if (first, last) in known:
        return known[(first, last)][...]
    if last - first == 1:
        return leaf(first)
    middle = (first + last) // 2
    return tree_product(first, middle, known, leaf) + tree_product(middle, last, known, leaf)


def early_kernel(nodes_mine, early, core_ref, ws_ref, wn_ref, *refs):
    f_refs = dict(zip(early, refs))
    w_refs = dict(zip(early[1:], refs[len(early) :]))
    outs = refs[2 * len(early) - 1 :]
    first = core_ref[0] == 0
    own = jnp.where(first, ws_ref[...], wn_ref[...])
    other = jnp.where(first, wn_ref[...], ws_ref[...])
    for (begin, end), out_ref in zip(nodes_mine, outs):
        leaf = lambda s: dot_tn(own if s == 0 else w_refs[s][...], f_refs[s][...])
        out_ref[...] = tree_product(begin, end, {}, leaf)
    outs[-1][...] = dot_tn(other, f_refs[0][...])


def mine_kernel(nodes_mine, late, feat_count, *refs):
    known = dict(zip(nodes_mine, refs))
    refs = refs[len(nodes_mine) :]
    w_refs = dict(zip(late, refs))
    halves = refs[len(late) : 3 * len(late)]
    out_ref, joined = refs[3 * len(late)], refs[3 * len(late) + 1 :]
    for i, block in enumerate(joined):
        low, high = halves[2 * i : 2 * i + 2]
        block[: low.shape[0]] = low[...]
        block[low.shape[0] :] = high[...]
    f_refs = dict(zip(late, joined))
    out_ref[...] = tree_product(0, feat_count, known, lambda s: dot_tn(w_refs[s][...], f_refs[s][...]))


def forward_kernel(feat_count, fanout, *refs):
    f_refs, refs = refs[: feat_count - 1], refs[feat_count - 1 :]
    core_ref, labels_ref, weight_ref, at_ref, w2s_ref, w2n_ref, mine_ref, other_ref = refs[:8]
    partner_refs = refs[8 : 7 + feat_count]
    send_ref, keep_ref, g_ref, hidden_ref, proj, pair = refs[7 + feat_count :]
    core = core_ref[0]
    classes = w2s_ref.shape[0]
    nodes = at_ref.shape[1]
    scale = 1.0 / fanout
    proj[core] = mine_ref[...]
    proj[1 - core] = tree_product(
        0, feat_count, {(0, 1): other_ref}, lambda s: dot_tn(partner_refs[swapped(s, feat_count) - 1][...], f_refs[s - 1][...])
    )
    at = at_ref[...]
    pre = proj[0] + dot_nn(proj[1].astype(BF16), at) * scale
    hidden = jnp.maximum(pre, 0.0).astype(BF16)
    hidden_ref[...] = hidden
    second = (dot_nn(hidden, at) * scale).astype(BF16)
    logits = dot_nn(w2s_ref[...], hidden) + dot_nn(w2n_ref[...], second)
    shifted = logits - jnp.max(logits, axis=0, keepdims=True)
    powers = jnp.exp(shifted)
    total = jnp.sum(powers, axis=0, keepdims=True)
    hot = lax.broadcasted_iota(jnp.int32, (classes, nodes), 0) == labels_ref[...]
    picked = jnp.sum(jnp.where(hot, shifted, 0.0), axis=0, keepdims=True) - jnp.log(total)
    chance = jnp.exp(picked)
    rest = 1.0 - chance
    weight = weight_ref[...]
    terms = -rest * rest * picked
    slope = weight * (2.0 * rest * chance * picked - rest * rest)
    grad = (jnp.where(hot, slope, 0.0) - (slope / total) * powers).astype(BF16)
    g_ref[...] = grad
    pair[0] = hidden
    pair[1] = second
    loss_part = jnp.sum(weight * terms)
    norm_part = jnp.sum(weight)
    for out_ref, which in ((send_ref, 1 - core), (keep_ref, core)):
        rows, cols = out_ref.shape
        row = lax.broadcasted_iota(jnp.int32, (rows, cols), 0)
        col = lax.broadcasted_iota(jnp.int32, (rows, cols), 1)
        extra = jnp.where(col == 0, loss_part, jnp.where(col == 1, norm_part, 0.0))
        out_ref[...] = jnp.where(row >= classes, extra, 0.0)
        out_ref[:classes, :] = dot_nt(grad, pair[which])


def backward_kernel(
    fanout, groups, core_ref, g_ref, hidden_ref, at_ref, w2s_ref, w2n_ref, f_ref, send_ref, keep_ref
):
    core = core_ref[0]
    scale = 1.0 / fanout
    grad = g_ref[...]
    at = at_ref[...]
    summed = dot_nt(grad, at)
    high = summed.astype(BF16)
    low = (summed - high.astype(F32)).astype(BF16)
    w2n = w2n_ref[...]
    hidden_grad = dot_tn(w2s_ref[...], grad) + (dot_tn(w2n, high) + dot_tn(w2n, low)) * scale
    pre_grad = jnp.where(hidden_ref[...] > 0, hidden_grad, 0.0).astype(BF16)
    proj_grad = (dot_nt(pre_grad, at) * scale).astype(BF16)
    features = f_ref[...]
    full = (dot_nt(features, pre_grad), dot_nt(features, proj_grad))
    rows = send_ref.shape[1] // 2
    first = core == 0
    for z in range(groups):
        for part in range(2):
            low_rows = full[part][2 * z * rows : (2 * z + 1) * rows]
            high_rows = full[part][(2 * z + 1) * rows : (2 * z + 2) * rows]
            send_ref[z, part * rows : (part + 1) * rows] = jnp.where(first, high_rows, low_rows)
            keep_ref[z, part * rows : (part + 1) * rows] = jnp.where(first, low_rows, high_rows)


def split_rows(total, classes):
    high = total.astype(BF16).astype(F32)
    rest = total - high
    middle = rest.astype(BF16).astype(F32)
    low = rest - middle
    row = lax.broadcasted_iota(jnp.int32, total.shape, 0)
    return jnp.where(row == classes + 1, middle, jnp.where(row == classes + 2, low, high)).astype(BF16)


def pair_kernel(classes, keep_ref, recv_ref, out_ref):
    out_ref[...] = split_rows(keep_ref[...] + recv_ref[...], classes)


def fold_second_kernel(classes, order_ref, own_ref, recv_ref, out_ref):
    total = own_ref[...].astype(F32) + recv_ref[...].astype(F32)
    row = lax.broadcasted_iota(jnp.int32, total.shape, 0)
    inside = jnp.logical_and(row >= classes, row < classes + 3)
    whole = jnp.sum(jnp.where(inside, total, 0.0), axis=0, keepdims=True)
    out_ref[...] = split_rows(jnp.where(row >= classes, whole, total), classes)


def chunk_kernel(groups, z_ref, core_ref, keep_ref, recv_ref, kept_ref, send_ref):
    z, core, chunk = z_ref[0], core_ref[0], keep_ref.shape[1]

    def total(step):
        group = jnp.bitwise_xor(z, step + core * (swapped(step, groups) - step))
        return keep_ref[group] + recv_ref[group]

    for i in range(groups // 2):
        kept_ref[i] = total(2 * i)
        send_ref[i * chunk : (i + 1) * chunk] = total(2 * i + 1).astype(BF16)


def fold_first_kernel(own_ref, recv_ref, kept_ref, send_ref):
    chunk = own_ref.shape[1]
    for i in range(own_ref.shape[0] // 2):
        kept_ref[i] = own_ref[2 * i] + recv_ref[2 * i * chunk : (2 * i + 1) * chunk].astype(F32)
        other = own_ref[2 * i + 1] + recv_ref[(2 * i + 1) * chunk : (2 * i + 2) * chunk].astype(F32)
        send_ref[i * chunk : (i + 1) * chunk] = other.astype(BF16)


def second_sum_kernel(*refs):
    out_ref = refs[-1]
    out_ref[...] = tree_sum([r[...].astype(F32) for r in refs[:-1]])


def scalars(total, classes):
    row = lax.broadcasted_iota(jnp.int32, total.shape, 0)
    col = lax.broadcasted_iota(jnp.int32, total.shape, 1)
    inside = jnp.logical_and(row >= classes, row < classes + 3)
    loss = jnp.sum(jnp.where(jnp.logical_and(inside, col == 0), total, 0.0), keepdims=True)
    norm = jnp.sum(jnp.where(jnp.logical_and(inside, col == 1), total, 0.0), keepdims=True)
    return loss, norm


def first_sum_kernel(own_ref, *refs):
    refs[-1][...] = own_ref[0] + refs[0][...].astype(F32)


def out_kernel(classes, core_ref, own_ref, other_ref, first_ref, grad1_ref, grad2_ref, loss_ref):
    first = core_ref[0] == 0
    halves = jnp.where(first, own_ref[...], other_ref[...]), jnp.where(first, other_ref[...], own_ref[...])
    loss, norm = scalars(halves[0], classes)
    for slot, half in enumerate(halves):
        half = half[:classes] / norm
        lanes = half.shape[1] // 128
        for j in range(lanes):
            grad2_ref[pl.ds(2 * j + slot, classes, stride=2 * lanes), :] = half[:, 128 * j : 128 * (j + 1)]
    loss_ref[...] = loss / norm
    rows = grad1_ref.shape[1]
    grad1_ref[0] = first_ref[:rows] / norm
    grad1_ref[1] = first_ref[rows:] / norm


def exchange(value, axis, step):
    size = lax.axis_size(axis)
    return lax.ppermute(value, axis, [(i, i ^ step) for i in range(size)])


def swapped(step, count):
    bits = count.bit_length() - 1
    if bits % 2:
        return step
    half = bits // 2
    return (step & ((1 << half) - 1)) << half | step >> half


def hop(value, step):
    count, wide = lax.axis_size("feat"), lax.axis_size("dp")
    pairs = []
    for f in range(count):
        for d in range(wide):
            other = f ^ (step if d % 2 == 0 else swapped(step, count))
            pairs.append((f * wide + d, other * wide + d))
    return lax.ppermute(value, ("feat", "dp"), pairs)


def fold_hop(value, step):
    count = lax.axis_size("dp")
    pairs = []
    for d in range(count):
        z = d // 2 ^ (step if d % 2 == 0 else swapped(step, count // 2))
        pairs.append((d, 2 * z + d % 2))
    return lax.ppermute(value, "dp", pairs)


def gather_parts(block, count):
    half = block.shape[0] // 2
    parts = [[block]]
    for s in range(1, count):
        low_bit = s & -s
        rest = s ^ low_bit
        if rest == 0:
            parts.append([hop(block, s)])
        else:
            low = parts[rest][0][:half] if len(parts[rest]) == 1 else parts[rest][0]
            high = parts[low_bit][0][half:]
            parts.append([hop(low, low_bit), hop(high, rest)])
    return parts


def on_device(features, neighbors, labels, loss_weight, w1_self, w1_neigh, w2_self, w2_neigh):
    feat_count = lax.axis_size("feat")
    dp_count = lax.axis_size("dp")
    groups = dp_count // 2
    nodes, fanout = neighbors.shape
    rows, hid = w1_self.shape
    classes = w2_self.shape[1]
    place = lax.axis_index("dp").astype(jnp.int32)
    core = (place % 2).reshape(1)
    z = (place // 2).reshape(1)

    wide = gather_parts(features, feat_count)
    early = [s for s in range(feat_count) if len(wide[s]) == 1]
    late = [s for s in range(feat_count) if len(wide[s]) > 1]
    nodes_mine = early_nodes(early, 0, feat_count)
    mine_own = jnp.where(core[0] == 0, w1_self, w1_neigh)
    mine = [hop(mine_own, s) for s in range(1, feat_count)]
    limit = 12 + 6 * nodes * nodes // (1024 * 1024)
    passing = [labels.reshape(1, nodes), loss_weight.reshape(1, nodes), w2_self.T, w2_neigh.T]
    at, labels, loss_weight, w2s, w2n = call(
        functools.partial(count_kernel, fanout),
        [shape((nodes, nodes), BF16)] + [shape(p.shape, p.dtype) for p in passing],
        [neighbors.T] + passing,
        flops=nodes * nodes * fanout,
    )
    *known, other_proj = call(
        functools.partial(early_kernel, nodes_mine, early),
        [shape((hid, nodes), F32)] * (len(nodes_mine) + 1),
        [core, w1_self, w1_neigh] + [wide[s][0] for s in early] + [mine[s - 1] for s in early[1:]],
        flops=2 * nodes * hid * rows * (len(early) + 1),
        smem=(0,),
        limit=limit,
    )
    mine_proj, *joined = call(
        functools.partial(mine_kernel, nodes_mine, late, feat_count),
        [shape((hid, nodes), F32)] + [shape((rows, nodes), BF16)] * len(late),
        known + [mine[s - 1] for s in late] + [part for s in late for part in wide[s]],
        flops=30 * nodes * hid * rows * feat_count,
        limit=limit,
    )
    rest = iter(joined)
    whole = [block[0] if len(block) == 1 else next(rest) for block in wide]
    partner = [exchange(block, "dp", 1) for block in mine]
    padded = (classes + 3 + 15) // 16 * 16
    send2, keep2, grad, hidden = call(
        functools.partial(forward_kernel, feat_count, fanout),
        [
            shape((padded, hid), F32),
            shape((padded, hid), F32),
            shape((classes, nodes), BF16),
            shape((hid, nodes), BF16),
        ],
        whole[1:] + [core, labels, loss_weight, at, w2s, w2n, mine_proj, other_proj] + partner,
        scratch=[
            pltpu.VMEM((2, hid, nodes), F32),
            pltpu.VMEM((2, hid, nodes), BF16),
        ],
        flops=2 * nodes * hid * 2 * (rows * feat_count + nodes),
        smem=(feat_count - 1,),
        limit=limit,
    )
    recv2 = exchange(send2, "dp", 1)
    chunk = 2 * (rows // dp_count)
    send1, keep1 = call(
        functools.partial(backward_kernel, fanout, groups),
        [shape((groups, chunk, hid), F32)] * 2,
        [core, grad, hidden, at, w2s, w2n, features],
        flops=2 * nodes * hid * 2 * (rows + nodes),
        smem=(0,),
        limit=limit,
    )
    recv1 = exchange(send1, "dp", 1)
    (own2,) = call(functools.partial(pair_kernel, classes), [shape((padded, hid), BF16)], [keep2, recv2])
    left = groups // 2
    kept1, send1 = call(
        functools.partial(chunk_kernel, groups),
        [shape((left, chunk, hid), F32), shape((left * chunk, hid), BF16)],
        [z, core, keep1, recv1],
        smem=(0, 1),
    )
    step = 1
    while left > 1:
        far2, far1 = fold_hop(own2, step), fold_hop(send1, step)
        left, step = left // 2, 2 * step
        (own2,) = call(
            functools.partial(fold_second_kernel, classes), [shape((padded, hid), BF16)], [kept1, own2, far2]
        )
        kept1, send1 = call(
            fold_first_kernel,
            [shape((left, chunk, hid), F32), shape((left * chunk, hid), BF16)],
            [kept1, far1],
        )
    far2, far1 = fold_hop(own2, step), fold_hop(send1, step)
    (total2,) = call(second_sum_kernel, [shape((padded, hid), F32)], [own2, far2])
    other2 = exchange(total2, "dp", 1)
    (sum1,) = call(first_sum_kernel, [shape((chunk, hid), F32)], [kept1, far1], flops=300 * rows * nodes * hid)
    grad_w1, grad_w2, loss = call(
        functools.partial(out_kernel, classes),
        [shape((2, rows // dp_count, hid), F32), shape((classes * 2 * (hid // 128), 128), F32), shape((1, 1), F32)],
        [core, total2, other2, sum1],
        smem=(0,),
        final=True,
    )
    grad_w2 = grad_w2.reshape(classes, hid // 128, 2, 128).transpose(2, 1, 3, 0).reshape(2, hid, classes)
    return loss[0, 0], grad_w1, grad_w2


def solution(mesh):
    in_specs = (
        P("feat", "dp"),
        P("dp", None),
        P("dp"),
        P("dp"),
        P("feat", None),
        P("feat", None),
        P(),
        P(),
    )
    out_specs = (P(), P(None, ("feat", "dp"), None), P())
    return jax.shard_map(
        on_device, mesh=mesh, in_specs=in_specs, out_specs=out_specs, check_vma=False
    )
```

```python
import functools

import jax
import jax.numpy as jnp
from jax import lax
from jax.experimental import pallas as pl
from jax.experimental.pallas import tpu as pltpu
from jax.sharding import PartitionSpec as P

BF16 = jnp.bfloat16
F32 = jnp.float32


def dot_nn(left, right):
    return lax.dot_general(left, right, (((1,), (0,)), ((), ())), preferred_element_type=F32)


def dot_nt(left, right):
    return lax.dot_general(left, right, (((1,), (1,)), ((), ())), preferred_element_type=F32)


def dot_tn(left, right):
    return lax.dot_general(left, right, (((0,), (0,)), ((), ())), preferred_element_type=F32)


def tree_sum(terms):
    terms = list(terms)
    while len(terms) > 1:
        terms = [terms[i] + terms[i + 1] for i in range(0, len(terms), 2)]
    return terms[0]


def call(kernel, outs, args, flops=0, scratch=(), smem=(), limit=16, final=False, place=True):
    size = sum(a.size * a.dtype.itemsize for a in args)
    size += sum(o.dtype.itemsize * o.size for o in outs)
    spaces = [pltpu.SMEM if i in smem else pltpu.VMEM for i in range(len(args))]
    space = pltpu.VMEM if place else pltpu.HBM
    placed = [a if i in smem else pltpu.with_memory_space_constraint(a, space) for i, a in enumerate(args)]
    return pl.pallas_call(
        kernel,
        out_shape=outs if final else [pltpu.VMEM(o.shape, o.dtype) for o in outs],
        in_specs=[pl.BlockSpec(memory_space=kind) for kind in spaces],
        out_specs=[pl.BlockSpec(memory_space=pltpu.VMEM)] * len(outs),
        scratch_shapes=list(scratch),
        cost_estimate=pl.CostEstimate(flops=flops, bytes_accessed=size, transcendentals=0),
        compiler_params=pltpu.CompilerParams(vmem_limit_bytes=limit * 1024 * 1024),
    )(*placed)


def shape(dims, dtype):
    return jax.ShapeDtypeStruct(dims, dtype)


def count_kernel(fanout, core_ref, nbr_ref, ws_ref, wn_ref, *refs):
    passing = (len(refs) - 3) // 2
    at_ref, mine_ref, other_ref = refs[passing : passing + 3]
    first = core_ref[0] == 0
    mine_ref[...] = jnp.where(first, ws_ref[...], wn_ref[...])
    other_ref[...] = jnp.where(first, wn_ref[...], ws_ref[...])
    for i in range(passing):
        refs[passing + 3 + i][...] = refs[i][...]
    nodes = at_ref.shape[1]
    step = 32

    def body(i, carry):
        row = lax.broadcasted_iota(jnp.int32, (step, nodes), 0) + i * step
        total = jnp.zeros((step, nodes), F32)
        for k in range(fanout):
            total = total + jnp.where(nbr_ref[k : k + 1, :] == row, 1.0, 0.0)
        at_ref[pl.ds(pl.multiple_of(i * step, step), step), :] = total.astype(BF16)
        return carry

    lax.fori_loop(0, nodes // step, body, 0)


def early_nodes(early, first, last):
    if all(s in early for s in range(first, last)):
        return [(first, last)]
    if last - first == 1:
        return []
    middle = (first + last) // 2
    return early_nodes(early, first, middle) + early_nodes(early, middle, last)


def tree_product(first, last, known, leaf):
    if (first, last) in known:
        return known[(first, last)][...]
    if last - first == 1:
        return leaf(first)
    middle = (first + last) // 2
    return tree_product(first, middle, known, leaf) + tree_product(middle, last, known, leaf)


def early_kernel(nodes_mine, early, own_ref, other_ref, *refs):
    f_refs = dict(zip(early, refs))
    w_refs = dict(zip(early[1:], refs[len(early) :]))
    outs = refs[2 * len(early) - 1 :]
    for (begin, end), out_ref in zip(nodes_mine, outs):
        leaf = lambda s: dot_tn(own_ref[...] if s == 0 else w_refs[s][...], f_refs[s][...])
        out_ref[...] = tree_product(begin, end, {}, leaf)
    outs[-1][...] = dot_tn(other_ref[...], f_refs[0][...])


def mine_kernel(nodes_mine, late, feat_count, *refs):
    known = dict(zip(nodes_mine, refs))
    refs = refs[len(nodes_mine) :]
    w_refs, f_refs = dict(zip(late, refs)), dict(zip(late, refs[len(late) :]))
    refs[-1][...] = tree_product(0, feat_count, known, lambda s: dot_tn(w_refs[s][...], f_refs[s][...]))


def forward_kernel(feat_count, fanout, *refs):
    f_refs, refs = refs[: feat_count - 1], refs[feat_count - 1 :]
    core_ref, labels_ref, weight_ref, at_ref, w2s_ref, w2n_ref, mine_ref, other_ref = refs[:8]
    partner_refs = refs[8 : 7 + feat_count]
    send_ref, keep_ref, g_ref, hidden_ref, proj, pair = refs[7 + feat_count :]
    core = core_ref[0]
    classes = w2s_ref.shape[0]
    nodes = at_ref.shape[1]
    scale = 1.0 / fanout
    proj[core] = mine_ref[...]
    proj[1 - core] = tree_product(
        0, feat_count, {(0, 1): other_ref}, lambda s: dot_tn(partner_refs[swapped(s, feat_count) - 1][...], f_refs[s - 1][...])
    )
    at = at_ref[...]
    pre = proj[0] + dot_nn(proj[1].astype(BF16), at) * scale
    hidden = jnp.maximum(pre, 0.0).astype(BF16)
    hidden_ref[...] = hidden
    second = (dot_nn(hidden, at) * scale).astype(BF16)
    logits = dot_nn(w2s_ref[...], hidden) + dot_nn(w2n_ref[...], second)
    shifted = logits - jnp.max(logits, axis=0, keepdims=True)
    powers = jnp.exp(shifted)
    total = jnp.sum(powers, axis=0, keepdims=True)
    hot = lax.broadcasted_iota(jnp.int32, (classes, nodes), 0) == labels_ref[...]
    picked = jnp.sum(jnp.where(hot, shifted, 0.0), axis=0, keepdims=True) - jnp.log(total)
    chance = jnp.exp(picked)
    rest = 1.0 - chance
    weight = weight_ref[...]
    terms = -rest * rest * picked
    slope = weight * (2.0 * rest * chance * picked - rest * rest)
    grad = (jnp.where(hot, slope, 0.0) - (slope / total) * powers).astype(BF16)
    g_ref[...] = grad
    pair[0] = hidden
    pair[1] = second
    loss_part = jnp.sum(weight * terms)
    norm_part = jnp.sum(weight)
    for out_ref, which in ((send_ref, 1 - core), (keep_ref, core)):
        rows, cols = out_ref.shape
        row = lax.broadcasted_iota(jnp.int32, (rows, cols), 0)
        col = lax.broadcasted_iota(jnp.int32, (rows, cols), 1)
        extra = jnp.where(col == 0, loss_part, jnp.where(col == 1, norm_part, 0.0))
        out_ref[...] = jnp.where(row >= classes, extra, 0.0)
        out_ref[:classes, :] = dot_nt(grad, pair[which])


def backward_kernel(
    fanout, groups, core_ref, g_ref, hidden_ref, at_ref, w2s_ref, w2n_ref, f_ref, send_ref, keep_ref
):
    core = core_ref[0]
    scale = 1.0 / fanout
    grad = g_ref[...]
    at = at_ref[...]
    summed = dot_nt(grad, at)
    high = summed.astype(BF16)
    low = (summed - high.astype(F32)).astype(BF16)
    w2n = w2n_ref[...]
    hidden_grad = dot_tn(w2s_ref[...], grad) + (dot_tn(w2n, high) + dot_tn(w2n, low)) * scale
    pre_grad = jnp.where(hidden_ref[...] > 0, hidden_grad, 0.0).astype(BF16)
    proj_grad = (dot_nt(pre_grad, at) * scale).astype(BF16)
    features = f_ref[...]
    full = (dot_nt(features, pre_grad), dot_nt(features, proj_grad))
    rows = send_ref.shape[1] // 2
    first = core == 0
    for z in range(groups):
        for part in range(2):
            low_rows = full[part][2 * z * rows : (2 * z + 1) * rows]
            high_rows = full[part][(2 * z + 1) * rows : (2 * z + 2) * rows]
            send_ref[z, part * rows : (part + 1) * rows] = jnp.where(first, high_rows, low_rows)
            keep_ref[z, part * rows : (part + 1) * rows] = jnp.where(first, low_rows, high_rows)


def split_rows(total, classes):
    high = total.astype(BF16).astype(F32)
    rest = total - high
    middle = rest.astype(BF16).astype(F32)
    low = rest - middle
    row = lax.broadcasted_iota(jnp.int32, total.shape, 0)
    return jnp.where(row == classes + 1, middle, jnp.where(row == classes + 2, low, high)).astype(BF16)


def pair_kernel(classes, keep_ref, recv_ref, out_ref):
    out_ref[...] = split_rows(keep_ref[...] + recv_ref[...], classes)


def fold_second_kernel(classes, order_ref, own_ref, recv_ref, out_ref):
    total = own_ref[...].astype(F32) + recv_ref[...].astype(F32)
    row = lax.broadcasted_iota(jnp.int32, total.shape, 0)
    inside = jnp.logical_and(row >= classes, row < classes + 3)
    whole = jnp.sum(jnp.where(inside, total, 0.0), axis=0, keepdims=True)
    out_ref[...] = split_rows(jnp.where(row >= classes, whole, total), classes)


def chunk_kernel(groups, z_ref, core_ref, keep_ref, recv_ref, kept_ref, send_ref):
    z, core, chunk = z_ref[0], core_ref[0], keep_ref.shape[1]

    def total(step):
        group = jnp.bitwise_xor(z, step + core * (swapped(step, groups) - step))
        return keep_ref[group] + recv_ref[group]

    for i in range(groups // 2):
        kept_ref[i] = total(2 * i)
        send_ref[i * chunk : (i + 1) * chunk] = total(2 * i + 1).astype(BF16)


def fold_first_kernel(own_ref, recv_ref, kept_ref, send_ref):
    chunk = own_ref.shape[1]
    for i in range(own_ref.shape[0] // 2):
        kept_ref[i] = own_ref[2 * i] + recv_ref[2 * i * chunk : (2 * i + 1) * chunk].astype(F32)
        other = own_ref[2 * i + 1] + recv_ref[(2 * i + 1) * chunk : (2 * i + 2) * chunk].astype(F32)
        send_ref[i * chunk : (i + 1) * chunk] = other.astype(BF16)


def second_sum_kernel(*refs):
    out_ref = refs[-1]
    out_ref[...] = tree_sum([r[...].astype(F32) for r in refs[:-1]])


def scalars(total, classes):
    row = lax.broadcasted_iota(jnp.int32, total.shape, 0)
    col = lax.broadcasted_iota(jnp.int32, total.shape, 1)
    inside = jnp.logical_and(row >= classes, row < classes + 3)
    loss = jnp.sum(jnp.where(jnp.logical_and(inside, col == 0), total, 0.0), keepdims=True)
    norm = jnp.sum(jnp.where(jnp.logical_and(inside, col == 1), total, 0.0), keepdims=True)
    return loss, norm


def first_sum_kernel(own_ref, *refs):
    refs[-1][...] = own_ref[0] + refs[0][...].astype(F32)


def out_kernel(classes, core_ref, own_ref, other_ref, first_ref, grad1_ref, grad2_ref, loss_ref):
    first = core_ref[0] == 0
    halves = jnp.where(first, own_ref[...], other_ref[...]), jnp.where(first, other_ref[...], own_ref[...])
    loss, norm = scalars(halves[0], classes)
    for slot, half in enumerate(halves):
        half = half[:classes] / norm
        lanes = half.shape[1] // 128
        for j in range(lanes):
            grad2_ref[pl.ds(2 * j + slot, classes, stride=2 * lanes), :] = half[:, 128 * j : 128 * (j + 1)]
    loss_ref[...] = loss / norm
    rows = grad1_ref.shape[1]
    grad1_ref[0] = first_ref[:rows] / norm
    grad1_ref[1] = first_ref[rows:] / norm


def exchange(value, axis, step):
    size = lax.axis_size(axis)
    return lax.ppermute(value, axis, [(i, i ^ step) for i in range(size)])


def swapped(step, count):
    bits = count.bit_length() - 1
    if bits % 2:
        return step
    half = bits // 2
    return (step & ((1 << half) - 1)) << half | step >> half


def hop(value, step):
    count, wide = lax.axis_size("feat"), lax.axis_size("dp")
    pairs = []
    for f in range(count):
        for d in range(wide):
            other = f ^ (step if d % 2 == 0 else swapped(step, count))
            pairs.append((f * wide + d, other * wide + d))
    return lax.ppermute(value, ("feat", "dp"), pairs)


def fold_hop(value, step):
    count = lax.axis_size("dp")
    pairs = []
    for d in range(count):
        z = d // 2 ^ (step if d % 2 == 0 else swapped(step, count // 2))
        pairs.append((d, 2 * z + d % 2))
    return lax.ppermute(value, "dp", pairs)


def gather_blocks(block, count):
    blocks = [block]
    for s in range(1, count):
        low_bit = s & -s
        blocks.append(hop(blocks[low_bit] if s != low_bit else block, s ^ low_bit if s != low_bit else s))
    return blocks


def on_device(features, neighbors, labels, loss_weight, w1_self, w1_neigh, w2_self, w2_neigh):
    feat_count = lax.axis_size("feat")
    dp_count = lax.axis_size("dp")
    groups = dp_count // 2
    nodes, fanout = neighbors.shape
    rows, hid = w1_self.shape
    classes = w2_self.shape[1]
    place = lax.axis_index("dp").astype(jnp.int32)
    core = (place % 2).reshape(1)
    z = (place // 2).reshape(1)

    wide = gather_blocks(features, feat_count)
    early = [s for s in range(feat_count) if s & (s - 1) == 0]
    late = [s for s in range(feat_count) if s & (s - 1)]
    nodes_mine = early_nodes(early, 0, feat_count)
    limit = 12 + 6 * nodes * nodes // (1024 * 1024)
    passing = [labels.reshape(1, nodes), loss_weight.reshape(1, nodes), w2_self.T, w2_neigh.T]
    at, mine_own, other_own, labels, loss_weight, w2s, w2n = call(
        functools.partial(count_kernel, fanout),
        [shape((nodes, nodes), BF16)]
        + [shape((rows, hid), BF16)] * 2
        + [shape(p.shape, p.dtype) for p in passing],
        [core, neighbors.T, w1_self, w1_neigh] + passing,
        flops=nodes * nodes * fanout,
        smem=(0,),
        place=False,
    )
    mine = gather_blocks(mine_own, feat_count)[1:]
    *known, other_proj = call(
        functools.partial(early_kernel, nodes_mine, early),
        [shape((hid, nodes), F32)] * (len(nodes_mine) + 1),
        [mine_own, other_own] + [wide[s] for s in early] + [mine[s - 1] for s in early[1:]],
        flops=2 * nodes * hid * rows * (len(early) + 1),
        limit=limit,
    )
    (mine_proj,) = call(
        functools.partial(mine_kernel, nodes_mine, late, feat_count),
        [shape((hid, nodes), F32)],
        known + [mine[s - 1] for s in late] + [wide[s] for s in late],
        flops=30 * nodes * hid * rows * feat_count,
        limit=limit,
    )
    partner = [exchange(block, "dp", 1) for block in mine]
    padded = (classes + 3 + 15) // 16 * 16
    send2, keep2, grad, hidden = call(
        functools.partial(forward_kernel, feat_count, fanout),
        [
            shape((padded, hid), F32),
            shape((padded, hid), F32),
            shape((classes, nodes), BF16),
            shape((hid, nodes), BF16),
        ],
        wide[1:] + [core, labels, loss_weight, at, w2s, w2n, mine_proj, other_proj] + partner,
        scratch=[
            pltpu.VMEM((2, hid, nodes), F32),
            pltpu.VMEM((2, hid, nodes), BF16),
        ],
        flops=2 * nodes * hid * 2 * (rows * feat_count + nodes),
        smem=(feat_count - 1,),
        limit=limit,
    )
    recv2 = exchange(send2, "dp", 1)
    chunk = 2 * (rows // dp_count)
    send1, keep1 = call(
        functools.partial(backward_kernel, fanout, groups),
        [shape((groups, chunk, hid), F32)] * 2,
        [core, grad, hidden, at, w2s, w2n, features],
        flops=2 * nodes * hid * 2 * (rows + nodes),
        smem=(0,),
        limit=limit,
    )
    recv1 = exchange(send1, "dp", 1)
    (own2,) = call(functools.partial(pair_kernel, classes), [shape((padded, hid), BF16)], [keep2, recv2])
    left = groups // 2
    kept1, send1 = call(
        functools.partial(chunk_kernel, groups),
        [shape((left, chunk, hid), F32), shape((left * chunk, hid), BF16)],
        [z, core, keep1, recv1],
        smem=(0, 1),
    )
    step = 1
    while left > 1:
        far2, far1 = fold_hop(own2, step), fold_hop(send1, step)
        left, step = left // 2, 2 * step
        (own2,) = call(
            functools.partial(fold_second_kernel, classes), [shape((padded, hid), BF16)], [kept1, own2, far2]
        )
        kept1, send1 = call(
            fold_first_kernel,
            [shape((left, chunk, hid), F32), shape((left * chunk, hid), BF16)],
            [kept1, far1],
        )
    far2, far1 = fold_hop(own2, step), fold_hop(send1, step)
    (total2,) = call(second_sum_kernel, [shape((padded, hid), F32)], [own2, far2])
    other2 = exchange(total2, "dp", 1)
    (sum1,) = call(first_sum_kernel, [shape((chunk, hid), F32)], [kept1, far1], flops=300 * rows * nodes * hid)
    grad_w1, grad_w2, loss = call(
        functools.partial(out_kernel, classes),
        [shape((2, rows // dp_count, hid), F32), shape((classes * 2 * (hid // 128), 128), F32), shape((1, 1), F32)],
        [core, total2, other2, sum1],
        smem=(0,),
        final=True,
    )
    grad_w2 = grad_w2.reshape(classes, hid // 128, 2, 128).transpose(2, 1, 3, 0).reshape(2, hid, classes)
    return loss[0, 0], grad_w1, grad_w2


def solution(mesh):
    in_specs = (
        P("feat", "dp"),
        P("dp", None),
        P("dp"),
        P("dp"),
        P("feat", None),
        P("feat", None),
        P(),
        P(),
    )
    out_specs = (P(), P(None, ("feat", "dp"), None), P())
    return jax.shard_map(
        on_device, mesh=mesh, in_specs=in_specs, out_specs=out_specs, check_vma=False
    )
```

```python
import functools

import jax
import jax.numpy as jnp
from jax import lax
from jax.experimental import pallas as pl
from jax.experimental.pallas import tpu as pltpu
from jax.sharding import PartitionSpec as P

BF16 = jnp.bfloat16
F32 = jnp.float32


def dot_nn(left, right):
    return lax.dot_general(left, right, (((1,), (0,)), ((), ())), preferred_element_type=F32)


def dot_nt(left, right):
    return lax.dot_general(left, right, (((1,), (1,)), ((), ())), preferred_element_type=F32)


def dot_tn(left, right):
    return lax.dot_general(left, right, (((0,), (0,)), ((), ())), preferred_element_type=F32)


def tree_sum(terms):
    terms = list(terms)
    while len(terms) > 1:
        terms = [terms[i] + terms[i + 1] for i in range(0, len(terms), 2)]
    return terms[0]


def call(kernel, outs, args, flops=0, scratch=(), smem=(), limit=16, final=False, place=True):
    size = sum(a.size * a.dtype.itemsize for a in args)
    size += sum(o.dtype.itemsize * o.size for o in outs)
    spaces = [pltpu.SMEM if i in smem else pltpu.VMEM for i in range(len(args))]
    space = pltpu.VMEM if place else pltpu.HBM
    placed = [a if i in smem else pltpu.with_memory_space_constraint(a, space) for i, a in enumerate(args)]
    return pl.pallas_call(
        kernel,
        out_shape=outs if final else [pltpu.VMEM(o.shape, o.dtype) for o in outs],
        in_specs=[pl.BlockSpec(memory_space=kind) for kind in spaces],
        out_specs=[pl.BlockSpec(memory_space=pltpu.VMEM)] * len(outs),
        scratch_shapes=list(scratch),
        cost_estimate=pl.CostEstimate(flops=flops, bytes_accessed=size, transcendentals=0),
        compiler_params=pltpu.CompilerParams(vmem_limit_bytes=limit * 1024 * 1024),
    )(*placed)


def shape(dims, dtype):
    return jax.ShapeDtypeStruct(dims, dtype)


def count_kernel(fanout, core_ref, nbr_ref, ws_ref, wn_ref, *refs):
    passing = (len(refs) - 3) // 2
    at_ref, mine_ref, other_ref = refs[passing : passing + 3]
    first = core_ref[0] == 0
    mine_ref[...] = jnp.where(first, ws_ref[...], wn_ref[...])
    other_ref[...] = jnp.where(first, wn_ref[...], ws_ref[...])
    for i in range(passing):
        refs[passing + 3 + i][...] = refs[i][...]
    nodes = at_ref.shape[1]
    step = 32

    def body(i, carry):
        row = lax.broadcasted_iota(jnp.int32, (step, nodes), 0) + i * step
        total = jnp.zeros((step, nodes), F32)
        for k in range(fanout):
            total = total + jnp.where(nbr_ref[k : k + 1, :] == row, 1.0, 0.0)
        at_ref[pl.ds(pl.multiple_of(i * step, step), step), :] = total.astype(BF16)
        return carry

    lax.fori_loop(0, nodes // step, body, 0)


def early_nodes(early, first, last):
    if all(s in early for s in range(first, last)):
        return [(first, last)]
    if last - first == 1:
        return []
    middle = (first + last) // 2
    return early_nodes(early, first, middle) + early_nodes(early, middle, last)


def tree_product(first, last, known, leaf):
    if (first, last) in known:
        return known[(first, last)][...]
    if last - first == 1:
        return leaf(first)
    middle = (first + last) // 2
    return tree_product(first, middle, known, leaf) + tree_product(middle, last, known, leaf)


def early_kernel(nodes_mine, early, own_ref, other_ref, *refs):
    f_refs = dict(zip(early, refs))
    w_refs = dict(zip(early[1:], refs[len(early) :]))
    outs = refs[2 * len(early) - 1 :]
    for (begin, end), out_ref in zip(nodes_mine, outs):
        leaf = lambda s: dot_tn(own_ref[...] if s == 0 else w_refs[s][...], f_refs[s][...])
        out_ref[...] = tree_product(begin, end, {}, leaf)
    outs[-1][...] = dot_tn(other_ref[...], f_refs[0][...])


def partner_kernel(tree_nodes, early, own_ref, *refs):
    f_refs = dict(zip(early[1:], refs))
    w_refs = dict(zip(early[1:], refs[len(early) - 1 :]))
    for (begin, end), out_ref in zip(tree_nodes, refs[2 * len(early) - 2 :]):
        leaf = lambda s: dot_tn(w_refs[s][...], f_refs[s][...])
        out_ref[...] = tree_product(begin, end, {(0, 1): own_ref}, leaf)


def mine_kernel(nodes_mine, late, feat_count, *refs):
    known = dict(zip(nodes_mine, refs))
    refs = refs[len(nodes_mine) :]
    w_refs, f_refs = dict(zip(late, refs)), dict(zip(late, refs[len(late) :]))
    refs[-1][...] = tree_product(0, feat_count, known, lambda s: dot_tn(w_refs[s][...], f_refs[s][...]))


def forward_kernel(tree_nodes, late, feat_count, fanout, *refs):
    core_ref, labels_ref, weight_ref, at_ref, w2s_ref, w2n_ref, mine_ref = refs[:7]
    known = dict(zip(tree_nodes, refs[7:]))
    refs = refs[7 + len(tree_nodes) :]
    f_refs, w_refs = dict(zip(late, refs)), dict(zip(late, refs[len(late) :]))
    send_ref, keep_ref, g_ref, hidden_ref, proj, pair = refs[2 * len(late) :]
    core = core_ref[0]
    classes = w2s_ref.shape[0]
    nodes = at_ref.shape[1]
    scale = 1.0 / fanout
    proj[core] = mine_ref[...]
    proj[1 - core] = tree_product(0, feat_count, known, lambda s: dot_tn(w_refs[s][...], f_refs[s][...]))
    at = at_ref[...]
    pre = proj[0] + dot_nn(proj[1].astype(BF16), at) * scale
    hidden = jnp.maximum(pre, 0.0).astype(BF16)
    hidden_ref[...] = hidden
    second = (dot_nn(hidden, at) * scale).astype(BF16)
    logits = dot_nn(w2s_ref[...], hidden) + dot_nn(w2n_ref[...], second)
    shifted = logits - jnp.max(logits, axis=0, keepdims=True)
    powers = jnp.exp(shifted)
    total = jnp.sum(powers, axis=0, keepdims=True)
    hot = lax.broadcasted_iota(jnp.int32, (classes, nodes), 0) == labels_ref[...]
    picked = jnp.sum(jnp.where(hot, shifted, 0.0), axis=0, keepdims=True) - jnp.log(total)
    chance = jnp.exp(picked)
    rest = 1.0 - chance
    weight = weight_ref[...]
    terms = -rest * rest * picked
    slope = weight * (2.0 * rest * chance * picked - rest * rest)
    grad = (jnp.where(hot, slope, 0.0) - (slope / total) * powers).astype(BF16)
    g_ref[...] = grad
    pair[0] = hidden
    pair[1] = second
    loss_part = jnp.sum(weight * terms)
    norm_part = jnp.sum(weight)
    for out_ref, which in ((send_ref, 1 - core), (keep_ref, core)):
        rows, cols = out_ref.shape
        row = lax.broadcasted_iota(jnp.int32, (rows, cols), 0)
        col = lax.broadcasted_iota(jnp.int32, (rows, cols), 1)
        extra = jnp.where(col == 0, loss_part, jnp.where(col == 1, norm_part, 0.0))
        out_ref[...] = jnp.where(row >= classes, extra, 0.0)
        out_ref[:classes, :] = dot_nt(grad, pair[which])


def backward_kernel(
    fanout, groups, core_ref, g_ref, hidden_ref, at_ref, w2s_ref, w2n_ref, f_ref, send_ref, keep_ref
):
    core = core_ref[0]
    scale = 1.0 / fanout
    grad = g_ref[...]
    at = at_ref[...]
    summed = dot_nt(grad, at)
    high = summed.astype(BF16)
    low = (summed - high.astype(F32)).astype(BF16)
    w2n = w2n_ref[...]
    hidden_grad = dot_tn(w2s_ref[...], grad) + (dot_tn(w2n, high) + dot_tn(w2n, low)) * scale
    pre_grad = jnp.where(hidden_ref[...] > 0, hidden_grad, 0.0).astype(BF16)
    proj_grad = (dot_nt(pre_grad, at) * scale).astype(BF16)
    features = f_ref[...]
    full = (dot_nt(features, pre_grad), dot_nt(features, proj_grad))
    rows = send_ref.shape[1] // 2
    first = core == 0
    for z in range(groups):
        for part in range(2):
            low_rows = full[part][2 * z * rows : (2 * z + 1) * rows]
            high_rows = full[part][(2 * z + 1) * rows : (2 * z + 2) * rows]
            send_ref[z, part * rows : (part + 1) * rows] = jnp.where(first, high_rows, low_rows)
            keep_ref[z, part * rows : (part + 1) * rows] = jnp.where(first, low_rows, high_rows)


def split_rows(total, classes):
    high = total.astype(BF16).astype(F32)
    rest = total - high
    middle = rest.astype(BF16).astype(F32)
    low = rest - middle
    row = lax.broadcasted_iota(jnp.int32, total.shape, 0)
    return jnp.where(row == classes + 1, middle, jnp.where(row == classes + 2, low, high)).astype(BF16)


def pair_kernel(classes, keep_ref, recv_ref, out_ref):
    out_ref[...] = split_rows(keep_ref[...] + recv_ref[...], classes)


def fold_second_kernel(classes, order_ref, own_ref, recv_ref, out_ref):
    total = own_ref[...].astype(F32) + recv_ref[...].astype(F32)
    row = lax.broadcasted_iota(jnp.int32, total.shape, 0)
    inside = jnp.logical_and(row >= classes, row < classes + 3)
    whole = jnp.sum(jnp.where(inside, total, 0.0), axis=0, keepdims=True)
    out_ref[...] = split_rows(jnp.where(row >= classes, whole, total), classes)


def chunk_kernel(groups, z_ref, core_ref, keep_ref, recv_ref, kept_ref, send_ref):
    z, core, chunk = z_ref[0], core_ref[0], keep_ref.shape[1]

    def total(step):
        group = jnp.bitwise_xor(z, step + core * (swapped(step, groups) - step))
        return keep_ref[group] + recv_ref[group]

    for i in range(groups // 2):
        kept_ref[i] = total(2 * i)
        send_ref[i * chunk : (i + 1) * chunk] = total(2 * i + 1).astype(BF16)


def fold_first_kernel(own_ref, recv_ref, kept_ref, send_ref):
    chunk = own_ref.shape[1]
    for i in range(own_ref.shape[0] // 2):
        kept_ref[i] = own_ref[2 * i] + recv_ref[2 * i * chunk : (2 * i + 1) * chunk].astype(F32)
        other = own_ref[2 * i + 1] + recv_ref[(2 * i + 1) * chunk : (2 * i + 2) * chunk].astype(F32)
        send_ref[i * chunk : (i + 1) * chunk] = other.astype(BF16)


def second_sum_kernel(*refs):
    out_ref = refs[-1]
    out_ref[...] = tree_sum([r[...].astype(F32) for r in refs[:-1]])


def scalars(total, classes):
    row = lax.broadcasted_iota(jnp.int32, total.shape, 0)
    col = lax.broadcasted_iota(jnp.int32, total.shape, 1)
    inside = jnp.logical_and(row >= classes, row < classes + 3)
    loss = jnp.sum(jnp.where(jnp.logical_and(inside, col == 0), total, 0.0), keepdims=True)
    norm = jnp.sum(jnp.where(jnp.logical_and(inside, col == 1), total, 0.0), keepdims=True)
    return loss, norm


def first_sum_kernel(own_ref, *refs):
    refs[-1][...] = own_ref[0] + refs[0][...].astype(F32)


def out_kernel(classes, core_ref, own_ref, other_ref, first_ref, grad1_ref, grad2_ref, loss_ref):
    first = core_ref[0] == 0
    halves = jnp.where(first, own_ref[...], other_ref[...]), jnp.where(first, other_ref[...], own_ref[...])
    loss, norm = scalars(halves[0], classes)
    for slot, half in enumerate(halves):
        half = half[:classes] / norm
        lanes = half.shape[1] // 128
        for j in range(lanes):
            grad2_ref[pl.ds(2 * j + slot, classes, stride=2 * lanes), :] = half[:, 128 * j : 128 * (j + 1)]
    loss_ref[...] = loss / norm
    rows = grad1_ref.shape[1]
    grad1_ref[0] = first_ref[:rows] / norm
    grad1_ref[1] = first_ref[rows:] / norm


def exchange(value, axis, step):
    size = lax.axis_size(axis)
    return lax.ppermute(value, axis, [(i, i ^ step) for i in range(size)])


def swapped(step, count):
    bits = count.bit_length() - 1
    if bits % 2:
        return step
    half = bits // 2
    return (step & ((1 << half) - 1)) << half | step >> half


def hop(value, step):
    count, wide = lax.axis_size("feat"), lax.axis_size("dp")
    pairs = []
    for f in range(count):
        for d in range(wide):
            other = f ^ (step if d % 2 == 0 else swapped(step, count))
            pairs.append((f * wide + d, other * wide + d))
    return lax.ppermute(value, ("feat", "dp"), pairs)


def fold_hop(value, step):
    count = lax.axis_size("dp")
    pairs = []
    for d in range(count):
        z = d // 2 ^ (step if d % 2 == 0 else swapped(step, count // 2))
        pairs.append((d, 2 * z + d % 2))
    return lax.ppermute(value, "dp", pairs)


def gather_blocks(block, count):
    blocks = [block]
    for s in range(1, count):
        low_bit = s & -s
        blocks.append(hop(blocks[low_bit] if s != low_bit else block, s ^ low_bit if s != low_bit else s))
    return blocks


def on_device(features, neighbors, labels, loss_weight, w1_self, w1_neigh, w2_self, w2_neigh):
    feat_count = lax.axis_size("feat")
    dp_count = lax.axis_size("dp")
    groups = dp_count // 2
    nodes, fanout = neighbors.shape
    rows, hid = w1_self.shape
    classes = w2_self.shape[1]
    place = lax.axis_index("dp").astype(jnp.int32)
    core = (place % 2).reshape(1)
    z = (place // 2).reshape(1)

    wide = gather_blocks(features, feat_count)
    early = [s for s in range(feat_count) if s & (s - 1) == 0]
    late = [s for s in range(feat_count) if s & (s - 1)]
    nodes_mine = early_nodes(early, 0, feat_count)
    limit = 12 + 6 * nodes * nodes // (1024 * 1024)
    passing = [labels.reshape(1, nodes), loss_weight.reshape(1, nodes), w2_self.T, w2_neigh.T]
    at, mine_own, other_own, labels, loss_weight, w2s, w2n = call(
        functools.partial(count_kernel, fanout),
        [shape((nodes, nodes), BF16)]
        + [shape((rows, hid), BF16)] * 2
        + [shape(p.shape, p.dtype) for p in passing],
        [core, neighbors.T, w1_self, w1_neigh] + passing,
        flops=nodes * nodes * fanout,
        smem=(0,),
        place=False,
    )
    mine = gather_blocks(mine_own, feat_count)[1:]
    *known, other_proj = call(
        functools.partial(early_kernel, nodes_mine, early),
        [shape((hid, nodes), F32)] * (len(nodes_mine) + 1),
        [mine_own, other_own] + [wide[s] for s in early] + [mine[s - 1] for s in early[1:]],
        flops=2 * nodes * hid * rows * (len(early) + 1),
        limit=limit,
    )
    (mine_proj,) = call(
        functools.partial(mine_kernel, nodes_mine, late, feat_count),
        [shape((hid, nodes), F32)],
        known + [mine[s - 1] for s in late] + [wide[s] for s in late],
        flops=30 * nodes * hid * rows * feat_count,
        limit=limit,
    )
    partner = [exchange(block, "dp", 1) for block in mine]
    partner = [partner[swapped(s, feat_count) - 1] for s in range(1, feat_count)]
    known_other = call(
        functools.partial(partner_kernel, nodes_mine, early),
        [shape((hid, nodes), F32)] * len(nodes_mine),
        [other_proj] + [wide[s] for s in early[1:]] + [partner[s - 1] for s in early[1:]],
        flops=2 * nodes * hid * rows * (len(early) - 1),
        limit=limit,
    )
    padded = (classes + 3 + 15) // 16 * 16
    send2, keep2, grad, hidden = call(
        functools.partial(forward_kernel, nodes_mine, late, feat_count, fanout),
        [
            shape((padded, hid), F32),
            shape((padded, hid), F32),
            shape((classes, nodes), BF16),
            shape((hid, nodes), BF16),
        ],
        [core, labels, loss_weight, at, w2s, w2n, mine_proj]
        + list(known_other)
        + [wide[s] for s in late]
        + [partner[s - 1] for s in late],
        scratch=[
            pltpu.VMEM((2, hid, nodes), F32),
            pltpu.VMEM((2, hid, nodes), BF16),
        ],
        flops=2 * nodes * hid * 2 * (rows * feat_count + nodes),
        smem=(0,),
        limit=limit,
    )
    recv2 = exchange(send2, "dp", 1)
    chunk = 2 * (rows // dp_count)
    send1, keep1 = call(
        functools.partial(backward_kernel, fanout, groups),
        [shape((groups, chunk, hid), F32)] * 2,
        [core, grad, hidden, at, w2s, w2n, features],
        flops=2 * nodes * hid * 2 * (rows + nodes),
        smem=(0,),
        limit=limit,
    )
    recv1 = exchange(send1, "dp", 1)
    (own2,) = call(functools.partial(pair_kernel, classes), [shape((padded, hid), BF16)], [keep2, recv2])
    left = groups // 2
    kept1, send1 = call(
        functools.partial(chunk_kernel, groups),
        [shape((left, chunk, hid), F32), shape((left * chunk, hid), BF16)],
        [z, core, keep1, recv1],
        smem=(0, 1),
    )
    step = 1
    while left > 1:
        far2, far1 = fold_hop(own2, step), fold_hop(send1, step)
        left, step = left // 2, 2 * step
        (own2,) = call(
            functools.partial(fold_second_kernel, classes), [shape((padded, hid), BF16)], [kept1, own2, far2]
        )
        kept1, send1 = call(
            fold_first_kernel,
            [shape((left, chunk, hid), F32), shape((left * chunk, hid), BF16)],
            [kept1, far1],
        )
    far2, far1 = fold_hop(own2, step), fold_hop(send1, step)
    (total2,) = call(second_sum_kernel, [shape((padded, hid), F32)], [own2, far2])
    other2 = exchange(total2, "dp", 1)
    (sum1,) = call(first_sum_kernel, [shape((chunk, hid), F32)], [kept1, far1], flops=300 * rows * nodes * hid)
    grad_w1, grad_w2, loss = call(
        functools.partial(out_kernel, classes),
        [shape((2, rows // dp_count, hid), F32), shape((classes * 2 * (hid // 128), 128), F32), shape((1, 1), F32)],
        [core, total2, other2, sum1],
        smem=(0,),
        final=True,
    )
    grad_w2 = grad_w2.reshape(classes, hid // 128, 2, 128).transpose(2, 1, 3, 0).reshape(2, hid, classes)
    return loss[0, 0], grad_w1, grad_w2


def solution(mesh):
    in_specs = (
        P("feat", "dp"),
        P("dp", None),
        P("dp"),
        P("dp"),
        P("feat", None),
        P("feat", None),
        P(),
        P(),
    )
    out_specs = (P(), P(None, ("feat", "dp"), None), P())
    return jax.shard_map(
        on_device, mesh=mesh, in_specs=in_specs, out_specs=out_specs, check_vma=False
    )
```

```python
import functools

import jax
import jax.numpy as jnp
from jax import lax
from jax.experimental import pallas as pl
from jax.experimental.pallas import tpu as pltpu
from jax.sharding import PartitionSpec as P

BF16 = jnp.bfloat16
F32 = jnp.float32


def dot_nn(left, right):
    return lax.dot_general(left, right, (((1,), (0,)), ((), ())), preferred_element_type=F32)


def dot_nt(left, right):
    return lax.dot_general(left, right, (((1,), (1,)), ((), ())), preferred_element_type=F32)


def dot_tn(left, right):
    return lax.dot_general(left, right, (((0,), (0,)), ((), ())), preferred_element_type=F32)


def tree_sum(terms):
    terms = list(terms)
    while len(terms) > 1:
        terms = [terms[i] + terms[i + 1] for i in range(0, len(terms), 2)]
    return terms[0]


def call(kernel, outs, args, flops=0, scratch=(), smem=(), limit=16, final=False, place=True):
    size = sum(a.size * a.dtype.itemsize for a in args)
    size += sum(o.dtype.itemsize * o.size for o in outs)
    spaces = [pltpu.SMEM if i in smem else pltpu.VMEM for i in range(len(args))]
    space = pltpu.VMEM if place else pltpu.HBM
    placed = [a if i in smem else pltpu.with_memory_space_constraint(a, space) for i, a in enumerate(args)]
    return pl.pallas_call(
        kernel,
        out_shape=outs if final else [pltpu.VMEM(o.shape, o.dtype) for o in outs],
        in_specs=[pl.BlockSpec(memory_space=kind) for kind in spaces],
        out_specs=[pl.BlockSpec(memory_space=pltpu.VMEM)] * len(outs),
        scratch_shapes=list(scratch),
        cost_estimate=pl.CostEstimate(flops=flops, bytes_accessed=size, transcendentals=0),
        compiler_params=pltpu.CompilerParams(vmem_limit_bytes=limit * 1024 * 1024),
    )(*placed)


def shape(dims, dtype):
    return jax.ShapeDtypeStruct(dims, dtype)


def count_kernel(fanout, core_ref, nbr_ref, ws_ref, wn_ref, *refs):
    passing = (len(refs) - 3) // 2
    at_ref, mine_ref, other_ref = refs[passing : passing + 3]
    first = core_ref[0] == 0
    mine_ref[...] = jnp.where(first, ws_ref[...], wn_ref[...])
    other_ref[...] = jnp.where(first, wn_ref[...], ws_ref[...])
    for i in range(passing):
        refs[passing + 3 + i][...] = refs[i][...]
    nodes = at_ref.shape[1]
    step = 32

    def body(i, carry):
        row = lax.broadcasted_iota(jnp.int32, (step, nodes), 0) + i * step
        total = jnp.zeros((step, nodes), F32)
        for k in range(fanout):
            total = total + jnp.where(nbr_ref[k : k + 1, :] == row, 1.0, 0.0)
        at_ref[pl.ds(pl.multiple_of(i * step, step), step), :] = total.astype(BF16)
        return carry

    lax.fori_loop(0, nodes // step, body, 0)


def early_nodes(early, first, last):
    if all(s in early for s in range(first, last)):
        return [(first, last)]
    if last - first == 1:
        return []
    middle = (first + last) // 2
    return early_nodes(early, first, middle) + early_nodes(early, middle, last)


def tree_product(first, last, known, leaf):
    if (first, last) in known:
        return known[(first, last)][...]
    if last - first == 1:
        return leaf(first)
    middle = (first + last) // 2
    return tree_product(first, middle, known, leaf) + tree_product(middle, last, known, leaf)


def early_kernel(nodes_mine, early, own_ref, other_ref, *refs):
    f_refs = dict(zip(early, refs))
    w_refs = dict(zip(early[1:], refs[len(early) :]))
    outs = refs[2 * len(early) - 1 :]
    for (begin, end), out_ref in zip(nodes_mine, outs):
        leaf = lambda s: dot_tn(own_ref[...] if s == 0 else w_refs[s][...], f_refs[s][...])
        out_ref[...] = tree_product(begin, end, {}, leaf)
    outs[-1][...] = dot_tn(other_ref[...], f_refs[0][...])


def mine_kernel(nodes_mine, late, feat_count, *refs):
    known = dict(zip(nodes_mine, refs))
    refs = refs[len(nodes_mine) :]
    w_refs, f_refs = dict(zip(late, refs)), dict(zip(late, refs[len(late) :]))
    refs[-1][...] = tree_product(0, feat_count, known, lambda s: dot_tn(w_refs[s][...], f_refs[s][...]))


def forward_kernel(feat_count, fanout, *refs):
    f_refs, refs = refs[: feat_count - 1], refs[feat_count - 1 :]
    core_ref, labels_ref, weight_ref, at_ref, w2s_ref, w2n_ref, mine_ref, other_ref = refs[:8]
    partner_refs = refs[8 : 7 + feat_count]
    send_ref, keep_ref, g_ref, hidden_ref, pair = refs[7 + feat_count :]
    core = core_ref[0]
    classes = w2s_ref.shape[0]
    nodes = at_ref.shape[1]
    scale = 1.0 / fanout
    first, mine = core == 0, mine_ref[...]
    other = tree_product(
        0, feat_count, {(0, 1): other_ref}, lambda s: dot_tn(partner_refs[swapped(s, feat_count) - 1][...], f_refs[s - 1][...])
    )
    at = at_ref[...]
    pre = jnp.where(first, mine, other) + dot_nn(jnp.where(first, other, mine).astype(BF16), at) * scale
    hidden = jnp.maximum(pre, 0.0).astype(BF16)
    hidden_ref[...] = hidden
    second = (dot_nn(hidden, at) * scale).astype(BF16)
    logits = dot_nn(w2s_ref[...], hidden) + dot_nn(w2n_ref[...], second)
    shifted = logits - jnp.max(logits, axis=0, keepdims=True)
    powers = jnp.exp(shifted)
    total = jnp.sum(powers, axis=0, keepdims=True)
    hot = lax.broadcasted_iota(jnp.int32, (classes, nodes), 0) == labels_ref[...]
    picked = jnp.sum(jnp.where(hot, shifted, 0.0), axis=0, keepdims=True) - jnp.log(total)
    chance = jnp.exp(picked)
    rest = 1.0 - chance
    weight = weight_ref[...]
    terms = -rest * rest * picked
    slope = weight * (2.0 * rest * chance * picked - rest * rest)
    grad = (jnp.where(hot, slope, 0.0) - (slope / total) * powers).astype(BF16)
    g_ref[...] = grad
    pair[0] = hidden
    pair[1] = second
    loss_part = jnp.sum(weight * terms)
    norm_part = jnp.sum(weight)
    for out_ref, which in ((send_ref, 1 - core), (keep_ref, core)):
        rows, cols = out_ref.shape
        col = lax.broadcasted_iota(jnp.int32, (rows - classes, cols), 1)
        out_ref[classes:, :] = jnp.where(col == 0, loss_part, jnp.where(col == 1, norm_part, 0.0))
        out_ref[:classes, :] = dot_nt(grad, pair[which])


def backward_kernel(
    fanout, groups, core_ref, g_ref, hidden_ref, at_ref, w2s_ref, w2n_ref, f_ref, send_ref, keep_ref
):
    core = core_ref[0]
    scale = 1.0 / fanout
    grad = g_ref[...]
    at = at_ref[...]
    summed = dot_nt(grad, at)
    high = summed.astype(BF16)
    low = (summed - high.astype(F32)).astype(BF16)
    w2n = w2n_ref[...]
    hidden_grad = dot_tn(w2s_ref[...], grad) + (dot_tn(w2n, high) + dot_tn(w2n, low)) * scale
    pre_grad = jnp.where(hidden_ref[...] > 0, hidden_grad, 0.0).astype(BF16)
    proj_grad = (dot_nt(pre_grad, at) * scale).astype(BF16)
    features = f_ref[...]
    full = (dot_nt(features, pre_grad), dot_nt(features, proj_grad))
    rows = send_ref.shape[1] // 2
    first = core == 0
    for z in range(groups):
        for part in range(2):
            low_rows = full[part][2 * z * rows : (2 * z + 1) * rows]
            high_rows = full[part][(2 * z + 1) * rows : (2 * z + 2) * rows]
            send_ref[z, part * rows : (part + 1) * rows] = jnp.where(first, high_rows, low_rows)
            keep_ref[z, part * rows : (part + 1) * rows] = jnp.where(first, low_rows, high_rows)


def split_rows(total, classes):
    high = total.astype(BF16).astype(F32)
    rest = total - high
    middle = rest.astype(BF16).astype(F32)
    low = rest - middle
    row = lax.broadcasted_iota(jnp.int32, total.shape, 0)
    return jnp.where(row == classes + 1, middle, jnp.where(row == classes + 2, low, high)).astype(BF16)


def pair_kernel(classes, keep_ref, recv_ref, out_ref):
    out_ref[...] = split_rows(keep_ref[...] + recv_ref[...], classes)


def fold_second_kernel(classes, order_ref, own_ref, recv_ref, out_ref):
    total = own_ref[...].astype(F32) + recv_ref[...].astype(F32)
    row = lax.broadcasted_iota(jnp.int32, total.shape, 0)
    inside = jnp.logical_and(row >= classes, row < classes + 3)
    whole = jnp.sum(jnp.where(inside, total, 0.0), axis=0, keepdims=True)
    out_ref[...] = split_rows(jnp.where(row >= classes, whole, total), classes)


def chunk_kernel(groups, z_ref, core_ref, keep_ref, recv_ref, kept_ref, send_ref):
    z, core, chunk = z_ref[0], core_ref[0], keep_ref.shape[1]

    def total(step):
        group = jnp.bitwise_xor(z, step + core * (swapped(step, groups) - step))
        return keep_ref[group] + recv_ref[group]

    for i in range(groups // 2):
        kept_ref[i] = total(2 * i)
        send_ref[i * chunk : (i + 1) * chunk] = total(2 * i + 1).astype(BF16)


def fold_first_kernel(own_ref, recv_ref, kept_ref, send_ref):
    chunk = own_ref.shape[1]
    for i in range(own_ref.shape[0] // 2):
        kept_ref[i] = own_ref[2 * i] + recv_ref[2 * i * chunk : (2 * i + 1) * chunk].astype(F32)
        other = own_ref[2 * i + 1] + recv_ref[(2 * i + 1) * chunk : (2 * i + 2) * chunk].astype(F32)
        send_ref[i * chunk : (i + 1) * chunk] = other.astype(BF16)


def second_sum_kernel(*refs):
    out_ref = refs[-1]
    out_ref[...] = tree_sum([r[...].astype(F32) for r in refs[:-1]])


def scalars(total, classes):
    row = lax.broadcasted_iota(jnp.int32, total.shape, 0)
    col = lax.broadcasted_iota(jnp.int32, total.shape, 1)
    inside = jnp.logical_and(row >= classes, row < classes + 3)
    loss = jnp.sum(jnp.where(jnp.logical_and(inside, col == 0), total, 0.0), keepdims=True)
    norm = jnp.sum(jnp.where(jnp.logical_and(inside, col == 1), total, 0.0), keepdims=True)
    return loss, norm


def first_sum_kernel(own_ref, *refs):
    refs[-1][...] = own_ref[0] + refs[0][...].astype(F32)


def out_kernel(classes, core_ref, own_ref, other_ref, first_ref, grad1_ref, grad2_ref, loss_ref):
    first = core_ref[0] == 0
    halves = jnp.where(first, own_ref[...], other_ref[...]), jnp.where(first, other_ref[...], own_ref[...])
    loss, norm = scalars(halves[0], classes)
    for slot, half in enumerate(halves):
        half = half[:classes] / norm
        lanes = half.shape[1] // 128
        for j in range(lanes):
            grad2_ref[pl.ds(2 * j + slot, classes, stride=2 * lanes), :] = half[:, 128 * j : 128 * (j + 1)]
    loss_ref[...] = loss / norm
    rows = grad1_ref.shape[1]
    grad1_ref[0] = first_ref[:rows] / norm
    grad1_ref[1] = first_ref[rows:] / norm


def exchange(value, axis, step):
    size = lax.axis_size(axis)
    return lax.ppermute(value, axis, [(i, i ^ step) for i in range(size)])


def swapped(step, count):
    bits = count.bit_length() - 1
    if bits % 2:
        return step
    half = bits // 2
    return (step & ((1 << half) - 1)) << half | step >> half


def hop(value, step):
    count, wide = lax.axis_size("feat"), lax.axis_size("dp")
    pairs = []
    for f in range(count):
        for d in range(wide):
            other = f ^ (step if d % 2 == 0 else swapped(step, count))
            pairs.append((f * wide + d, other * wide + d))
    return lax.ppermute(value, ("feat", "dp"), pairs)


def fold_hop(value, step):
    count = lax.axis_size("dp")
    pairs = []
    for d in range(count):
        z = d // 2 ^ (step if d % 2 == 0 else swapped(step, count // 2))
        pairs.append((d, 2 * z + d % 2))
    return lax.ppermute(value, "dp", pairs)


def gather_blocks(block, count):
    blocks = [block]
    for s in range(1, count):
        low_bit = s & -s
        blocks.append(hop(blocks[low_bit] if s != low_bit else block, s ^ low_bit if s != low_bit else s))
    return blocks


def on_device(features, neighbors, labels, loss_weight, w1_self, w1_neigh, w2_self, w2_neigh):
    feat_count = lax.axis_size("feat")
    dp_count = lax.axis_size("dp")
    groups = dp_count // 2
    nodes, fanout = neighbors.shape
    rows, hid = w1_self.shape
    classes = w2_self.shape[1]
    place = lax.axis_index("dp").astype(jnp.int32)
    core = (place % 2).reshape(1)
    z = (place // 2).reshape(1)

    wide = gather_blocks(features, feat_count)
    early = [s for s in range(feat_count) if s & (s - 1) == 0]
    late = [s for s in range(feat_count) if s & (s - 1)]
    nodes_mine = early_nodes(early, 0, feat_count)
    limit = 12 + 6 * nodes * nodes // (1024 * 1024)
    passing = [labels.reshape(1, nodes), loss_weight.reshape(1, nodes), w2_self.T, w2_neigh.T]
    at, mine_own, other_own, labels, loss_weight, w2s, w2n = call(
        functools.partial(count_kernel, fanout),
        [shape((nodes, nodes), BF16)]
        + [shape((rows, hid), BF16)] * 2
        + [shape(p.shape, p.dtype) for p in passing],
        [core, neighbors.T, w1_self, w1_neigh] + passing,
        flops=nodes * nodes * fanout,
        smem=(0,),
        place=False,
    )
    mine = gather_blocks(mine_own, feat_count)[1:]
    *known, other_proj = call(
        functools.partial(early_kernel, nodes_mine, early),
        [shape((hid, nodes), F32)] * (len(nodes_mine) + 1),
        [mine_own, other_own] + [wide[s] for s in early] + [mine[s - 1] for s in early[1:]],
        flops=2 * nodes * hid * rows * (len(early) + 1),
        limit=limit,
    )
    (mine_proj,) = call(
        functools.partial(mine_kernel, nodes_mine, late, feat_count),
        [shape((hid, nodes), F32)],
        known + [mine[s - 1] for s in late] + [wide[s] for s in late],
        flops=30 * nodes * hid * rows * feat_count,
        limit=limit,
    )
    partner = [exchange(block, "dp", 1) for block in mine]
    padded = (classes + 3 + 15) // 16 * 16
    send2, keep2, grad, hidden = call(
        functools.partial(forward_kernel, feat_count, fanout),
        [
            shape((padded, hid), F32),
            shape((padded, hid), F32),
            shape((classes, nodes), BF16),
            shape((hid, nodes), BF16),
        ],
        wide[1:] + [core, labels, loss_weight, at, w2s, w2n, mine_proj, other_proj] + partner,
        scratch=[
            pltpu.VMEM((2, hid, nodes), BF16),
        ],
        flops=2 * nodes * hid * 2 * (rows * feat_count + nodes),
        smem=(feat_count - 1,),
        limit=limit,
    )
    recv2 = exchange(send2, "dp", 1)
    chunk = 2 * (rows // dp_count)
    send1, keep1 = call(
        functools.partial(backward_kernel, fanout, groups),
        [shape((groups, chunk, hid), F32)] * 2,
        [core, grad, hidden, at, w2s, w2n, features],
        flops=2 * nodes * hid * 2 * (rows + nodes),
        smem=(0,),
        limit=limit,
    )
    recv1 = exchange(send1, "dp", 1)
    (own2,) = call(functools.partial(pair_kernel, classes), [shape((padded, hid), BF16)], [keep2, recv2])
    left = groups // 2
    kept1, send1 = call(
        functools.partial(chunk_kernel, groups),
        [shape((left, chunk, hid), F32), shape((left * chunk, hid), BF16)],
        [z, core, keep1, recv1],
        smem=(0, 1),
    )
    step = 1
    while left > 1:
        far2, far1 = fold_hop(own2, step), fold_hop(send1, step)
        left, step = left // 2, 2 * step
        (own2,) = call(
            functools.partial(fold_second_kernel, classes), [shape((padded, hid), BF16)], [kept1, own2, far2]
        )
        kept1, send1 = call(
            fold_first_kernel,
            [shape((left, chunk, hid), F32), shape((left * chunk, hid), BF16)],
            [kept1, far1],
        )
    far2, far1 = fold_hop(own2, step), fold_hop(send1, step)
    (total2,) = call(second_sum_kernel, [shape((padded, hid), F32)], [own2, far2])
    other2 = exchange(total2, "dp", 1)
    (sum1,) = call(first_sum_kernel, [shape((chunk, hid), F32)], [kept1, far1], flops=300 * rows * nodes * hid)
    grad_w1, grad_w2, loss = call(
        functools.partial(out_kernel, classes),
        [shape((2, rows // dp_count, hid), F32), shape((classes * 2 * (hid // 128), 128), F32), shape((1, 1), F32)],
        [core, total2, other2, sum1],
        smem=(0,),
        final=True,
    )
    grad_w2 = grad_w2.reshape(classes, hid // 128, 2, 128).transpose(2, 1, 3, 0).reshape(2, hid, classes)
    return loss[0, 0], grad_w1, grad_w2


def solution(mesh):
    in_specs = (
        P("feat", "dp"),
        P("dp", None),
        P("dp"),
        P("dp"),
        P("feat", None),
        P("feat", None),
        P(),
        P(),
    )
    out_specs = (P(), P(None, ("feat", "dp"), None), P())
    return jax.shard_map(
        on_device, mesh=mesh, in_specs=in_specs, out_specs=out_specs, check_vma=False
    )
```

```python
import functools

import jax
import jax.numpy as jnp
from jax import lax
from jax.experimental import pallas as pl
from jax.experimental.pallas import tpu as pltpu
from jax.sharding import PartitionSpec as P

BF16 = jnp.bfloat16
F32 = jnp.float32


def dot_nn(left, right):
    return lax.dot_general(left, right, (((1,), (0,)), ((), ())), preferred_element_type=F32)


def dot_nt(left, right):
    return lax.dot_general(left, right, (((1,), (1,)), ((), ())), preferred_element_type=F32)


def dot_tn(left, right):
    return lax.dot_general(left, right, (((0,), (0,)), ((), ())), preferred_element_type=F32)


def tree_sum(terms):
    terms = list(terms)
    while len(terms) > 1:
        terms = [terms[i] + terms[i + 1] for i in range(0, len(terms), 2)]
    return terms[0]


def call(kernel, outs, args, flops=0, scratch=(), smem=(), limit=16, final=False, place=True):
    size = sum(a.size * a.dtype.itemsize for a in args)
    size += sum(o.dtype.itemsize * o.size for o in outs)
    spaces = [pltpu.SMEM if i in smem else pltpu.VMEM for i in range(len(args))]
    space = pltpu.VMEM if place else pltpu.HBM
    placed = [a if i in smem else pltpu.with_memory_space_constraint(a, space) for i, a in enumerate(args)]
    return pl.pallas_call(
        kernel,
        out_shape=outs if final else [pltpu.VMEM(o.shape, o.dtype) for o in outs],
        in_specs=[pl.BlockSpec(memory_space=kind) for kind in spaces],
        out_specs=[pl.BlockSpec(memory_space=pltpu.VMEM)] * len(outs),
        scratch_shapes=list(scratch),
        cost_estimate=pl.CostEstimate(flops=flops, bytes_accessed=size, transcendentals=0),
        compiler_params=pltpu.CompilerParams(vmem_limit_bytes=limit * 1024 * 1024),
    )(*placed)


def shape(dims, dtype):
    return jax.ShapeDtypeStruct(dims, dtype)


def count_kernel(fanout, core_ref, nbr_ref, ws_ref, wn_ref, *refs):
    passing = (len(refs) - 3) // 2
    at_ref, mine_ref, other_ref = refs[passing : passing + 3]
    first = core_ref[0] == 0
    mine_ref[...] = jnp.where(first, ws_ref[...], wn_ref[...])
    other_ref[...] = jnp.where(first, wn_ref[...], ws_ref[...])
    for i in range(passing):
        refs[passing + 3 + i][...] = refs[i][...]
    nodes = at_ref.shape[1]
    step = 32

    def body(i, carry):
        row = (lax.broadcasted_iota(jnp.int32, (step, nodes), 0) + i * step).astype(jnp.int16)
        total = jnp.zeros((step, nodes), BF16)
        for k in range(fanout):
            hit = jnp.broadcast_to(nbr_ref[k : k + 1, :], (step, nodes)).astype(jnp.int16) == row
            total = total + jnp.where(hit, jnp.ones((step, nodes), BF16), jnp.zeros((step, nodes), BF16))
        at_ref[pl.ds(pl.multiple_of(i * step, step), step), :] = total
        return carry

    lax.fori_loop(0, nodes // step, body, 0)


def early_nodes(early, first, last):
    if all(s in early for s in range(first, last)):
        return [(first, last)]
    if last - first == 1:
        return []
    middle = (first + last) // 2
    return early_nodes(early, first, middle) + early_nodes(early, middle, last)


def tree_product(first, last, known, leaf):
    if (first, last) in known:
        return known[(first, last)][...]
    if last - first == 1:
        return leaf(first)
    middle = (first + last) // 2
    return tree_product(first, middle, known, leaf) + tree_product(middle, last, known, leaf)


def early_kernel(nodes_mine, early, own_ref, other_ref, *refs):
    f_refs = dict(zip(early, refs))
    w_refs = dict(zip(early[1:], refs[len(early) :]))
    outs = refs[2 * len(early) - 1 :]
    for (begin, end), out_ref in zip(nodes_mine, outs):
        leaf = lambda s: dot_tn(own_ref[...] if s == 0 else w_refs[s][...], f_refs[s][...])
        out_ref[...] = tree_product(begin, end, {}, leaf)
    outs[-1][...] = dot_tn(other_ref[...], f_refs[0][...])


def mine_kernel(nodes_mine, late, feat_count, *refs):
    known = dict(zip(nodes_mine, refs))
    refs = refs[len(nodes_mine) :]
    w_refs, f_refs = dict(zip(late, refs)), dict(zip(late, refs[len(late) :]))
    refs[-1][...] = tree_product(0, feat_count, known, lambda s: dot_tn(w_refs[s][...], f_refs[s][...]))


def forward_kernel(feat_count, fanout, *refs):
    f_refs, refs = refs[: feat_count - 1], refs[feat_count - 1 :]
    core_ref, labels_ref, weight_ref, at_ref, w2s_ref, w2n_ref, mine_ref, other_ref = refs[:8]
    partner_refs = refs[8 : 7 + feat_count]
    send_ref, keep_ref, g_ref, hidden_ref, proj, pair = refs[7 + feat_count :]
    core = core_ref[0]
    classes = w2s_ref.shape[0]
    nodes = at_ref.shape[1]
    scale = 1.0 / fanout
    proj[core] = mine_ref[...]
    proj[1 - core] = tree_product(
        0, feat_count, {(0, 1): other_ref}, lambda s: dot_tn(partner_refs[swapped(s, feat_count) - 1][...], f_refs[s - 1][...])
    )
    at = at_ref[...]
    pre = proj[0] + dot_nn(proj[1].astype(BF16), at) * scale
    hidden = jnp.maximum(pre, 0.0).astype(BF16)
    hidden_ref[...] = hidden
    second = (dot_nn(hidden, at) * scale).astype(BF16)
    logits = dot_nn(w2s_ref[...], hidden) + dot_nn(w2n_ref[...], second)
    shifted = logits - jnp.max(logits, axis=0, keepdims=True)
    powers = jnp.exp(shifted)
    total = jnp.sum(powers, axis=0, keepdims=True)
    hot = lax.broadcasted_iota(jnp.int32, (classes, nodes), 0) == labels_ref[...]
    picked = jnp.sum(jnp.where(hot, shifted, 0.0), axis=0, keepdims=True) - jnp.log(total)
    chance = jnp.exp(picked)
    rest = 1.0 - chance
    weight = weight_ref[...]
    terms = -rest * rest * picked
    slope = weight * (2.0 * rest * chance * picked - rest * rest)
    grad = (jnp.where(hot, slope, 0.0) - (slope / total) * powers).astype(BF16)
    g_ref[...] = grad
    pair[0] = hidden
    pair[1] = second
    loss_part = jnp.sum(weight * terms)
    norm_part = jnp.sum(weight)
    for out_ref, which in ((send_ref, 1 - core), (keep_ref, core)):
        rows, cols = out_ref.shape
        row = lax.broadcasted_iota(jnp.int32, (rows, cols), 0)
        col = lax.broadcasted_iota(jnp.int32, (rows, cols), 1)
        extra = jnp.where(col == 0, loss_part, jnp.where(col == 1, norm_part, 0.0))
        out_ref[...] = jnp.where(row >= classes, extra, 0.0)
        out_ref[:classes, :] = dot_nt(grad, pair[which])


def backward_kernel(
    fanout, groups, core_ref, g_ref, hidden_ref, at_ref, w2s_ref, w2n_ref, f_ref, send_ref, keep_ref
):
    core = core_ref[0]
    scale = 1.0 / fanout
    grad = g_ref[...]
    at = at_ref[...]
    summed = dot_nt(grad, at)
    high = summed.astype(BF16)
    low = (summed - high.astype(F32)).astype(BF16)
    w2n = w2n_ref[...]
    hidden_grad = dot_tn(w2s_ref[...], grad) + (dot_tn(w2n, high) + dot_tn(w2n, low)) * scale
    pre_grad = jnp.where(hidden_ref[...] > 0, hidden_grad, 0.0).astype(BF16)
    proj_grad = (dot_nt(pre_grad, at) * scale).astype(BF16)
    features = f_ref[...]
    full = (dot_nt(features, pre_grad), dot_nt(features, proj_grad))
    rows = send_ref.shape[1] // 2
    first = core == 0
    for z in range(groups):
        for part in range(2):
            low_rows = full[part][2 * z * rows : (2 * z + 1) * rows]
            high_rows = full[part][(2 * z + 1) * rows : (2 * z + 2) * rows]
            send_ref[z, part * rows : (part + 1) * rows] = jnp.where(first, high_rows, low_rows)
            keep_ref[z, part * rows : (part + 1) * rows] = jnp.where(first, low_rows, high_rows)


def split_rows(total, classes):
    high = total.astype(BF16).astype(F32)
    rest = total - high
    middle = rest.astype(BF16).astype(F32)
    low = rest - middle
    row = lax.broadcasted_iota(jnp.int32, total.shape, 0)
    return jnp.where(row == classes + 1, middle, jnp.where(row == classes + 2, low, high)).astype(BF16)


def pair_kernel(classes, keep_ref, recv_ref, out_ref):
    out_ref[...] = split_rows(keep_ref[...] + recv_ref[...], classes)


def fold_second_kernel(classes, order_ref, own_ref, recv_ref, out_ref):
    total = own_ref[...].astype(F32) + recv_ref[...].astype(F32)
    row = lax.broadcasted_iota(jnp.int32, total.shape, 0)
    inside = jnp.logical_and(row >= classes, row < classes + 3)
    whole = jnp.sum(jnp.where(inside, total, 0.0), axis=0, keepdims=True)
    out_ref[...] = split_rows(jnp.where(row >= classes, whole, total), classes)


def chunk_kernel(groups, z_ref, core_ref, keep_ref, recv_ref, kept_ref, send_ref):
    z, core, chunk = z_ref[0], core_ref[0], keep_ref.shape[1]

    def total(step):
        group = jnp.bitwise_xor(z, step + core * (swapped(step, groups) - step))
        return keep_ref[group] + recv_ref[group]

    for i in range(groups // 2):
        kept_ref[i] = total(2 * i)
        send_ref[i * chunk : (i + 1) * chunk] = total(2 * i + 1).astype(BF16)


def fold_first_kernel(own_ref, recv_ref, kept_ref, send_ref):
    chunk = own_ref.shape[1]
    for i in range(own_ref.shape[0] // 2):
        kept_ref[i] = own_ref[2 * i] + recv_ref[2 * i * chunk : (2 * i + 1) * chunk].astype(F32)
        other = own_ref[2 * i + 1] + recv_ref[(2 * i + 1) * chunk : (2 * i + 2) * chunk].astype(F32)
        send_ref[i * chunk : (i + 1) * chunk] = other.astype(BF16)


def second_sum_kernel(*refs):
    out_ref = refs[-1]
    out_ref[...] = tree_sum([r[...].astype(F32) for r in refs[:-1]])


def scalars(total, classes):
    row = lax.broadcasted_iota(jnp.int32, total.shape, 0)
    col = lax.broadcasted_iota(jnp.int32, total.shape, 1)
    inside = jnp.logical_and(row >= classes, row < classes + 3)
    loss = jnp.sum(jnp.where(jnp.logical_and(inside, col == 0), total, 0.0), keepdims=True)
    norm = jnp.sum(jnp.where(jnp.logical_and(inside, col == 1), total, 0.0), keepdims=True)
    return loss, norm


def first_sum_kernel(own_ref, *refs):
    refs[-1][...] = own_ref[0] + refs[0][...].astype(F32)


def out_kernel(classes, core_ref, own_ref, other_ref, first_ref, grad1_ref, grad2_ref, loss_ref):
    first = core_ref[0] == 0
    halves = jnp.where(first, own_ref[...], other_ref[...]), jnp.where(first, other_ref[...], own_ref[...])
    loss, norm = scalars(halves[0], classes)
    for slot, half in enumerate(halves):
        half = half[:classes] / norm
        lanes = half.shape[1] // 128
        for j in range(lanes):
            grad2_ref[pl.ds(2 * j + slot, classes, stride=2 * lanes), :] = half[:, 128 * j : 128 * (j + 1)]
    loss_ref[...] = loss / norm
    rows = grad1_ref.shape[1]
    grad1_ref[0] = first_ref[:rows] / norm
    grad1_ref[1] = first_ref[rows:] / norm


def exchange(value, axis, step):
    size = lax.axis_size(axis)
    return lax.ppermute(value, axis, [(i, i ^ step) for i in range(size)])


def swapped(step, count):
    bits = count.bit_length() - 1
    if bits % 2:
        return step
    half = bits // 2
    return (step & ((1 << half) - 1)) << half | step >> half


def hop(value, step):
    count, wide = lax.axis_size("feat"), lax.axis_size("dp")
    pairs = []
    for f in range(count):
        for d in range(wide):
            other = f ^ (step if d % 2 == 0 else swapped(step, count))
            pairs.append((f * wide + d, other * wide + d))
    return lax.ppermute(value, ("feat", "dp"), pairs)


def fold_hop(value, step):
    count = lax.axis_size("dp")
    pairs = []
    for d in range(count):
        z = d // 2 ^ (step if d % 2 == 0 else swapped(step, count // 2))
        pairs.append((d, 2 * z + d % 2))
    return lax.ppermute(value, "dp", pairs)


def gather_blocks(block, count):
    blocks = [block]
    for s in range(1, count):
        low_bit = s & -s
        blocks.append(hop(blocks[low_bit] if s != low_bit else block, s ^ low_bit if s != low_bit else s))
    return blocks


def on_device(features, neighbors, labels, loss_weight, w1_self, w1_neigh, w2_self, w2_neigh):
    feat_count = lax.axis_size("feat")
    dp_count = lax.axis_size("dp")
    groups = dp_count // 2
    nodes, fanout = neighbors.shape
    rows, hid = w1_self.shape
    classes = w2_self.shape[1]
    place = lax.axis_index("dp").astype(jnp.int32)
    core = (place % 2).reshape(1)
    z = (place // 2).reshape(1)

    wide = gather_blocks(features, feat_count)
    early = [s for s in range(feat_count) if s & (s - 1) == 0]
    late = [s for s in range(feat_count) if s & (s - 1)]
    nodes_mine = early_nodes(early, 0, feat_count)
    limit = 12 + 6 * nodes * nodes // (1024 * 1024)
    passing = [labels.reshape(1, nodes), loss_weight.reshape(1, nodes), w2_self.T, w2_neigh.T]
    at, mine_own, other_own, labels, loss_weight, w2s, w2n = call(
        functools.partial(count_kernel, fanout),
        [shape((nodes, nodes), BF16)]
        + [shape((rows, hid), BF16)] * 2
        + [shape(p.shape, p.dtype) for p in passing],
        [core, neighbors.T, w1_self, w1_neigh] + passing,
        flops=nodes * nodes * fanout,
        smem=(0,),
        place=False,
    )
    mine = gather_blocks(mine_own, feat_count)[1:]
    *known, other_proj = call(
        functools.partial(early_kernel, nodes_mine, early),
        [shape((hid, nodes), F32)] * (len(nodes_mine) + 1),
        [mine_own, other_own] + [wide[s] for s in early] + [mine[s - 1] for s in early[1:]],
        flops=2 * nodes * hid * rows * (len(early) + 1),
        limit=limit,
    )
    (mine_proj,) = call(
        functools.partial(mine_kernel, nodes_mine, late, feat_count),
        [shape((hid, nodes), F32)],
        known + [mine[s - 1] for s in late] + [wide[s] for s in late],
        flops=30 * nodes * hid * rows * feat_count,
        limit=limit,
    )
    partner = [exchange(block, "dp", 1) for block in mine]
    padded = (classes + 3 + 15) // 16 * 16
    send2, keep2, grad, hidden = call(
        functools.partial(forward_kernel, feat_count, fanout),
        [
            shape((padded, hid), F32),
            shape((padded, hid), F32),
            shape((classes, nodes), BF16),
            shape((hid, nodes), BF16),
        ],
        wide[1:] + [core, labels, loss_weight, at, w2s, w2n, mine_proj, other_proj] + partner,
        scratch=[
            pltpu.VMEM((2, hid, nodes), F32),
            pltpu.VMEM((2, hid, nodes), BF16),
        ],
        flops=2 * nodes * hid * 2 * (rows * feat_count + nodes),
        smem=(feat_count - 1,),
        limit=limit,
    )
    recv2 = exchange(send2, "dp", 1)
    chunk = 2 * (rows // dp_count)
    send1, keep1 = call(
        functools.partial(backward_kernel, fanout, groups),
        [shape((groups, chunk, hid), F32)] * 2,
        [core, grad, hidden, at, w2s, w2n, features],
        flops=2 * nodes * hid * 2 * (rows + nodes),
        smem=(0,),
        limit=limit,
    )
    recv1 = exchange(send1, "dp", 1)
    (own2,) = call(functools.partial(pair_kernel, classes), [shape((padded, hid), BF16)], [keep2, recv2])
    left = groups // 2
    kept1, send1 = call(
        functools.partial(chunk_kernel, groups),
        [shape((left, chunk, hid), F32), shape((left * chunk, hid), BF16)],
        [z, core, keep1, recv1],
        smem=(0, 1),
    )
    step = 1
    while left > 1:
        far2, far1 = fold_hop(own2, step), fold_hop(send1, step)
        left, step = left // 2, 2 * step
        (own2,) = call(
            functools.partial(fold_second_kernel, classes), [shape((padded, hid), BF16)], [kept1, own2, far2]
        )
        kept1, send1 = call(
            fold_first_kernel,
            [shape((left, chunk, hid), F32), shape((left * chunk, hid), BF16)],
            [kept1, far1],
        )
    far2, far1 = fold_hop(own2, step), fold_hop(send1, step)
    (total2,) = call(second_sum_kernel, [shape((padded, hid), F32)], [own2, far2])
    other2 = exchange(total2, "dp", 1)
    (sum1,) = call(first_sum_kernel, [shape((chunk, hid), F32)], [kept1, far1], flops=300 * rows * nodes * hid)
    grad_w1, grad_w2, loss = call(
        functools.partial(out_kernel, classes),
        [shape((2, rows // dp_count, hid), F32), shape((classes * 2 * (hid // 128), 128), F32), shape((1, 1), F32)],
        [core, total2, other2, sum1],
        smem=(0,),
        final=True,
    )
    grad_w2 = grad_w2.reshape(classes, hid // 128, 2, 128).transpose(2, 1, 3, 0).reshape(2, hid, classes)
    return loss[0, 0], grad_w1, grad_w2


def solution(mesh):
    in_specs = (
        P("feat", "dp"),
        P("dp", None),
        P("dp"),
        P("dp"),
        P("feat", None),
        P("feat", None),
        P(),
        P(),
    )
    out_specs = (P(), P(None, ("feat", "dp"), None), P())
    return jax.shard_map(
        on_device, mesh=mesh, in_specs=in_specs, out_specs=out_specs, check_vma=False
    )
```
